512 devices in a mesh: ctx: 64 (over x, z_lo, core), head: 8 (over y, z_hi).
Axes of the slice: x: 4, y: 4, z: 16 (z_hi: 2, z_lo: 8; z = z_hi * 8 + z_lo), core: 2. Of those that a mesh axis runs over, the one named last changes fastest.
Arguments:
- hidden: bfloat16 [12288, 5120], P('ctx', 'head'), may hold values from -64 to 64
- norm_gain: bfloat16 [5120], replicated, may hold values from 0.099609375 to 1.8984375
- query_gain: float32 [128], replicated, may hold values from 1.4 to 6
- key_gain: float32 [128], replicated, may hold values from 1.4 to 6
- weight_store: bfloat16 [5120, 6144], P('ctx', 'head'), may hold values from -0.0559017 to 0.0559017
- documents: int32 [12288], P('ctx'), may hold values from 0 to 63, never falling along the last dimension, each value on 1 to 6144 neighbouring positions
- owners: int32 [64], replicated, may hold values from 0 to 63, each once
Outputs:
- keys_fresh: bfloat16 [12288, 1024], P('ctx', 'head')
- values_fresh: bfloat16 [12288, 1024], P('ctx', 'head')
- context: bfloat16 [12288, 4096], P('ctx', 'head')
The draws below stay inside these ranges and needn't reach their ends.
Inputs may be any that keep to these rules, and one draw needn't show every extreme that they name: `documents`: segment numbers never fall along the slab; each of the 64 segments holds 1 to 6144 tokens and one holds exactly 6144. `owners`: each slot holds exactly one panel.
All inputs are finite; a program needn't handle non-finite values.
Results may differ from the reference program's by a relative error of at most 0.012.
The reference program's roundings to bfloat16 on the way count: a program that leaves them out, or rounds other values in their place, can miss the bound.
Values may be sent and summed in bfloat16 or wider, within the bound.
No kernel may reach another device: no remote copies, remote signals or barrier semaphores. Data moves between devices by JAX's collectives and lax.ppermute only.
A program may use at most 128 MiB of HBM per device.

```python
import math
import jax
import jax.numpy as jnp
import numpy as np
from jax import lax

D = 5120
HD = 128
QPER = 4
TOK_DEV = 192
TOKENS = 12288
KVH = 8
HQ = 32
SEGS = 64
MAXDOC = 6144
N_CTX = 64


def draw_hidden(key, part):
    key = jax.random.fold_in(key, 11)
    first, second, third = jax.random.split(key, 3)
    row_scale = jnp.exp(jax.random.uniform(second, (TOKENS, 1), jnp.float32, 0.0, math.log(30.0)))
    column_scale = 0.3 * jnp.exp(jax.random.uniform(third, (1, D), jnp.float32, 0.0, math.log(10.0)))
    base = jnp.clip(jax.random.normal(first, (TOKENS, D), jnp.float32), -6.0, 6.0)
    return jnp.clip(base * row_scale * column_scale, -64.0, 64.0).astype(jnp.bfloat16)


def draw_weight_store(key, part):
    key = jax.random.fold_in(key, 37)
    first = jax.random.fold_in(key, 0)
    base = jax.random.normal(first, (D, KVH, QPER + 2, HD), jnp.float32)
    panels = base
    scaled = jnp.clip(panels, -3.984, 3.984) * D ** (-0.5)
    return scaled.reshape(D, KVH * (QPER + 2) * HD).astype(jnp.bfloat16)


def gain_between(key, lower, upper):
    return jnp.exp(jax.random.uniform(key, (HD,), jnp.float32, math.log(lower), math.log(upper)))


def draw_query_gain(key, part):
    key = jax.random.fold_in(key, 23)
    return gain_between(key, 1.4, 2.8)


def draw_key_gain(key, part):
    key = jax.random.fold_in(key, 29)
    return gain_between(key, 1.4, 2.8)


def split_up(count, total, limit, lean):
    loads = [(1 << 20) // math.isqrt(grade ** lean) + 1 for grade in range(2, count + 1)]
    spare, holding = total - limit - (count - 1), [1] * (count - 1)
    while spare > 0:
        candidates = [i for i in range(count - 1) if holding[i] < limit]
        whole, left = sum([loads[i] for i in candidates]), spare
        for i in candidates:
            more = min(limit - holding[i], max(1, left * loads[i] // whole), spare)
            holding[i] = holding[i] + more
            spare = spare - more
    return np.array([limit] + holding)


def uneven(key, number_of, total, reach, lean):
    if number_of == 2:
        one = jax.random.randint(key, (), max(1, total - reach), min(reach, total - 1) + 1)
        return jnp.stack([one, total - one])
    sizes = jnp.asarray(split_up(number_of, total, reach, lean), jnp.int32)
    couples = (number_of - 1) // 2
    donor, sink = sizes[1:1 + 2 * couples:2], sizes[2:2 + 2 * couples:2]
    room = jnp.minimum(donor - 1, reach - sink)
    shifted = jax.random.randint(jax.random.fold_in(key, 1), (couples,), 0, 1 << 20) % (room + 1)
    sizes = sizes.at[1:1 + 2 * couples:2].set(donor - shifted).at[2:2 + 2 * couples:2].set(sink + shifted)
    return sizes[jax.random.permutation(jax.random.fold_in(key, 2), number_of)]


def setup_inputs(seed: int = 0) -> dict:
    streams_of = jax.random.split(jax.random.key(seed), 8)
    return {
        "hidden": draw_hidden(jax.random.fold_in(streams_of[7], 71), 0),
        "norm_gain": jnp.clip(1.0 + 0.18 * jax.random.normal(streams_of[1], (D,), jnp.float32), 0.099609375, 1.8984375).astype(jnp.bfloat16),
        "query_gain": draw_query_gain(jax.random.fold_in(streams_of[7], 71), 0),
        "key_gain": draw_key_gain(jax.random.fold_in(streams_of[7], 71), 0),
        "weight_store": draw_weight_store(jax.random.fold_in(streams_of[7], 71), 0),
        "documents": jnp.searchsorted(jnp.cumsum(uneven(streams_of[5], SEGS, TOKENS, MAXDOC, 0)), jnp.arange(TOKENS), side="right").astype(jnp.int32),
        "owners": jax.random.permutation(streams_of[6], N_CTX).astype(jnp.int32),
    }


epsilon = 1e-06
rope_base = 1000000.0

def rms_scale(values, gain_vector):
    mean_square = lax.optimization_barrier(jnp.mean(values * values, axis=-1, keepdims=True))
    return values * lax.rsqrt(mean_square + epsilon) * gain_vector

def rotate(values, positions):
    half_width = values.shape[-1] // 2
    exponent = jnp.arange(half_width, dtype=jnp.float32) * (2.0 / values.shape[-1])
    frequency = jnp.exp(exponent * -math.log(rope_base))
    angles = positions.astype(jnp.float32)[:, None] * frequency[None, :]
    layout = (values.shape[0],) + (1,) * (values.ndim - 2) + (values.shape[-1],)
    cosine = jnp.concatenate([jnp.cos(angles), jnp.cos(angles)], axis=-1).reshape(layout)
    sine_part = jnp.concatenate([jnp.sin(angles), jnp.sin(angles)], axis=-1).reshape(layout)
    turned = jnp.concatenate([-values[..., half_width:], values[..., :half_width]], axis=-1)
    return values * cosine + turned * sine_part

def reference(hidden, norm_gain, query_gain, key_gain, weight_store, documents, owners):
    normed = rms_scale(hidden.astype(jnp.float32), norm_gain.astype(jnp.float32)).astype(jnp.bfloat16)
    panel_rows = D // N_CTX
    weights = jnp.take(weight_store.reshape(N_CTX, panel_rows, -1), owners, axis=0).reshape(D, -1)
    projected = jnp.dot(normed, weights, preferred_element_type=jnp.float32)
    projected = projected.reshape(TOKENS, KVH, QPER + 2, HD)
    segment_table = jnp.arange(SEGS, dtype=jnp.int32)
    one_hot = (documents[:, None] == segment_table[None, :]).astype(jnp.int32)
    counted = lax.optimization_barrier(jnp.sum(one_hot, axis=0)).astype(jnp.int32)
    starts = (jnp.cumsum(counted) - counted).astype(jnp.int32)
    token_index = jnp.arange(TOKENS, dtype=jnp.int32)
    positions = token_index - lax.optimization_barrier(jnp.sum(one_hot * starts[None, :], axis=1)).astype(jnp.int32)
    queries = rotate(rms_scale(projected[:, :, :QPER, :], query_gain), positions).astype(jnp.bfloat16)
    keys_all = rotate(rms_scale(projected[:, :, QPER, :], key_gain), positions).astype(jnp.bfloat16)
    values_all = projected[:, :, QPER + 1, :].astype(jnp.bfloat16)
    window = MAXDOC + TOK_DEV
    inverse_root = 1.0 / math.sqrt(HD)

    def attend_block(block_index):
        begin = (block_index * TOK_DEV).astype(jnp.int32)
        anchor = jnp.maximum(begin - MAXDOC, 0).astype(jnp.int32)
        query_block = lax.dynamic_slice_in_dim(queries, begin, TOK_DEV, 0).astype(jnp.float32)
        key_block = lax.dynamic_slice_in_dim(keys_all, anchor, window, 0).astype(jnp.float32)
        value_block = lax.dynamic_slice_in_dim(values_all, anchor, window, 0).astype(jnp.float32)
        query_docs = lax.dynamic_slice_in_dim(documents, begin, TOK_DEV, 0)
        key_docs = lax.dynamic_slice_in_dim(documents, anchor, window, 0)
        query_index = begin + jnp.arange(TOK_DEV, dtype=jnp.int32)
        key_index = anchor + jnp.arange(window, dtype=jnp.int32)
        allowed = (key_docs[None, :] == query_docs[:, None]) & (key_index[None, :] <= query_index[:, None])
        allowed = allowed[:, None, None, :]
        scores = jnp.einsum('tgqd,sgd->tgqs', query_block, key_block) * inverse_root
        masked = jnp.where(allowed, scores, -1e+30)
        row_top = lax.optimization_barrier(jnp.max(masked, axis=-1, keepdims=True))
        expterms = jnp.where(allowed, jnp.exp(masked - row_top), 0.0)
        denominator = lax.optimization_barrier(jnp.sum(expterms, axis=-1))
        rounded = expterms.astype(jnp.bfloat16).astype(jnp.float32)
        mixed = jnp.einsum('tgqs,sgd->tgqd', rounded, value_block) / denominator[..., None]
        return mixed.astype(jnp.bfloat16)
    blocks = lax.map(attend_block, jnp.arange(N_CTX, dtype=jnp.int32))
    context = blocks.reshape(TOKENS, HQ * HD)
    return (keys_all.reshape(TOKENS, KVH * HD), values_all.reshape(TOKENS, KVH * HD), context)
```

```python
import functools
import math

import jax
import jax.numpy as jnp
from jax import lax
from jax.experimental import pallas as pl
from jax.experimental.pallas import tpu as pltpu
from jax.sharding import Mesh
from jax.sharding import PartitionSpec as P

epsilon = 1e-06
rope_base = 1000000.0
NEG = -1e30
MASKED = -3e38
KEY_BLOCK = 512
VMEM_LIMIT = 48 * 1024 * 1024


def call(kernel, out_shape, n_smem, n_vmem, scratch=(), flops=0):
    specs = [pl.BlockSpec(memory_space=pltpu.SMEM)] * n_smem
    specs += [pl.BlockSpec(memory_space=pltpu.VMEM)] * n_vmem
    n_out = len(out_shape)
    return pl.pallas_call(
        kernel,
        out_shape=out_shape,
        in_specs=specs,
        out_specs=[pl.BlockSpec(memory_space=pltpu.VMEM)] * n_out,
        scratch_shapes=list(scratch),
        compiler_params=pltpu.CompilerParams(vmem_limit_bytes=VMEM_LIMIT),
        cost_estimate=pl.CostEstimate(flops=flops, bytes_accessed=4 << 20, transcendentals=0),
    )


def norm_kernel(where, gain, *refs):
    blocks, out = refs[:-1], refs[-1]
    ny = len(blocks) // 2
    rows, width = blocks[0].shape[1:]
    core, me = where[0], where[1]
    for side in range(2):
        first = pl.multiple_of(rows * (core if side == 0 else 1 - core), rows)
        total = jnp.zeros((rows, 128), jnp.float32)
        for s in range(ny):
            for half in range(2):
                v = blocks[side * ny + s][half].astype(jnp.float32)
                v = v * v
                for k in range(width // 128):
                    total = total + v[:, k * 128 : (k + 1) * 128]
        mean = jnp.sum(total, axis=-1, keepdims=True) * (1.0 / (2 * ny * width))
        scale = lax.rsqrt(mean + epsilon)
        for s in range(ny):
            source = lax.rem(me + ny - s, ny)
            for half in range(2):
                cols = pl.ds(pl.multiple_of((source * 2 + half) * width, 128), width)
                v = blocks[side * ny + s][half].astype(jnp.float32)
                v = v * scale * gain[:, cols]
                out[pl.ds(first, rows), cols] = v.astype(jnp.bfloat16)


def head_norm_rope(v, gain, cosine, sine):
    mean = jnp.mean(v * v, axis=-1, keepdims=True)
    v = v * lax.rsqrt(mean + epsilon) * gain
    return v * cosine + pltpu.roll(v, 64, 1) * sine


def collect(offsets, where, blocks, weights):
    nx = len(blocks)
    nz, both, _ = blocks[0].shape
    panel = both // 2
    for s in range(nx):
        source = lax.rem(where[1] + nx - s, nx)
        for k in range(nz):
            for c in range(2):
                slot = source * (nz * 2) + k * 2 + c
                first = pl.multiple_of(offsets[slot], 16)
                weights[pl.ds(first, panel), :] = blocks[s][k, c * panel : (c + 1) * panel, :]


def pair_kernel(offsets, where, normed, gain, cosine, sine, *refs):
    blocks, out, weights = refs[:-2], refs[-2], refs[-1]
    collect(offsets, where, blocks, weights)
    v = jnp.dot(normed[...], weights[...], preferred_element_type=jnp.float32)
    keys = head_norm_rope(v, gain[...], cosine[...], sine[...])
    out[...] = jnp.where(where[0] == 0, keys, v).astype(jnp.bfloat16)


def query_kernel(offsets, where, normed, gain, cosine, sine, *refs):
    blocks, out, weights = refs[:-2], refs[-2], refs[-1]
    collect(offsets, where, blocks, weights)
    rows = out.shape[2]
    for side in range(2):
        span = pl.ds(side * rows, rows)
        v = jnp.dot(normed[span, :], weights[...], preferred_element_type=jnp.float32)
        for h in range(2):
            q = head_norm_rope(
                v[:, h * 128 : (h + 1) * 128], gain[...], cosine[span, :], sine[span, :]
            )
            out[side, h] = q.astype(jnp.bfloat16)


def attention_kernel(where, starts, mine, other, q0, q1, q2, o0, o1, o2, lse, keys, values, acc, top, total):
    core = where[0]

    @pl.when(core == 0)
    def _():
        keys[...] = mine[...]
        values[...] = other[...]

    @pl.when(core == 1)
    def _():
        keys[...] = other[...]
        values[...] = mine[...]

    rows = starts.shape[1]
    plane = keys.shape[0]
    scale = math.log2(math.e) / math.sqrt(128)
    eye = lax.broadcasted_iota(jnp.int32, (128, 128), 0) == lax.broadcasted_iota(
        jnp.int32, (128, 128), 1
    )
    lse[...] = jnp.full(lse.shape, NEG, jnp.float32)
    for s, (query, out) in enumerate(((q0, o0), (q1, o1), (q2, o2))):
        low, high = where[1 + 2 * s], where[2 + 2 * s]
        acc[...] = jnp.zeros_like(acc)
        top[...] = jnp.full(top.shape, NEG, jnp.float32)
        total[...] = jnp.zeros_like(total)
        index = (
            s * plane
            + where[7]
            + lax.broadcasted_iota(jnp.int32, (rows, 1), 0)
        )
        begin = starts[s]

        def step(b, carry, s=s, query=query, index=index, begin=begin):
            base = pl.multiple_of(b * KEY_BLOCK, KEY_BLOCK)
            key = keys[pl.ds(base, KEY_BLOCK), :]
            value = values[pl.ds(base, KEY_BLOCK), :]
            col = base + lax.broadcasted_iota(jnp.int32, (rows, KEY_BLOCK), 1)
            allowed = col >= begin
            if s == 0:
                allowed = allowed & (col <= index)
            for h in range(query.shape[0] // rows):
                span = pl.ds(h * rows, rows)
                raw = lax.dot_general(
                    query[span, :], key, (((1,), (1,)), ((), ())),
                    preferred_element_type=jnp.float32,
                )
                raw = jnp.where(allowed, raw * scale, MASKED)
                old = top[span, :]
                new = jnp.maximum(old, jnp.max(raw, axis=-1, keepdims=True))
                terms = jnp.exp2(raw - new)
                decay = jnp.exp2(old - new)
                top[span, :] = new
                total[span, :] = total[span, :] * decay + jnp.sum(terms, axis=-1, keepdims=True)
                acc[span, :] = acc[span, :] * decay + jnp.dot(
                    terms.astype(jnp.bfloat16), value, preferred_element_type=jnp.float32
                )
            return carry

        lax.fori_loop(low // KEY_BLOCK, (high + KEY_BLOCK - 1) // KEY_BLOCK, step, 0)
        summed = total[...]
        safe = jnp.where(summed > 0, summed, 1.0)
        out[...] = (acc[...] / safe).astype(out.dtype)
        log = jnp.where(summed > 0, top[...] + jnp.log2(safe), NEG)
        for g in range(log.shape[0] // 128):
            piece = jnp.where(eye, log[g * 128 : (g + 1) * 128, :], 0.0)
            lse[s, g : g + 1, :] = jnp.sum(piece, axis=0, keepdims=True)


def combine_kernel(where, o0, o1, o2, l0, l1, l2, out):
    rows = out.shape[0]
    eye = lax.broadcasted_iota(jnp.int32, (128, 128), 0) == lax.broadcasted_iota(
        jnp.int32, (128, 128), 1
    )

    def column(ref):
        pieces = [
            jnp.sum(jnp.where(eye, ref[g : g + 1, :], 0.0), axis=1, keepdims=True)
            for g in range(o0.shape[0] // 128)
        ]
        return jnp.concatenate(pieces, axis=0)

    a = column(l0)
    b = jnp.where(where[1] == 1, column(l1), NEG)
    c = jnp.where(where[2] == 1, column(l2), NEG)
    top = jnp.maximum(jnp.maximum(a, b), c)
    a, b, c = jnp.exp2(a - top), jnp.exp2(b - top), jnp.exp2(c - top)
    summed = a * o0[...] + b * o1[...].astype(jnp.float32) + c * o2[...].astype(jnp.float32)
    result = (summed / (a + b + c)).astype(jnp.bfloat16)
    for side in range(2):
        first = 256 * (where[0] if side == 0 else 1 - where[0])
        for h in range(2):
            k = side * 2 + h
            cols = pl.ds(pl.multiple_of(first + h * 128, 128), 128)
            out[:, cols] = result[k * rows : (k + 1) * rows, :]


def ring(axis, size, shift):
    return [(i, (i + shift) % size) for i in range(size)]


def body(hidden, norm_gain, query_gain, key_gain, weight_store, documents, owners):
    x, z, c, y = (lax.axis_index(a) for a in ("x", "z", "c", "y"))
    nx, nz, ny = (lax.axis_size(a) for a in ("x", "z", "y"))
    rows, width = hidden.shape
    slots = owners.shape[0]
    panel = weight_store.shape[0]
    swap = [(0, 1), (1, 0)]
    bf16, f32 = jnp.bfloat16, jnp.float32

    both = lax.all_gather(weight_store, "c", axis=0, tiled=True)
    pair_cols = lax.dynamic_slice_in_dim(both, 512 + 128 * c, 128, 1)
    query_cols = lax.dynamic_slice_in_dim(both, 256 * c, 256, 1)
    line = lax.all_gather(jnp.concatenate([pair_cols, query_cols], axis=1), "z", axis=0)
    pair_line, query_line = line[:, :, :128], line[:, :, 128:]
    pair_blocks = [pair_line] + [
        lax.ppermute(pair_line, "x", ring("x", nx, s)) for s in range(1, nx)
    ]
    query_blocks = [query_line] + [
        lax.ppermute(query_line, "x", ring("x", nx, s)) for s in range(1, nx)
    ]

    wide = lax.all_gather(hidden, "w", axis=0)
    own_blocks = [wide] + [lax.ppermute(wide, "y", ring("y", ny, s)) for s in range(1, ny)]
    other_blocks = [lax.ppermute(v, "c", swap) for v in own_blocks]
    where = jnp.stack([c, y]).astype(jnp.int32)
    (normed,) = call(
        norm_kernel,
        [jax.ShapeDtypeStruct((2 * rows, 2 * ny * width), bf16)],
        1,
        1 + 2 * ny,
    )(where, norm_gain.astype(f32)[None, :], *own_blocks, *other_blocks)

    table = jnp.arange(slots, dtype=jnp.int32)
    counted = lax.psum(
        jnp.sum((documents[:, None] == table[None, :]).astype(jnp.int32), axis=0), ("x", "z", "c")
    )
    first = jnp.cumsum(counted) - counted
    pair_docs = lax.all_gather(documents, "c", axis=0, tiled=True)
    begin = jnp.sum(
        (pair_docs[:, None] == table[None, :]).astype(jnp.int32) * first[None, :], axis=1
    )
    plane = nz * 2 * rows
    token = x * plane + z * 2 * rows + jnp.arange(2 * rows, dtype=jnp.int32)
    positions = token - begin
    exponent = jnp.arange(64, dtype=f32) * (2.0 / 128)
    frequency = jnp.exp(exponent * -math.log(rope_base))
    angles = positions.astype(f32)[:, None] * frequency[None, :]
    cosine, sine = jnp.cos(angles), jnp.sin(angles)
    cosine = jnp.concatenate([cosine, cosine], axis=1)
    sine = jnp.concatenate([-sine, sine], axis=1)
    own_begin = lax.dynamic_slice_in_dim(begin, c * rows, rows, 0)
    near_begin = lax.ppermute(own_begin, "x", [(i, i - 1) for i in range(1, nx)])
    far_begin = lax.ppermute(own_begin, "x", [(i, i - 2) for i in range(2, nx)])

    offsets = jnp.sum(
        table[:, None] * (owners[:, None] == table[None, :]).astype(jnp.int32), axis=0
    ) * panel
    spot = jnp.stack([c, x]).astype(jnp.int32)
    (pair,) = call(
        pair_kernel,
        [jax.ShapeDtypeStruct((2 * rows, 128), bf16)],
        2,
        4 + nx,
        [pltpu.VMEM((slots * panel, 128), bf16)],
        2 * 2 * rows * slots * panel * 128,
    )(offsets, spot, normed, key_gain[None, :], cosine, sine, *pair_blocks)
    (query,) = call(
        query_kernel,
        [jax.ShapeDtypeStruct((2, 2, rows, 128), bf16)],
        2,
        4 + nx,
        [pltpu.VMEM((slots * panel, 256), bf16)],
        2 * 2 * rows * slots * panel * 256,
    )(offsets, spot, normed, query_gain[None, :], cosine, sine, *query_blocks)

    mine = lax.all_gather(pair, "z", axis=0, tiled=True)
    other = lax.ppermute(mine, "c", swap)
    own_query = lax.dynamic_index_in_dim(query, c, 0, keepdims=False)
    sent_query = lax.dynamic_index_in_dim(query, 1 - c, 0, keepdims=False)
    q0 = jnp.concatenate([own_query, lax.ppermute(sent_query, "c", swap)], axis=0)
    q0 = q0.reshape(4 * rows, 128)
    q1 = lax.ppermute(q0, "x", [(i, i - 1) for i in range(1, nx)])
    q2 = lax.ppermute(q0, "x", [(i, i - 2) for i in range(2, nx)])

    base = x * plane
    spread = jnp.stack([own_begin, near_begin, far_begin]) - base
    inside = z * 2 * rows + c * rows
    low = [jnp.clip(spread[s, 0], 0, plane) for s in range(3)]
    high = [inside + rows] + [jnp.where(x + s < nx, plane, 0) for s in (1, 2)]
    ranges = jnp.stack(
        [c, low[0], high[0], low[1], high[1], low[2], high[2], inside]
    ).astype(jnp.int32)
    parts = call(
        attention_kernel,
        [
            jax.ShapeDtypeStruct((4 * rows, 128), f32),
            jax.ShapeDtypeStruct((4 * rows, 128), bf16),
            jax.ShapeDtypeStruct((4 * rows, 128), bf16),
            jax.ShapeDtypeStruct((3, 8, 128), f32),
        ],
        1,
        6,
        [
            pltpu.VMEM((plane, 128), bf16),
            pltpu.VMEM((plane, 128), bf16),
            pltpu.VMEM((4 * rows, 128), f32),
            pltpu.VMEM((4 * rows, 1), f32),
            pltpu.VMEM((4 * rows, 1), f32),
        ],
        4 * rows * plane * 128 * 8,
    )(ranges, spread[:, :, None], mine, other, q0, q1, q2)
    o0, o1, o2, lse = parts
    o1 = lax.ppermute(o1, "x", [(i, i + 1) for i in range(nx - 1)])
    o2 = lax.ppermute(o2, "x", [(i, i + 2) for i in range(nx - 2)])
    l1 = lax.ppermute(lse[1], "x", [(i, i + 1) for i in range(nx - 1)])
    l2 = lax.ppermute(lse[2], "x", [(i, i + 2) for i in range(nx - 2)])
    came = jnp.stack([c, (x >= 1).astype(jnp.int32), (x >= 2).astype(jnp.int32)]).astype(jnp.int32)
    (context,) = call(
        combine_kernel, [jax.ShapeDtypeStruct((rows, 512), bf16)], 1, 6
    )(came, o0, o1, o2, lse[0], l1, l2)

    own_part = lax.dynamic_slice_in_dim(mine, inside, rows, 0)
    other_part = lax.dynamic_slice_in_dim(other, inside, rows, 0)
    keys_fresh = jnp.where(c == 0, own_part, other_part)
    values_fresh = jnp.where(c == 0, other_part, own_part)
    return keys_fresh, values_fresh, context


def solution(mesh):
    fine = Mesh(mesh.devices.reshape(4, 8, 2, 4, 2), ("x", "z", "c", "y", "w"))
    ctx, head = ("x", "z", "c"), ("y", "w")
    in_specs = (P(ctx, head), P(), P(), P(), P(ctx, head), P(ctx), P())
    out_specs = (P(ctx, head), P(ctx, head), P(ctx, head))
    return jax.shard_map(body, mesh=fine, in_specs=in_specs, out_specs=out_specs, check_vma=False)
```

```python
import functools
import math

import jax
import jax.numpy as jnp
from jax import lax
from jax.experimental import pallas as pl
from jax.experimental.pallas import tpu as pltpu
from jax.sharding import Mesh
from jax.sharding import PartitionSpec as P

epsilon = 1e-06
rope_base = 1000000.0
NEG = -1e30
MASKED = -3e38
KEY_BLOCK = 512
NO_SEGMENT = 100.0
VMEM_LIMIT = 48 * 1024 * 1024


def call(kernel, out_shape, n_smem, n_vmem, scratch=(), flops=0):
    specs = [pl.BlockSpec(memory_space=pltpu.SMEM)] * n_smem
    specs += [pl.BlockSpec(memory_space=pltpu.VMEM)] * n_vmem
    n_out = len(out_shape)
    return pl.pallas_call(
        kernel,
        out_shape=out_shape,
        in_specs=specs,
        out_specs=[pl.BlockSpec(memory_space=pltpu.VMEM)] * n_out,
        scratch_shapes=list(scratch),
        compiler_params=pltpu.CompilerParams(vmem_limit_bytes=VMEM_LIMIT),
        cost_estimate=pl.CostEstimate(flops=flops, bytes_accessed=4 << 20, transcendentals=0),
    )


PEER = (0, 4, 2, 6, 1, 5, 3, 7)


def head_norm_rope(v, gain, cosine, sine):
    mean = jnp.mean(v * v, axis=-1, keepdims=True)
    v = v * lax.rsqrt(mean + epsilon) * gain
    return v * cosine + pltpu.roll(v, 64, 1) * sine


def collect(offsets, where, blocks, weights, panel):
    nx = len(blocks)
    nz = blocks[0].shape[0]
    for s in range(nx):
        source = lax.rem(where[2] + nx - s, nx)
        for k in range(nz):
            for c in range(2):
                slot = source * (nz * 2) + (where[1] ^ PEER[k]) * 2 + c
                first = pl.multiple_of(offsets[slot], 16)
                weights[pl.ds(first, panel), :] = blocks[s][k, c * panel : (c + 1) * panel, :]


def pair_kernel(panel, offsets, where, norm_gain, gain, cosine, sine, *refs):
    hidden, blocks = refs[:4], refs[4:-3]
    normed, out, weights = refs[-3:]
    collect(offsets, where, blocks, weights, panel)
    ny, rows, width = hidden[0].shape
    for side in range(2):
        first = pl.multiple_of(rows * (where[0] if side == 0 else 1 - where[0]), rows)
        total = jnp.zeros((rows, 128), jnp.float32)
        for half in range(2):
            for s in range(ny):
                v = hidden[side * 2 + half][s].astype(jnp.float32)
                v = v * v
                for k in range(width // 128):
                    total = total + v[:, k * 128 : (k + 1) * 128]
        mean = jnp.sum(total, axis=-1, keepdims=True) * (1.0 / (2 * ny * width))
        scale = lax.rsqrt(mean + epsilon)
        for half in range(2):
            for s in range(ny):
                source = lax.rem(where[3] + ny - s, ny) * 2 + (where[4] ^ half)
                cols = pl.ds(pl.multiple_of(source * width, 128), width)
                v = hidden[side * 2 + half][s].astype(jnp.float32)
                v = v * scale * norm_gain[:, cols]
                normed[pl.ds(first, rows), cols] = v.astype(jnp.bfloat16)
    v = jnp.dot(normed[...], weights[...], preferred_element_type=jnp.float32)
    keys = head_norm_rope(v, gain[...], cosine[...], sine[...])
    out[...] = jnp.where(where[0] == 0, keys, v).astype(jnp.bfloat16)


def query_kernel(panel, offsets, where, normed, gain, cosine, sine, *refs):
    blocks, out, weights = refs[:-2], refs[-2], refs[-1]
    collect(offsets, where, blocks, weights, panel)
    rows = out.shape[2]
    for side in range(2):
        span = pl.ds(side * rows, rows)
        v = jnp.dot(normed[span, :], weights[...], preferred_element_type=jnp.float32)
        for h in range(2):
            q = head_norm_rope(
                v[:, h * 128 : (h + 1) * 128], gain[...], cosine[span, :], sine[span, :]
            )
            out[side, h] = q.astype(jnp.bfloat16)


def identity_mask():
    shape = (128, 128)
    return lax.broadcasted_iota(jnp.int32, shape, 0) == lax.broadcasted_iota(jnp.int32, shape, 1)


def attend(query, keys, values, begin, index, low, high, acc, top, total):
    rows = begin.shape[0]
    scale = math.log2(math.e) / math.sqrt(128)
    acc[...] = jnp.zeros_like(acc)
    top[...] = jnp.full(top.shape, NEG, jnp.float32)
    total[...] = jnp.zeros_like(total)

    def step(b, carry):
        base = pl.multiple_of(b * KEY_BLOCK, KEY_BLOCK)
        key = keys[pl.ds(base, KEY_BLOCK), :]
        value = values[pl.ds(base, KEY_BLOCK), :]
        col = base + lax.broadcasted_iota(jnp.int32, (rows, KEY_BLOCK), 1)
        allowed = col >= begin
        if index is not None:
            allowed = allowed & (col <= index)
        for h in range(query.shape[0] // rows):
            span = pl.ds(h * rows, rows)
            raw = lax.dot_general(
                query[span, :], key, (((1,), (1,)), ((), ())), preferred_element_type=jnp.float32
            )
            raw = jnp.where(allowed, raw * scale, MASKED)
            old = top[span, :]
            new = jnp.maximum(old, jnp.max(raw, axis=-1, keepdims=True))
            terms = jnp.exp2(raw - new)
            decay = jnp.exp2(old - new)
            top[span, :] = new
            total[span, :] = total[span, :] * decay + jnp.sum(terms, axis=-1, keepdims=True)
            acc[span, :] = acc[span, :] * decay + jnp.dot(
                terms.astype(jnp.bfloat16), value, preferred_element_type=jnp.float32
            )
        return carry

    lax.fori_loop(low // KEY_BLOCK, (high + KEY_BLOCK - 1) // KEY_BLOCK, step, 0)
    summed = total[...]
    safe = jnp.where(summed > 0, summed, 1.0)
    return acc[...] / safe, jnp.where(summed > 0, top[...] + jnp.log2(safe), NEG)


def remote_kernel(where, begins, near, far, mine0, mine1, other0, other1, out1, out2, keys, values, acc, top, total):
    block = mine0.shape[1]
    for core, (first, second) in enumerate((((mine0, mine1), (other0, other1)), ((other0, other1), (mine0, mine1)))):

        @pl.when(where[0] == core)
        def _(first=first, second=second):
            for k in range(8):
                spot = pl.ds(pl.multiple_of((where[1] ^ PEER[k]) * block, block), block)
                keys[spot, :] = first[k // 4][k % 4]
                values[spot, :] = second[k // 4][k % 4]

    eye = identity_mask()
    size = near.shape[0]
    for s, query, out in ((1, near, out1), (2, far, out2)):
        low, high = where[2 + 2 * s], where[3 + 2 * s]
        result, log = attend(query, keys, values, begins[s], None, low, high, acc, top, total)
        out[0:size, :] = result.astype(jnp.bfloat16)
        rest = jnp.concatenate(
            [
                jnp.sum(jnp.where(eye, log[g * 128 : (g + 1) * 128, :], 0.0), axis=0, keepdims=True)
                for g in range(size // 128)
            ]
            + [jnp.zeros((16 - size // 128, 128), jnp.float32)],
            axis=0,
        )
        for part in range(3):
            piece = rest.astype(jnp.bfloat16)
            out[size + 16 * part : size + 16 * (part + 1), :] = piece
            rest = rest - piece.astype(jnp.float32)


def own_kernel(where, begins, query, keys, values, out, log, acc, top, total):
    rows = begins.shape[1]
    index = where[8] + lax.broadcasted_iota(jnp.int32, (rows, 1), 0)
    result, level = attend(
        query, keys, values, begins[0], index, where[2], where[3], acc, top, total
    )
    out[...] = result
    log[...] = level


def combine_kernel(where, o0, l0, r1, r2, out):
    rows = out.shape[0]
    size = o0.shape[0]
    eye = identity_mask()

    def column(ref):
        level = sum(
            ref[size + 16 * part : size + 16 * (part + 1), :].astype(jnp.float32)
            for part in (2, 1, 0)
        )
        pieces = [
            jnp.sum(jnp.where(eye, level[g : g + 1, :], 0.0), axis=1, keepdims=True)
            for g in range(size // 128)
        ]
        return jnp.concatenate(pieces, axis=0)

    a = l0[...]
    b = jnp.where(where[1] == 1, column(r1), NEG)
    c = jnp.where(where[2] == 1, column(r2), NEG)
    top = jnp.maximum(jnp.maximum(a, b), c)
    a, b, c = jnp.exp2(a - top), jnp.exp2(b - top), jnp.exp2(c - top)
    summed = a * o0[...]
    summed = summed + b * r1[0:size, :].astype(jnp.float32) + c * r2[0:size, :].astype(jnp.float32)
    result = (summed / (a + b + c)).astype(jnp.bfloat16)
    for side in range(2):
        first = 256 * (where[0] if side == 0 else 1 - where[0])
        for h in range(2):
            k = side * 2 + h
            cols = pl.ds(pl.multiple_of(first + h * 128, 128), 128)
            out[:, cols] = result[k * rows : (k + 1) * rows, :]


def ring(size, shift):
    return [(i, (i + shift) % size) for i in range(size)]


def across(v, bit):
    return lax.ppermute(v, "z", [(i, i ^ bit) for i in range(8)])


def after(v, *earlier):
    return lax.optimization_barrier((v, *earlier))[0]


def body(hidden, norm_gain, query_gain, key_gain, weight_store, documents, owners):
    x, z, c, y, w = (lax.axis_index(a) for a in ("x", "z", "c", "y", "w"))
    nx, nz, ny = (lax.axis_size(a) for a in ("x", "z", "y"))
    rows = hidden.shape[0]
    slots = owners.shape[0]
    panel = weight_store.shape[0]
    swap = [(0, 1), (1, 0)]
    bf16, f32 = jnp.bfloat16, jnp.float32
    table = jnp.arange(slots, dtype=jnp.int32)

    far_half = lax.ppermute(hidden, "w", swap)

    both = lax.all_gather(weight_store, "c", axis=0, tiled=True)
    pair_docs = lax.all_gather(documents, "c", axis=0)
    riders = jnp.pad(
        pair_docs.astype(bf16), ((0, 0), (0, 256 - rows)), constant_values=NO_SEGMENT
    ).reshape(4, 128)
    pair_cols = jnp.concatenate(
        [
            lax.dynamic_slice_in_dim(both, 512 + 128 * c, 128, 1),
            riders,
            jnp.zeros((12, 128), bf16),
        ],
        axis=0,
    )
    query_cols = lax.dynamic_slice_in_dim(both, 256 * c, 256, 1)

    def spread_z(v, bits):
        for bit in bits:
            v = jnp.concatenate([v, across(v, bit)], axis=0)
        return v

    pair_two = spread_z(pair_cols[None], (4, 2))
    query_one = spread_z(query_cols[None], (4,))
    pair_line = spread_z(pair_two, (1,))
    query_line = spread_z(query_one, (2, 1))
    pair_blocks = [pair_line] + [lax.ppermute(pair_line, "x", ring(nx, s)) for s in (1, 3, 2)]
    pair_blocks = [pair_blocks[i] for i in (0, 1, 3, 2)]
    query_blocks = [query_line] + [lax.ppermute(query_line, "x", ring(nx, s)) for s in (1, 3, 2)]
    query_blocks = [query_blocks[i] for i in (0, 1, 3, 2)]

    def spread_y(v):
        parts = {s: lax.ppermute(v, "y", ring(ny, s)) for s in (1, 3, 2)}
        return jnp.stack([v, parts[1], parts[2], parts[3]])

    own_near = spread_y(hidden)
    other_near = lax.ppermute(own_near, "c", swap)
    own_far = spread_y(far_half)
    other_far = lax.ppermute(own_far, "c", swap)

    riding = jnp.stack([v[:, 2 * panel : 2 * panel + 4, :] for v in pair_blocks]).astype(f32)
    starts = jnp.sum(
        (riding.reshape(-1, 1) < table.astype(f32)[None, :]).astype(f32), axis=0
    ).astype(jnp.int32)

    def begin_of(docs):
        return jnp.sum(
            (docs[:, None] == table[None, :]).astype(jnp.int32) * starts[None, :], axis=1
        )

    pair_begin = begin_of(pair_docs.reshape(-1))
    plane = nz * 2 * rows
    token = x * plane + z * 2 * rows + jnp.arange(2 * rows, dtype=jnp.int32)
    positions = token - pair_begin
    exponent = jnp.arange(64, dtype=f32) * (2.0 / 128)
    frequency = jnp.exp(exponent * -math.log(rope_base))
    angles = positions.astype(f32)[:, None] * frequency[None, :]
    cosine, sine = jnp.cos(angles), jnp.sin(angles)
    cosine = jnp.concatenate([cosine, cosine], axis=1)
    sine = jnp.concatenate([-sine, sine], axis=1)
    spread = [lax.dynamic_slice_in_dim(pair_begin, c * rows, rows, 0)]
    for s in (1, 2):
        docs = lax.dynamic_slice_in_dim(riding[nx - s, 0], 2 * c, 2, 0).reshape(-1)[:rows]
        spread.append(begin_of(docs.astype(jnp.int32)))
    spread = jnp.stack(spread) - x * plane

    offsets = panel * jnp.sum(
        table[:, None] * (owners[:, None] == table[None, :]).astype(jnp.int32), axis=0
    )
    spot = jnp.stack([c, z, x, y, w]).astype(jnp.int32)
    features = norm_gain.shape[0]
    normed, pair = call(
        functools.partial(pair_kernel, panel),
        [
            jax.ShapeDtypeStruct((2 * rows, features), bf16),
            jax.ShapeDtypeStruct((2 * rows, 128), bf16),
        ],
        2,
        8 + nx,
        [pltpu.VMEM((features, 128), bf16)],
        4 * 10**9,
    )(
        offsets, spot, norm_gain.astype(f32)[None, :], key_gain[None, :], cosine, sine,
        own_near, own_far, other_near, other_far, *pair_blocks,
    )
    (query,) = call(
        functools.partial(query_kernel, panel),
        [jax.ShapeDtypeStruct((2, 2, rows, 128), bf16)],
        2,
        4 + nx,
        [pltpu.VMEM((features, 256), bf16)],
        4 * 10**9,
    )(offsets, spot, normed, query_gain[None, :], cosine, sine, *query_blocks)

    mine0 = spread_z(pair[None], (4, 2))
    mine1 = across(mine0, 1)
    other0 = lax.ppermute(mine0, "c", swap)
    other1 = lax.ppermute(mine1, "c", swap)
    own_query = lax.dynamic_index_in_dim(query, c, 0, keepdims=False)
    sent_query = lax.dynamic_index_in_dim(query, 1 - c, 0, keepdims=False)
    q0 = jnp.concatenate([own_query, lax.ppermute(sent_query, "c", swap)], axis=0)
    q0 = q0.reshape(4 * rows, 128)
    q1 = lax.ppermute(q0, "x", [(i, i - 1) for i in range(1, nx)])
    q2 = lax.ppermute(q0, "x", [(i, i - 2) for i in range(2, nx)])

    inside = z * 2 * rows + c * rows
    low = [jnp.clip(spread[s, 0], 0, plane) for s in range(3)]
    high = [inside + rows] + [jnp.where(x + s < nx, plane, 0) for s in (1, 2)]
    ranges = jnp.stack(
        [c, z, low[0], high[0], low[1], high[1], low[2], high[2], inside]
    ).astype(jnp.int32)
    state = [
        pltpu.VMEM((4 * rows, 128), f32),
        pltpu.VMEM((4 * rows, 1), f32),
        pltpu.VMEM((4 * rows, 1), f32),
    ]
    r1, r2, keys, values = call(
        remote_kernel,
        [jax.ShapeDtypeStruct((4 * rows + 48, 128), bf16)] * 2
        + [jax.ShapeDtypeStruct((plane, 128), bf16)] * 2,
        1,
        7,
        state,
        10**10,
    )(ranges, spread[:, :, None], q1, q2, mine0, mine1, other0, other1)
    r1 = lax.ppermute(r1, "x", [(i, i + 1) for i in range(nx - 1)])
    r2 = lax.ppermute(r2, "x", [(i, i + 2) for i in range(nx - 2)])
    o0, l0 = call(
        own_kernel,
        [
            jax.ShapeDtypeStruct((4 * rows, 128), f32),
            jax.ShapeDtypeStruct((4 * rows, 1), f32),
        ],
        1,
        4,
        state,
        10**10,
    )(ranges, spread[:, :, None], q0, keys, values)
    came = jnp.stack([c, (x >= 1).astype(jnp.int32), (x >= 2).astype(jnp.int32)]).astype(jnp.int32)
    (context,) = call(combine_kernel, [jax.ShapeDtypeStruct((rows, 512), bf16)], 1, 4)(
        came, o0, l0, r1, r2
    )

    own_part = lax.dynamic_slice_in_dim(pair, c * rows, rows, 0)
    other_part = lax.dynamic_slice_in_dim(other0[0], c * rows, rows, 0)
    keys_fresh = jnp.where(c == 0, own_part, other_part)
    values_fresh = jnp.where(c == 0, other_part, own_part)
    return keys_fresh, values_fresh, context


def solution(mesh):
    fine = Mesh(mesh.devices.reshape(4, 8, 2, 4, 2), ("x", "z", "c", "y", "w"))
    ctx, head = ("x", "z", "c"), ("y", "w")
    in_specs = (P(ctx, head), P(), P(), P(), P(ctx, head), P(ctx), P())
    out_specs = (P(ctx, head), P(ctx, head), P(ctx, head))
    return jax.shard_map(body, mesh=fine, in_specs=in_specs, out_specs=out_specs, check_vma=False)
```

```python
import functools
import math

import jax
import jax.numpy as jnp
from jax import lax
from jax.experimental import pallas as pl
from jax.experimental.pallas import tpu as pltpu
from jax.sharding import Mesh
from jax.sharding import PartitionSpec as P

epsilon = 1e-06
rope_base = 1000000.0
NEG = -1e30
MASKED = -3e38
KEY_BLOCK = 1024
NO_SEGMENT = 100.0
VMEM_LIMIT = 48 * 1024 * 1024


def call(kernel, out_shape, n_smem, n_vmem, scratch=(), flops=0):
    specs = [pl.BlockSpec(memory_space=pltpu.SMEM)] * n_smem
    specs += [pl.BlockSpec(memory_space=pltpu.VMEM)] * n_vmem
    n_out = len(out_shape)
    return pl.pallas_call(
        kernel,
        out_shape=out_shape,
        in_specs=specs,
        out_specs=[pl.BlockSpec(memory_space=pltpu.VMEM)] * n_out,
        scratch_shapes=list(scratch),
        compiler_params=pltpu.CompilerParams(vmem_limit_bytes=VMEM_LIMIT),
        cost_estimate=pl.CostEstimate(flops=flops, bytes_accessed=4 << 20, transcendentals=0),
    )


PEER = (0, 4, 1, 5, 2, 6, 3, 7)


def head_norm_rope(v, gain, cosine, sine):
    mean = jnp.mean(v * v, axis=-1, keepdims=True)
    v = v * lax.rsqrt(mean + epsilon) * gain
    return v * cosine + pltpu.roll(v, 64, 1) * sine


def collect(offsets, where, blocks, weights, panel):
    nx = len(blocks)
    nz = blocks[0].shape[0]
    for s in range(nx):
        source = lax.rem(where[2] + nx - s, nx)
        for k in range(nz):
            for c in range(2):
                slot = source * (nz * 2) + (where[1] ^ PEER[k]) * 2 + c
                first = pl.multiple_of(offsets[slot], 16)
                weights[pl.ds(first, panel), :] = blocks[s][k, c * panel : (c + 1) * panel, :]


def pair_kernel(panel, offsets, where, norm_gain, gain, cosine, sine, *refs):
    hidden, blocks = refs[:4], refs[4:-3]
    normed, out, weights = refs[-3:]
    collect(offsets, where, blocks, weights, panel)
    ny, rows, width = hidden[0].shape
    for side in range(2):
        first = pl.multiple_of(rows * (where[0] if side == 0 else 1 - where[0]), rows)
        total = jnp.zeros((rows, 128), jnp.float32)
        for half in range(2):
            for s in range(ny):
                v = hidden[side * 2 + half][s].astype(jnp.float32)
                v = v * v
                for k in range(width // 128):
                    total = total + v[:, k * 128 : (k + 1) * 128]
        mean = jnp.sum(total, axis=-1, keepdims=True) * (1.0 / (2 * ny * width))
        scale = lax.rsqrt(mean + epsilon)
        for half in range(2):
            for s in range(ny):
                source = lax.rem(where[3] + ny - s, ny) * 2 + (where[4] ^ half)
                cols = pl.ds(pl.multiple_of(source * width, 128), width)
                v = hidden[side * 2 + half][s].astype(jnp.float32)
                v = v * scale * norm_gain[:, cols]
                normed[pl.ds(first, rows), cols] = v.astype(jnp.bfloat16)
    v = jnp.dot(normed[...], weights[...], preferred_element_type=jnp.float32)
    keys = head_norm_rope(v, gain[...], cosine[...], sine[...])
    out[...] = jnp.where(where[0] == 0, keys, v).astype(jnp.bfloat16)


def query_kernel(panel, offsets, where, normed, gain, cosine, sine, *refs):
    blocks, out, weights = refs[:-2], refs[-2], refs[-1]
    collect(offsets, where, blocks, weights, panel)
    rows = out.shape[2]
    for side in range(2):
        span = pl.ds(side * rows, rows)
        v = jnp.dot(normed[span, :], weights[...], preferred_element_type=jnp.float32)
        for h in range(2):
            q = head_norm_rope(
                v[:, h * 128 : (h + 1) * 128], gain[...], cosine[span, :], sine[span, :]
            )
            out[side, h] = q.astype(jnp.bfloat16)


def identity_mask():
    shape = (128, 128)
    return lax.broadcasted_iota(jnp.int32, shape, 0) == lax.broadcasted_iota(jnp.int32, shape, 1)


def attend(query, keys, values, begin, index, low, high, clear, acc, top):
    rows = begin.shape[0]
    scale = math.log2(math.e) / math.sqrt(128)
    acc[...] = jnp.zeros_like(acc)
    top[...] = jnp.full(top.shape, NEG, jnp.float32)

    def block(base, masked):
        key = keys[pl.ds(base, KEY_BLOCK), :]
        value = values[pl.ds(base, KEY_BLOCK), :]
        if masked:
            col = base + lax.broadcasted_iota(jnp.int32, (rows, KEY_BLOCK), 1)
            allowed = col >= begin
            if index is not None:
                allowed = allowed & (col <= index)
        for h in range(query.shape[0] // rows):
            span = pl.ds(h * rows, rows)
            raw = lax.dot_general(
                query[span, :], key, (((1,), (1,)), ((), ())), preferred_element_type=jnp.float32
            )
            if masked:
                raw = jnp.where(allowed, raw, MASKED)
            old = top[span, :]
            new = jnp.maximum(old, jnp.max(raw, axis=-1, keepdims=True))
            terms = jnp.exp2(raw * scale - new * scale)
            decay = jnp.exp2((old - new) * scale)
            top[span, :] = new
            acc[span, :] = acc[span, :] * decay + jnp.dot(
                terms.astype(jnp.bfloat16), value, preferred_element_type=jnp.float32
            )

    def step(b, carry):
        base = pl.multiple_of(b * KEY_BLOCK, KEY_BLOCK)
        plain = base >= clear
        if index is not None:
            plain = plain & (base + KEY_BLOCK <= high - rows)

        @pl.when(plain)
        def _():
            block(base, False)

        @pl.when(jnp.logical_not(plain))
        def _():
            block(base, True)

        return carry

    lax.fori_loop(low // KEY_BLOCK, (high + KEY_BLOCK - 1) // KEY_BLOCK, step, 0)
    summed = acc[:, 128:]
    safe = jnp.where(summed > 0, summed, 1.0)
    one = safe[:, 0:1]
    return acc[:, :128] / safe, jnp.where(one > 0, top[...] * scale + jnp.log2(one), NEG)


def remote_kernel(where, begins, near, far, *refs):
    mine, other = refs[:4], refs[4:8]
    out1, out2, keys, values, acc, top = refs[8:]
    block = mine[0].shape[1]
    values[:, 128:] = jnp.ones((values.shape[0], 128), values.dtype)
    for core, (first, second) in enumerate(((mine, other), (other, mine))):

        @pl.when(where[0] == core)
        def _(first=first, second=second):
            for k in range(8):
                spot = pl.ds(pl.multiple_of((where[1] ^ PEER[k]) * block, block), block)
                keys[spot, :] = first[k // 2][k % 2]
                values[spot, :128] = second[k // 2][k % 2]

    eye = identity_mask()
    size = near.shape[0]
    for s, query, out in ((1, near, out1), (2, far, out2)):
        limits = [where[3 + 3 * s + i] for i in range(3)]
        result, log = attend(query, keys, values, begins[s], None, *limits, acc, top)
        out[0:size, :] = result.astype(jnp.bfloat16)
        rest = jnp.concatenate(
            [
                jnp.sum(jnp.where(eye, log[g * 128 : (g + 1) * 128, :], 0.0), axis=0, keepdims=True)
                for g in range(size // 128)
            ]
            + [jnp.zeros((16 - size // 128, 128), jnp.float32)],
            axis=0,
        )
        for part in range(3):
            piece = rest.astype(jnp.bfloat16)
            out[size + 16 * part : size + 16 * (part + 1), :] = piece
            rest = rest - piece.astype(jnp.float32)


def own_kernel(where, begins, query, keys, values, out, log, acc, top):
    rows = begins.shape[1]
    index = where[2] + lax.broadcasted_iota(jnp.int32, (rows, 1), 0)
    limits = [where[3 + i] for i in range(3)]
    result, level = attend(query, keys, values, begins[0], index, *limits, acc, top)
    out[...] = result
    log[...] = level


def combine_kernel(where, o0, l0, r1, r2, out):
    rows = out.shape[0]
    size = o0.shape[0]
    eye = identity_mask()

    def column(ref):
        level = sum(
            ref[size + 16 * part : size + 16 * (part + 1), :].astype(jnp.float32)
            for part in (2, 1, 0)
        )
        pieces = [
            jnp.sum(jnp.where(eye, level[g : g + 1, :], 0.0), axis=1, keepdims=True)
            for g in range(size // 128)
        ]
        return jnp.concatenate(pieces, axis=0)

    a = l0[...]
    b = jnp.where(where[1] == 1, column(r1), NEG)
    c = jnp.where(where[2] == 1, column(r2), NEG)
    top = jnp.maximum(jnp.maximum(a, b), c)
    a, b, c = jnp.exp2(a - top), jnp.exp2(b - top), jnp.exp2(c - top)
    summed = a * o0[...]
    summed = summed + b * r1[0:size, :].astype(jnp.float32) + c * r2[0:size, :].astype(jnp.float32)
    result = (summed / (a + b + c)).astype(jnp.bfloat16)
    for side in range(2):
        first = 256 * (where[0] if side == 0 else 1 - where[0])
        for h in range(2):
            k = side * 2 + h
            cols = pl.ds(pl.multiple_of(first + h * 128, 128), 128)
            out[:, cols] = result[k * rows : (k + 1) * rows, :]


def ring(size, shift):
    return [(i, (i + shift) % size) for i in range(size)]


def across(v, bit):
    return lax.ppermute(v, "z", [(i, i ^ bit) for i in range(8)])


def after(v, *earlier):
    return lax.optimization_barrier((v, *earlier))[0]


def body(hidden, norm_gain, query_gain, key_gain, weight_store, documents, owners):
    x, z, c, y, w = (lax.axis_index(a) for a in ("x", "z", "c", "y", "w"))
    nx, nz, ny = (lax.axis_size(a) for a in ("x", "z", "y"))
    rows = hidden.shape[0]
    slots = owners.shape[0]
    panel = weight_store.shape[0]
    swap = [(0, 1), (1, 0)]
    bf16, f32 = jnp.bfloat16, jnp.float32
    table = jnp.arange(slots, dtype=jnp.int32)

    far_half = lax.ppermute(hidden, "w", swap)

    both = lax.all_gather(weight_store, "c", axis=0, tiled=True)
    twin_docs = lax.ppermute(documents, "c", swap)
    pair_docs = jnp.where(
        c == 0, jnp.stack([documents, twin_docs]), jnp.stack([twin_docs, documents])
    )
    riders = jnp.pad(
        pair_docs.astype(bf16), ((0, 0), (0, 256 - rows)), constant_values=NO_SEGMENT
    ).reshape(4, 128)
    pair_cols = jnp.concatenate(
        [
            lax.dynamic_slice_in_dim(both, 512 + 128 * c, 128, 1),
            riders,
            jnp.zeros((12, 128), bf16),
        ],
        axis=0,
    )
    query_cols = lax.dynamic_slice_in_dim(both, 256 * c, 256, 1)

    def spread_z(half):
        return jnp.concatenate([half] + [across(half, bit) for bit in (1, 2, 3)], axis=0)

    pair_half = jnp.stack([pair_cols, across(pair_cols, 4)])
    pair_line = spread_z(pair_half)
    query_cols = after(query_cols, pair_half)
    query_line = spread_z(jnp.stack([query_cols, across(query_cols, 4)]))
    pair_blocks = [pair_line] + [lax.ppermute(pair_line, "x", ring(nx, s)) for s in (1, 3, 2)]
    pair_blocks = [pair_blocks[i] for i in (0, 1, 3, 2)]
    query_blocks = [query_line] + [lax.ppermute(query_line, "x", ring(nx, s)) for s in (1, 3, 2)]
    query_blocks = [query_blocks[i] for i in (0, 1, 3, 2)]

    def spread_y(v):
        parts = {s: lax.ppermute(v, "y", ring(ny, s)) for s in (1, 3, 2)}
        return jnp.stack([v, parts[1], parts[2], parts[3]])

    own_near = spread_y(hidden)
    other_near = lax.ppermute(own_near, "c", swap)
    own_far = spread_y(far_half)
    other_far = lax.ppermute(own_far, "c", swap)

    riding = jnp.stack([v[:, 2 * panel : 2 * panel + 4, :] for v in pair_blocks]).astype(f32)
    starts = jnp.sum(
        (riding.reshape(-1, 1) < table.astype(f32)[None, :]).astype(f32), axis=0
    ).astype(jnp.int32)

    def begin_of(docs):
        return jnp.sum(
            (docs[:, None] == table[None, :]).astype(jnp.int32) * starts[None, :], axis=1
        )

    pair_begin = begin_of(pair_docs.reshape(-1))
    plane = nz * 2 * rows
    token = x * plane + z * 2 * rows + jnp.arange(2 * rows, dtype=jnp.int32)
    positions = token - pair_begin
    exponent = jnp.arange(64, dtype=f32) * (2.0 / 128)
    frequency = jnp.exp(exponent * -math.log(rope_base))
    angles = positions.astype(f32)[:, None] * frequency[None, :]
    cosine, sine = jnp.cos(angles), jnp.sin(angles)
    cosine = jnp.concatenate([cosine, cosine], axis=1)
    sine = jnp.concatenate([-sine, sine], axis=1)
    spread = [lax.dynamic_slice_in_dim(pair_begin, c * rows, rows, 0)]
    for s in (1, 2):
        docs = lax.dynamic_slice_in_dim(riding[nx - s, 0], 2 * c, 2, 0).reshape(-1)[:rows]
        spread.append(begin_of(docs.astype(jnp.int32)))
    spread = jnp.stack(spread) - x * plane

    offsets = panel * jnp.sum(
        table[:, None] * (owners[:, None] == table[None, :]).astype(jnp.int32), axis=0
    )
    spot = jnp.stack([c, z, x, y, w]).astype(jnp.int32)
    features = norm_gain.shape[0]
    normed, pair = call(
        functools.partial(pair_kernel, panel),
        [
            jax.ShapeDtypeStruct((2 * rows, features), bf16),
            jax.ShapeDtypeStruct((2 * rows, 128), bf16),
        ],
        2,
        8 + nx,
        [pltpu.VMEM((features, 128), bf16)],
        4 * 10**9,
    )(
        offsets, spot, norm_gain.astype(f32)[None, :], key_gain[None, :], cosine, sine,
        own_near, own_far, other_near, other_far, *pair_blocks,
    )
    (query,) = call(
        functools.partial(query_kernel, panel),
        [jax.ShapeDtypeStruct((2, 2, rows, 128), bf16)],
        2,
        4 + nx,
        [pltpu.VMEM((features, 256), bf16)],
        4 * 10**9,
    )(offsets, spot, normed, query_gain[None, :], cosine, sine, *query_blocks)

    half = jnp.stack([pair, across(pair, 4)])
    mine = [half] + [across(half, bit) for bit in (1, 2, 3)]
    other = [lax.ppermute(v, "c", swap) for v in mine]
    own_query = lax.dynamic_index_in_dim(query, c, 0, keepdims=False)
    sent_query = lax.dynamic_index_in_dim(query, 1 - c, 0, keepdims=False)
    q0 = jnp.concatenate([own_query, lax.ppermute(sent_query, "c", swap)], axis=0)
    q0 = q0.reshape(4 * rows, 128)
    q1 = lax.ppermute(q0, "x", [(i, i - 1) for i in range(1, nx)])
    q2 = lax.ppermute(q0, "x", [(i, i - 2) for i in range(2, nx)])

    inside = z * 2 * rows + c * rows
    low = [jnp.clip(spread[s, 0], 0, plane) for s in range(3)]
    high = [inside + rows] + [jnp.where(x + s < nx, plane, 0) for s in (1, 2)]
    limits = [v for s in range(3) for v in (low[s], high[s], spread[s, rows - 1])]
    ranges = jnp.stack([c, z, inside] + limits).astype(jnp.int32)
    state = [pltpu.VMEM((4 * rows, 256), f32), pltpu.VMEM((4 * rows, 1), f32)]
    r1, r2, keys, values = call(
        remote_kernel,
        [jax.ShapeDtypeStruct((4 * rows + 48, 128), bf16)] * 2
        + [jax.ShapeDtypeStruct((plane, 128 * k), bf16) for k in (1, 2)],
        1,
        11,
        state,
        10**10,
    )(ranges, spread[:, :, None], q1, q2, *mine, *other)
    r1 = lax.ppermute(r1, "x", [(i, i + 1) for i in range(nx - 1)])
    r2 = lax.ppermute(r2, "x", [(i, i + 2) for i in range(nx - 2)])
    o0, l0 = call(
        own_kernel,
        [
            jax.ShapeDtypeStruct((4 * rows, 128), f32),
            jax.ShapeDtypeStruct((4 * rows, 1), f32),
        ],
        1,
        4,
        state,
        10**10,
    )(ranges, spread[:, :, None], q0, keys, values)
    came = jnp.stack([c, (x >= 1).astype(jnp.int32), (x >= 2).astype(jnp.int32)]).astype(jnp.int32)
    (context,) = call(combine_kernel, [jax.ShapeDtypeStruct((rows, 512), bf16)], 1, 4)(
        came, o0, l0, r1, r2
    )

    own_part = lax.dynamic_slice_in_dim(pair, c * rows, rows, 0)
    other_part = lax.dynamic_slice_in_dim(other[0][0], c * rows, rows, 0)
    keys_fresh = jnp.where(c == 0, own_part, other_part)
    values_fresh = jnp.where(c == 0, other_part, own_part)
    return keys_fresh, values_fresh, context


def solution(mesh):
    fine = Mesh(mesh.devices.reshape(4, 8, 2, 4, 2), ("x", "z", "c", "y", "w"))
    ctx, head = ("x", "z", "c"), ("y", "w")
    in_specs = (P(ctx, head), P(), P(), P(), P(ctx, head), P(ctx), P())
    out_specs = (P(ctx, head), P(ctx, head), P(ctx, head))
    return jax.shard_map(body, mesh=fine, in_specs=in_specs, out_specs=out_specs, check_vma=False)
```

```python
import functools
import math

import jax
import jax.numpy as jnp
from jax import lax
from jax.experimental import pallas as pl
from jax.experimental.pallas import tpu as pltpu
from jax.sharding import Mesh
from jax.sharding import PartitionSpec as P

epsilon = 1e-06
rope_base = 1000000.0
NEG = -1e30
MASKED = -3e38
KEY_BLOCK = 1024
NO_SEGMENT = 100.0
VMEM_LIMIT = 20 * 1024 * 1024


def call(kernel, out_shape, n_smem, n_vmem, scratch=(), flops=0):
    specs = [pl.BlockSpec(memory_space=pltpu.SMEM)] * n_smem
    specs += [pl.BlockSpec(memory_space=pltpu.VMEM)] * n_vmem
    n_out = len(out_shape)
    return pl.pallas_call(
        kernel,
        out_shape=out_shape,
        in_specs=specs,
        out_specs=[pl.BlockSpec(memory_space=pltpu.VMEM)] * n_out,
        scratch_shapes=list(scratch),
        compiler_params=pltpu.CompilerParams(vmem_limit_bytes=VMEM_LIMIT),
        cost_estimate=pl.CostEstimate(flops=flops, bytes_accessed=4 << 20, transcendentals=0),
    )


PEER = (0, 4, 2, 6, 1, 5, 3, 7)


def head_norm_rope(v, gain, cosine, sine):
    mean = jnp.mean(v * v, axis=-1, keepdims=True)
    v = v * lax.rsqrt(mean + epsilon) * gain
    return v * cosine + pltpu.roll(v, 64, 1) * sine


def collect(offsets, where, blocks, weights, panel):
    per = blocks[0].shape[0]
    parts = len(PEER) // per
    nx = len(blocks) // parts
    for s in range(nx):
        source = lax.rem(where[2] + nx - s, nx)
        for k, peer in enumerate(PEER):
            for c in range(2):
                slot = source * (2 * len(PEER)) + (where[1] ^ peer) * 2 + c
                first = pl.multiple_of(offsets[slot], 16)
                block = blocks[s * parts + k // per]
                weights[pl.ds(first, panel), :] = block[k % per, c * panel : (c + 1) * panel, :]


def norm_kernel(where, norm_gain, *refs):
    hidden, normed = refs[:-1], refs[-1]
    ny, rows, width = hidden[0].shape
    for side in range(2):
        first = pl.multiple_of(rows * (where[0] if side == 0 else 1 - where[0]), rows)
        total = jnp.zeros((rows, 128), jnp.float32)
        for half in range(2):
            for s in range(ny):
                v = hidden[side * 2 + half][s].astype(jnp.float32)
                v = v * v
                for k in range(width // 128):
                    total = total + v[:, k * 128 : (k + 1) * 128]
        mean = jnp.sum(total, axis=-1, keepdims=True) * (1.0 / (2 * ny * width))
        scale = lax.rsqrt(mean + epsilon)
        for half in range(2):
            for s in range(ny):
                source = lax.rem(where[3] + ny - s, ny) * 2 + (where[4] ^ half)
                cols = pl.ds(pl.multiple_of(source * width, 128), width)
                v = hidden[side * 2 + half][s].astype(jnp.float32)
                v = v * scale * norm_gain[:, cols]
                normed[pl.ds(first, rows), cols] = v.astype(jnp.bfloat16)


def pair_kernel(panel, offsets, where, normed, gain, cosine, sine, *refs):
    blocks, out, weights = refs[:-2], refs[-2], refs[-1]
    collect(offsets, where, blocks, weights, panel)
    v = jnp.dot(normed[...], weights[...], preferred_element_type=jnp.float32)
    keys = head_norm_rope(v, gain[...], cosine[...], sine[...])
    out[...] = jnp.where(where[0] == 0, keys, v).astype(jnp.bfloat16)


def query_kernel(panel, offsets, where, normed, gain, cosine, sine, *refs):
    blocks, out, weights = refs[:-2], refs[-2], refs[-1]
    collect(offsets, where, blocks, weights, panel)
    rows = out.shape[2]
    for side in range(2):
        span = pl.ds(side * rows, rows)
        v = jnp.dot(normed[span, :], weights[...], preferred_element_type=jnp.float32)
        for h in range(2):
            q = head_norm_rope(
                v[:, h * 128 : (h + 1) * 128], gain[...], cosine[span, :], sine[span, :]
            )
            out[side, h] = q.astype(jnp.bfloat16)


def identity_mask():
    shape = (128, 128)
    return lax.broadcasted_iota(jnp.int32, shape, 0) == lax.broadcasted_iota(jnp.int32, shape, 1)


def attend(query, keys, values, begin, index, low, high, clear, acc, top):
    rows = begin.shape[0]
    scale = math.log2(math.e) / math.sqrt(128)
    acc[...] = jnp.zeros_like(acc)
    top[...] = jnp.full(top.shape, NEG, jnp.float32)

    def block(base, masked):
        key = keys[pl.ds(base, KEY_BLOCK), :]
        value = values[pl.ds(base, KEY_BLOCK), :]
        if masked:
            col = base + lax.broadcasted_iota(jnp.int32, (rows, KEY_BLOCK), 1)
            allowed = col >= begin
            if index is not None:
                allowed = allowed & (col <= index)
        for h in range(query.shape[0] // rows):
            span = pl.ds(h * rows, rows)
            raw = lax.dot_general(
                query[span, :], key, (((1,), (1,)), ((), ())), preferred_element_type=jnp.float32
            )
            if masked:
                raw = jnp.where(allowed, raw, MASKED)
            old = top[span, :]
            new = jnp.maximum(old, jnp.max(raw, axis=-1, keepdims=True))
            terms = jnp.exp2(raw * scale - new * scale)
            decay = jnp.exp2((old - new) * scale)
            top[span, :] = new
            acc[span, :] = acc[span, :] * decay + jnp.dot(
                terms.astype(jnp.bfloat16), value, preferred_element_type=jnp.float32
            )

    def step(b, carry):
        base = pl.multiple_of(b * KEY_BLOCK, KEY_BLOCK)
        plain = base >= clear
        if index is not None:
            plain = plain & (base + KEY_BLOCK <= high - rows)

        @pl.when(plain)
        def _():
            block(base, False)

        @pl.when(jnp.logical_not(plain))
        def _():
            block(base, True)

        return carry

    lax.fori_loop(low // KEY_BLOCK, (high + KEY_BLOCK - 1) // KEY_BLOCK, step, 0)
    summed = acc[:, 128:]
    safe = jnp.where(summed > 0, summed, 1.0)
    one = safe[:, 0:1]
    return acc[:, :128] / safe, jnp.where(one > 0, top[...] * scale + jnp.log2(one), NEG)


def remote_kernel(where, begins, near, far, *refs):
    mine, other = refs[:2], refs[2:4]
    out1, out2, keys, values, acc, top = refs[4:]
    block = mine[0].shape[1]
    values[:, 128:] = jnp.ones((values.shape[0], 128), values.dtype)
    for core, (first, second) in enumerate(((mine, other), (other, mine))):

        @pl.when(where[0] == core)
        def _(first=first, second=second):
            for k in range(8):
                spot = pl.ds(pl.multiple_of((where[1] ^ PEER[k]) * block, block), block)
                keys[spot, :] = first[k // 4][k % 4]
                values[spot, :128] = second[k // 4][k % 4]

    eye = identity_mask()
    size = near.shape[0]
    for s, query, out in ((1, near, out1), (2, far, out2)):
        limits = [where[3 + 3 * s + i] for i in range(3)]
        result, log = attend(query, keys, values, begins[s], None, *limits, acc, top)
        out[0:size, :] = result.astype(jnp.bfloat16)
        rest = jnp.concatenate(
            [
                jnp.sum(jnp.where(eye, log[g * 128 : (g + 1) * 128, :], 0.0), axis=0, keepdims=True)
                for g in range(size // 128)
            ]
            + [jnp.zeros((16 - size // 128, 128), jnp.float32)],
            axis=0,
        )
        for part in range(3):
            piece = rest.astype(jnp.bfloat16)
            out[size + 16 * part : size + 16 * (part + 1), :] = piece
            rest = rest - piece.astype(jnp.float32)


def own_kernel(where, begins, query, keys, values, out, log, acc, top):
    rows = begins.shape[1]
    index = where[2] + lax.broadcasted_iota(jnp.int32, (rows, 1), 0)
    limits = [where[3 + i] for i in range(3)]
    result, level = attend(query, keys, values, begins[0], index, *limits, acc, top)
    out[...] = result
    log[...] = level


def combine_kernel(where, o0, l0, r1, r2, out):
    rows = out.shape[0]
    size = o0.shape[0]
    eye = identity_mask()

    def column(ref):
        level = sum(
            ref[size + 16 * part : size + 16 * (part + 1), :].astype(jnp.float32)
            for part in (2, 1, 0)
        )
        pieces = [
            jnp.sum(jnp.where(eye, level[g : g + 1, :], 0.0), axis=1, keepdims=True)
            for g in range(size // 128)
        ]
        return jnp.concatenate(pieces, axis=0)

    a = l0[...]
    b = jnp.where(where[1] == 1, column(r1), NEG)
    c = jnp.where(where[2] == 1, column(r2), NEG)
    top = jnp.maximum(jnp.maximum(a, b), c)
    a, b, c = jnp.exp2(a - top), jnp.exp2(b - top), jnp.exp2(c - top)
    summed = a * o0[...]
    summed = summed + b * r1[0:size, :].astype(jnp.float32) + c * r2[0:size, :].astype(jnp.float32)
    result = (summed / (a + b + c)).astype(jnp.bfloat16)
    for side in range(2):
        first = 256 * (where[0] if side == 0 else 1 - where[0])
        for h in range(2):
            k = side * 2 + h
            cols = pl.ds(pl.multiple_of(first + h * 128, 128), 128)
            out[:, cols] = result[k * rows : (k + 1) * rows, :]


def ring(size, shift):
    return [(i, (i + shift) % size) for i in range(size)]


def across(v, bit):
    return lax.ppermute(v, "z", [(i, i ^ bit) for i in range(8)])


def after(v, *earlier):
    return lax.optimization_barrier((v, *earlier))[0]


def body(hidden, norm_gain, query_gain, key_gain, weight_store, documents, owners):
    x, z, c, y, w = (lax.axis_index(a) for a in ("x", "z", "c", "y", "w"))
    nx, nz, ny = (lax.axis_size(a) for a in ("x", "z", "y"))
    rows = hidden.shape[0]
    slots = owners.shape[0]
    panel = weight_store.shape[0]
    swap = [(0, 1), (1, 0)]
    bf16, f32 = jnp.bfloat16, jnp.float32
    table = jnp.arange(slots, dtype=jnp.int32)

    def turn(v, axis, size):
        return [lax.ppermute(v, axis, ring(size, s)) for s in range(1, size)]

    riders = jnp.pad(documents.astype(bf16), (0, 256 - rows), constant_values=NO_SEGMENT)
    riders = jnp.pad(riders[None], ((0, 15), (0, weight_store.shape[1] - 256)))
    both = lax.all_gather(jnp.concatenate([weight_store, riders], axis=0), "c", axis=0)
    pair_docs = both[:, panel, :256]
    columns = both[:, :panel].reshape(2 * panel, -1)
    columns = jnp.concatenate(
        [
            lax.dynamic_slice_in_dim(columns, 512 + 128 * c, 128, 1),
            lax.dynamic_slice_in_dim(columns, 256 * c, 256, 1),
        ],
        axis=1,
    )
    tail = jnp.pad(pair_docs.reshape(4, 128), ((0, 12), (0, 256)))
    line = jnp.concatenate([columns, tail], axis=0)[None]
    pair_docs = pair_docs[:, :rows].astype(jnp.int32)

    far = lax.ppermute(hidden, "w", swap)
    near_parts = turn(hidden, "y", ny)
    step = across(line, 4)
    far, step, *near_parts = lax.optimization_barrier((far, step, *near_parts))

    line = jnp.concatenate([line, step], axis=0)
    own_near = jnp.stack([hidden] + near_parts)
    far_parts = turn(far, "y", ny)
    step = across(line, 2)
    other_near = lax.ppermute(own_near, "c", swap)
    step, other_near, *far_parts = lax.optimization_barrier((step, other_near, *far_parts))

    line = jnp.concatenate([line, step], axis=0)
    own_far = jnp.stack([far] + far_parts)
    step = across(line, 1)
    other_far = lax.ppermute(own_far, "c", swap)
    first_parts = turn(line[:, :, :128], "x", nx)
    step, other_far, *first_parts = lax.optimization_barrier((step, other_far, *first_parts))

    second_parts = turn(step[:, :, :128], "x", nx)
    pair_blocks = [
        v
        for both in zip(
            [line[:, :, :128]] + first_parts, [step[:, :, :128]] + second_parts, strict=True
        )
        for v in both
    ]
    query_line = jnp.concatenate([line, step], axis=0)[:, : 2 * panel, 128:]
    query_line = after(query_line, second_parts[0])
    query_blocks = [query_line] + turn(query_line, "x", nx)

    spot = jnp.stack([c, z, x, y, w]).astype(jnp.int32)
    features = norm_gain.shape[0]
    (normed,) = call(
        norm_kernel, [jax.ShapeDtypeStruct((2 * rows, features), bf16)], 1, 5, (), 4 * 10**9
    )(spot, norm_gain.astype(f32)[None, :], own_near, own_far, other_near, other_far)

    riding = jnp.stack([v[:, 2 * panel : 2 * panel + 4, :] for v in pair_blocks]).astype(f32)
    riding = riding.reshape(nx, nz, 4, 128)
    starts = jnp.sum(
        (riding.reshape(-1, 1) < table.astype(f32)[None, :]).astype(f32), axis=0
    ).astype(jnp.int32)

    def begin_of(docs):
        return jnp.sum(
            (docs[:, None] == table[None, :]).astype(jnp.int32) * starts[None, :], axis=1
        )

    pair_begin = begin_of(pair_docs.reshape(-1))
    plane = nz * 2 * rows
    token = x * plane + z * 2 * rows + jnp.arange(2 * rows, dtype=jnp.int32)
    positions = token - pair_begin
    exponent = jnp.arange(64, dtype=f32) * (2.0 / 128)
    frequency = jnp.exp(exponent * -math.log(rope_base))
    angles = positions.astype(f32)[:, None] * frequency[None, :]
    cosine, sine = jnp.cos(angles), jnp.sin(angles)
    cosine = jnp.concatenate([cosine, cosine], axis=1)
    sine = jnp.concatenate([-sine, sine], axis=1)
    spread = [lax.dynamic_slice_in_dim(pair_begin, c * rows, rows, 0)]
    for s in (1, 2):
        docs = lax.dynamic_slice_in_dim(riding[nx - s, 0], 2 * c, 2, 0).reshape(-1)[:rows]
        spread.append(begin_of(docs.astype(jnp.int32)))
    spread = jnp.stack(spread) - x * plane

    offsets = panel * jnp.sum(
        table[:, None] * (owners[:, None] == table[None, :]).astype(jnp.int32), axis=0
    )
    (pair,) = call(
        functools.partial(pair_kernel, panel),
        [jax.ShapeDtypeStruct((2 * rows, 128), bf16)],
        2,
        4 + 2 * nx,
        [pltpu.VMEM((features, 128), bf16)],
        2 * 10**9,
    )(offsets, spot, normed, key_gain[None, :], cosine, sine, *pair_blocks)

    inside = z * 2 * rows + c * rows
    low = [jnp.clip(spread[s, 0], 0, plane) for s in range(3)]
    high = [inside + rows] + [jnp.where(x + s < nx, plane, 0) for s in (1, 2)]
    limits = [v for s in range(3) for v in (low[s], high[s], spread[s, rows - 1])]
    ranges = jnp.stack([c, z, inside] + limits).astype(jnp.int32)
    begins = spread[:, :, None]

    mine0 = jnp.stack([pair, across(pair, 4)])
    mine0, ranges, begins = lax.optimization_barrier((mine0, ranges, begins))
    mine0 = jnp.concatenate([mine0, across(mine0, 2)], axis=0)
    mine1 = across(mine0, 1)
    mine = [mine0, mine1]
    other = [lax.ppermute(v, "c", swap) for v in mine]

    normed = after(normed, mine0)
    (query,) = call(
        functools.partial(query_kernel, panel),
        [jax.ShapeDtypeStruct((2, 2, rows, 128), bf16)],
        2,
        4 + nx,
        [pltpu.VMEM((features, 256), bf16)],
        4 * 10**9,
    )(offsets, spot, normed, query_gain[None, :], cosine, sine, *query_blocks)

    own_query = lax.dynamic_index_in_dim(query, c, 0, keepdims=False)
    sent_query = lax.dynamic_index_in_dim(query, 1 - c, 0, keepdims=False)
    q0 = jnp.concatenate([own_query, lax.ppermute(sent_query, "c", swap)], axis=0)
    q0 = q0.reshape(4 * rows, 128)
    q1 = lax.ppermute(q0, "x", [(i, i - 1) for i in range(1, nx)])
    q2 = lax.ppermute(q0, "x", [(i, i - 2) for i in range(2, nx)])

    state = [pltpu.VMEM((4 * rows, 256), f32), pltpu.VMEM((4 * rows, 1), f32)]
    r1, r2, keys, values = call(
        remote_kernel,
        [jax.ShapeDtypeStruct((4 * rows + 48, 128), bf16)] * 2
        + [jax.ShapeDtypeStruct((plane, 128 * k), bf16) for k in (1, 2)],
        1,
        7,
        state,
        10**10,
    )(ranges, begins, q1, q2, *mine, *other)
    r1 = lax.ppermute(r1, "x", [(i, i + 1) for i in range(nx - 1)])
    r2 = lax.ppermute(r2, "x", [(i, i + 2) for i in range(nx - 2)])
    o0, l0 = call(
        own_kernel,
        [
            jax.ShapeDtypeStruct((4 * rows, 128), f32),
            jax.ShapeDtypeStruct((4 * rows, 1), f32),
        ],
        1,
        4,
        state,
        10**10,
    )(ranges, begins, q0, keys, values)
    came = jnp.stack([c, (x >= 1).astype(jnp.int32), (x >= 2).astype(jnp.int32)]).astype(jnp.int32)
    (context,) = call(combine_kernel, [jax.ShapeDtypeStruct((rows, 512), bf16)], 1, 4)(
        came, o0, l0, r1, r2
    )

    own_part = lax.dynamic_slice_in_dim(pair, c * rows, rows, 0)
    other_part = lax.dynamic_slice_in_dim(other[0][0], c * rows, rows, 0)
    keys_fresh = jnp.where(c == 0, own_part, other_part)
    values_fresh = jnp.where(c == 0, other_part, own_part)
    return keys_fresh, values_fresh, context


def solution(mesh):
    fine = Mesh(mesh.devices.reshape(4, 8, 2, 4, 2), ("x", "z", "c", "y", "w"))
    ctx, head = ("x", "z", "c"), ("y", "w")
    in_specs = (P(ctx, head), P(), P(), P(), P(ctx, head), P(ctx), P())
    out_specs = (P(ctx, head), P(ctx, head), P(ctx, head))
    return jax.shard_map(body, mesh=fine, in_specs=in_specs, out_specs=out_specs, check_vma=False)
```

```python
import functools
import math

import jax
import jax.numpy as jnp
from jax import lax
from jax.experimental import pallas as pl
from jax.experimental.pallas import tpu as pltpu
from jax.sharding import Mesh
from jax.sharding import PartitionSpec as P

epsilon = 1e-06
rope_base = 1000000.0
NEG = -1e30
MASKED = -3e38
KEY_BLOCK = 1024
NO_SEGMENT = 100.0
VMEM_LIMIT = 20 * 1024 * 1024


def call(kernel, out_shape, n_smem, n_vmem, scratch=(), flops=0, n_hbm=0, out_hbm=False):
    specs = [pl.BlockSpec(memory_space=pltpu.SMEM)] * n_smem
    specs += [pl.BlockSpec(memory_space=pltpu.HBM)] * n_hbm
    specs += [pl.BlockSpec(memory_space=pltpu.VMEM)] * n_vmem
    out = pl.BlockSpec(memory_space=pltpu.HBM if out_hbm else pltpu.VMEM)
    return pl.pallas_call(
        kernel,
        out_shape=out_shape,
        in_specs=specs,
        out_specs=[out] * len(out_shape),
        scratch_shapes=list(scratch),
        compiler_params=pltpu.CompilerParams(vmem_limit_bytes=VMEM_LIMIT),
        cost_estimate=pl.CostEstimate(flops=flops, bytes_accessed=4 << 20, transcendentals=0),
    )


PEER = (0, 4, 2, 6, 1, 5, 3, 7)


def head_norm_rope(v, gain, cosine, sine):
    mean = jnp.mean(v * v, axis=-1, keepdims=True)
    v = v * lax.rsqrt(mean + epsilon) * gain
    return v * cosine + pltpu.roll(v, 64, 1) * sine


def collect(offsets, block, source, weights, panel):
    for k in range(block.shape[0]):
        for c in range(2):
            slot = (source * block.shape[0] + k) * 2 + c
            first = pl.multiple_of(offsets[slot], 16)
            weights[pl.ds(first, panel), :] = block[k, c * panel : (c + 1) * panel, :]


def norm_kernel(where, norm_gain, *refs):
    hidden, out, normed, sem = refs[:-3], refs[-3], refs[-2], refs[-1]
    ny, rows, width = hidden[0].shape
    for side in range(2):
        first = pl.multiple_of(rows * (where[0] if side == 0 else 1 - where[0]), rows)
        total = jnp.zeros((rows, 128), jnp.float32)
        for half in range(2):
            for s in range(ny):
                v = hidden[side * 2 + half][s].astype(jnp.float32)
                v = v * v
                for k in range(width // 128):
                    total = total + v[:, k * 128 : (k + 1) * 128]
        mean = jnp.sum(total, axis=-1, keepdims=True) * (1.0 / (2 * ny * width))
        scale = lax.rsqrt(mean + epsilon)
        for half in range(2):
            for s in range(ny):
                cols = pl.ds((s * 2 + half) * width, width)
                v = hidden[side * 2 + half][s].astype(jnp.float32)
                v = v * scale * norm_gain[:, cols]
                normed[pl.ds(first, rows), cols] = v.astype(jnp.bfloat16)
    copy = pltpu.make_async_copy(normed, out, sem)
    copy.start()
    copy.wait()


def pair_kernel(panel, offsets, where, source, gain, cosine, sine, blocks, out, normed, weights, sem):
    copy = pltpu.make_async_copy(source, normed, sem)
    copy.start()
    for s in range(blocks.shape[0]):
        collect(offsets, blocks.at[s], s, weights, panel)
    copy.wait()
    v = jnp.dot(normed[...], weights[...], preferred_element_type=jnp.float32)
    keys = head_norm_rope(v, gain[...], cosine[...], sine[...])
    out[...] = jnp.where(where[0] == 0, keys, v).astype(jnp.bfloat16)


def query_kernel(panel, offsets, where, source, gain, cosine, sine, *refs):
    blocks, (out, normed, weights, sem) = refs[:-4], refs[-4:]
    copy = pltpu.make_async_copy(source, normed, sem)
    copy.start()
    nx = len(blocks)
    for s in range(nx):
        collect(offsets, blocks[s], lax.rem(where[2] + nx - s, nx), weights, panel)
    copy.wait()
    rows = out.shape[2]
    for side in range(2):
        span = pl.ds(side * rows, rows)
        v = jnp.dot(normed[span, :], weights[...], preferred_element_type=jnp.float32)
        for h in range(2):
            q = head_norm_rope(
                v[:, h * 128 : (h + 1) * 128], gain[...], cosine[span, :], sine[span, :]
            )
            out[side, h] = q.astype(jnp.bfloat16)


def identity_mask():
    shape = (128, 128)
    return lax.broadcasted_iota(jnp.int32, shape, 0) == lax.broadcasted_iota(jnp.int32, shape, 1)


def attend(query, keys, values, begin, index, low, high, clear, acc, top):
    rows = begin.shape[0]
    scale = math.log2(math.e) / math.sqrt(128)
    acc[...] = jnp.zeros_like(acc)
    top[...] = jnp.full(top.shape, NEG, jnp.float32)

    def block(base, masked):
        key = keys[pl.ds(base, KEY_BLOCK), :]
        value = values[pl.ds(base, KEY_BLOCK), :]
        if masked:
            col = base + lax.broadcasted_iota(jnp.int32, (rows, KEY_BLOCK), 1)
            allowed = col >= begin
            if index is not None:
                allowed = allowed & (col <= index)
        for h in range(query.shape[0] // rows):
            span = pl.ds(h * rows, rows)
            raw = lax.dot_general(
                query[span, :], key, (((1,), (1,)), ((), ())), preferred_element_type=jnp.float32
            )
            if masked:
                raw = jnp.where(allowed, raw, MASKED)
            old = top[span, :]
            new = jnp.maximum(old, jnp.max(raw, axis=-1, keepdims=True))
            terms = jnp.exp2(raw * scale - new * scale)
            decay = jnp.exp2((old - new) * scale)
            top[span, :] = new
            acc[span, :] = acc[span, :] * decay + jnp.dot(
                terms.astype(jnp.bfloat16), value, preferred_element_type=jnp.float32
            )

    def step(b, carry):
        base = pl.multiple_of(b * KEY_BLOCK, KEY_BLOCK)
        plain = base >= clear
        if index is not None:
            plain = plain & (base + KEY_BLOCK <= high - rows)

        @pl.when(plain)
        def _():
            block(base, False)

        @pl.when(jnp.logical_not(plain))
        def _():
            block(base, True)

        return carry

    lax.fori_loop(low // KEY_BLOCK, (high + KEY_BLOCK - 1) // KEY_BLOCK, step, 0)
    summed = acc[:, 128:]
    safe = jnp.where(summed > 0, summed, 1.0)
    one = safe[:, 0:1]
    return acc[:, :128] / safe, jnp.where(one > 0, top[...] * scale + jnp.log2(one), NEG)


def own_kernel(where, begins, query, *refs):
    mine, other = refs[:2], refs[2:4]
    out, log, keys, values, acc, top = refs[4:]
    block = mine[0].shape[1]
    values[:, 128:] = jnp.ones((values.shape[0], 128), values.dtype)
    for core, (first, second) in enumerate(((mine, other), (other, mine))):

        @pl.when(where[0] == core)
        def _(first=first, second=second):
            for k in range(8):
                spot = pl.ds(pl.multiple_of((where[1] ^ PEER[k]) * block, block), block)
                keys[spot, :] = first[k // 4][k % 4]
                values[spot, :128] = second[k // 4][k % 4]

    rows = begins.shape[1]
    index = where[2] + lax.broadcasted_iota(jnp.int32, (rows, 1), 0)
    limits = [where[3 + i] for i in range(3)]
    result, level = attend(query, keys, values, begins[0], index, *limits, acc, top)
    out[...] = result
    log[...] = level


def remote_kernel(where, begins, near, far, keys, values, out1, out2, acc, top):
    eye = identity_mask()
    size = near.shape[0]
    for s, query, out in ((1, near, out1), (2, far, out2)):
        limits = [where[3 + 3 * s + i] for i in range(3)]
        result, log = attend(query, keys, values, begins[s], None, *limits, acc, top)
        out[0:size, :] = result.astype(jnp.bfloat16)
        rest = jnp.concatenate(
            [
                jnp.sum(jnp.where(eye, log[g * 128 : (g + 1) * 128, :], 0.0), axis=0, keepdims=True)
                for g in range(size // 128)
            ]
            + [jnp.zeros((16 - size // 128, 128), jnp.float32)],
            axis=0,
        )
        for part in range(3):
            piece = rest.astype(jnp.bfloat16)
            out[size + 16 * part : size + 16 * (part + 1), :] = piece
            rest = rest - piece.astype(jnp.float32)


def combine_kernel(where, o0, l0, r1, r2, out):
    rows = out.shape[0]
    size = o0.shape[0]
    eye = identity_mask()

    def column(ref):
        level = sum(
            ref[size + 16 * part : size + 16 * (part + 1), :].astype(jnp.float32)
            for part in (2, 1, 0)
        )
        pieces = [
            jnp.sum(jnp.where(eye, level[g : g + 1, :], 0.0), axis=1, keepdims=True)
            for g in range(size // 128)
        ]
        return jnp.concatenate(pieces, axis=0)

    a = l0[...]
    b = jnp.where(where[1] == 1, column(r1), NEG)
    c = jnp.where(where[2] == 1, column(r2), NEG)
    top = jnp.maximum(jnp.maximum(a, b), c)
    a, b, c = jnp.exp2(a - top), jnp.exp2(b - top), jnp.exp2(c - top)
    summed = a * o0[...]
    summed = summed + b * r1[0:size, :].astype(jnp.float32) + c * r2[0:size, :].astype(jnp.float32)
    result = (summed / (a + b + c)).astype(jnp.bfloat16)
    for side in range(2):
        first = 256 * (where[0] if side == 0 else 1 - where[0])
        for h in range(2):
            k = side * 2 + h
            cols = pl.ds(pl.multiple_of(first + h * 128, 128), 128)
            out[:, cols] = result[k * rows : (k + 1) * rows, :]


def ring(size, shift):
    return [(i, (i + shift) % size) for i in range(size)]


def across(v, bit):
    return lax.ppermute(v, "z", [(i, i ^ bit) for i in range(8)])


def after(v, *earlier):
    return lax.optimization_barrier((v, *earlier))[0]


def body(hidden, norm_gain, query_gain, key_gain, weight_store, documents, owners):
    x, z, c = (lax.axis_index(a) for a in ("x", "z", "c"))
    nx, nz = (lax.axis_size(a) for a in ("x", "z"))
    rows = hidden.shape[0]
    slots = owners.shape[0]
    panel = weight_store.shape[0]
    swap = [(0, 1), (1, 0)]
    bf16, f32 = jnp.bfloat16, jnp.float32
    table = jnp.arange(slots, dtype=jnp.int32)

    riders = jnp.pad(documents.astype(bf16), (0, 256 - rows), constant_values=NO_SEGMENT)
    riders = jnp.pad(riders[None], ((0, 15), (0, weight_store.shape[1] - 256)))
    both = lax.all_gather(jnp.concatenate([weight_store, riders], axis=0), "c", axis=0)
    pair_docs = both[:, panel, :256]
    columns = both[:, :panel].reshape(2 * panel, -1)
    columns = jnp.concatenate(
        [
            lax.dynamic_slice_in_dim(columns, 512 + 128 * c, 128, 1),
            lax.dynamic_slice_in_dim(columns, 256 * c, 256, 1),
        ],
        axis=1,
    )
    tail = jnp.pad(pair_docs.reshape(4, 128), ((0, 12), (0, 256)))
    line = jnp.concatenate([columns, tail], axis=0)
    pair_docs = pair_docs[:, :rows].astype(jnp.int32)

    hidden, line = lax.optimization_barrier((hidden, line))
    line = lax.all_gather(line, "z", axis=0)
    pair_line = jnp.broadcast_to(line[None, :, :, :128], (nx, nz, *line.shape[1:2], 128))
    pair_blocks = lax.all_to_all(pair_line, "x", 0, 0)
    query_line = line[:, : 2 * panel, 128:]

    halves = lax.all_gather(hidden, "w", axis=0)
    own = [lax.all_gather(halves[i], "y", axis=0) for i in range(2)]
    other = [lax.ppermute(v, "c", swap) for v in own]
    spot = jnp.stack([c, z, x]).astype(jnp.int32)
    features = norm_gain.shape[0]
    (normed,) = call(
        norm_kernel,
        [jax.ShapeDtypeStruct((2 * rows, features), bf16)],
        1,
        5,
        [pltpu.VMEM((2 * rows, features), bf16), pltpu.SemaphoreType.DMA],
        4 * 10**9,
        out_hbm=True,
    )(spot, norm_gain.astype(f32)[None, :], *own, *other)

    riding = pair_blocks[:, :, 2 * panel : 2 * panel + 4, :].astype(f32)
    starts = jnp.sum(
        (riding.reshape(-1, 1) < table.astype(f32)[None, :]).astype(f32), axis=0
    ).astype(jnp.int32)

    def begin_of(docs):
        return jnp.sum(
            (docs[:, None] == table[None, :]).astype(jnp.int32) * starts[None, :], axis=1
        )

    pair_begin = begin_of(pair_docs.reshape(-1))
    plane = nz * 2 * rows
    token = x * plane + z * 2 * rows + jnp.arange(2 * rows, dtype=jnp.int32)
    positions = token - pair_begin
    exponent = jnp.arange(64, dtype=f32) * (2.0 / 128)
    frequency = jnp.exp(exponent * -math.log(rope_base))
    angles = positions.astype(f32)[:, None] * frequency[None, :]
    cosine, sine = jnp.cos(angles), jnp.sin(angles)
    cosine = jnp.concatenate([cosine, cosine], axis=1)
    sine = jnp.concatenate([-sine, sine], axis=1)
    spread = [lax.dynamic_slice_in_dim(pair_begin, c * rows, rows, 0)]
    for s in (1, 2):
        place = (jnp.minimum(x + s, nx - 1), z, 2 * c, 0)
        docs = lax.dynamic_slice(riding, place, (1, 1, 2, 128)).reshape(-1)[:rows]
        spread.append(begin_of(docs.astype(jnp.int32)))
    spread = jnp.stack(spread) - x * plane

    offsets = panel * jnp.sum(
        table[:, None] * (owners[:, None] == table[None, :]).astype(jnp.int32), axis=0
    )
    (pair,) = call(
        functools.partial(pair_kernel, panel),
        [jax.ShapeDtypeStruct((2 * rows, 128), bf16)],
        2,
        4,
        [
            pltpu.VMEM((2 * rows, features), bf16),
            pltpu.VMEM((features, 128), bf16),
            pltpu.SemaphoreType.DMA,
        ],
        2 * 10**9,
        n_hbm=1,
    )(offsets, spot, normed, key_gain[None, :], cosine, sine, pair_blocks)
    query_line = after(query_line, pair)
    query_blocks = [query_line] + [
        lax.ppermute(query_line, "x", ring(nx, s)) for s in range(1, nx)
    ]

    inside = z * 2 * rows + c * rows
    low = [jnp.clip(spread[s, 0], 0, plane) for s in range(3)]
    high = [inside + rows] + [jnp.where(x + s < nx, plane, 0) for s in (1, 2)]
    limits = [v for s in range(3) for v in (low[s], high[s], spread[s, rows - 1])]
    ranges = jnp.stack([c, z, inside] + limits).astype(jnp.int32)
    begins = spread[:, :, None]

    mine0 = jnp.stack([pair, across(pair, 4)])
    mine0, ranges, begins = lax.optimization_barrier((mine0, ranges, begins))
    mine0 = jnp.concatenate([mine0, across(mine0, 2)], axis=0)
    mine1 = across(mine0, 1)
    mine = [mine0, mine1]
    other = [lax.ppermute(v, "c", swap) for v in mine]

    normed = after(normed, mine0)
    (query,) = call(
        functools.partial(query_kernel, panel),
        [jax.ShapeDtypeStruct((2, 2, rows, 128), bf16)],
        2,
        3 + nx,
        [
            pltpu.VMEM((2 * rows, features), bf16),
            pltpu.VMEM((features, 256), bf16),
            pltpu.SemaphoreType.DMA,
        ],
        4 * 10**9,
        n_hbm=1,
    )(offsets, spot, normed, query_gain[None, :], cosine, sine, *query_blocks)

    own_query = lax.dynamic_index_in_dim(query, c, 0, keepdims=False)
    sent_query = lax.dynamic_index_in_dim(query, 1 - c, 0, keepdims=False)
    q0 = jnp.concatenate([own_query, lax.ppermute(sent_query, "c", swap)], axis=0)
    q0 = q0.reshape(4 * rows, 128)
    q1 = lax.ppermute(q0, "x", [(i, i - 1) for i in range(1, nx)])
    q2 = lax.ppermute(q0, "x", [(i, i - 2) for i in range(2, nx)])

    state = [pltpu.VMEM((4 * rows, 256), f32), pltpu.VMEM((4 * rows, 1), f32)]
    o0, l0, keys, values = call(
        own_kernel,
        [
            jax.ShapeDtypeStruct((4 * rows, 128), f32),
            jax.ShapeDtypeStruct((4 * rows, 1), f32),
            jax.ShapeDtypeStruct((plane, 128), bf16),
            jax.ShapeDtypeStruct((plane, 256), bf16),
        ],
        1,
        6,
        state,
        10**10,
    )(ranges, begins, q0, *mine, *other)
    r1, r2 = call(
        remote_kernel,
        [jax.ShapeDtypeStruct((4 * rows + 48, 128), bf16)] * 2,
        1,
        5,
        state,
        10**10,
    )(ranges, begins, q1, q2, keys, values)
    r1 = lax.ppermute(r1, "x", [(i, i + 1) for i in range(nx - 1)])
    r2 = lax.ppermute(r2, "x", [(i, i + 2) for i in range(nx - 2)])
    came = jnp.stack([c, (x >= 1).astype(jnp.int32), (x >= 2).astype(jnp.int32)]).astype(jnp.int32)
    (context,) = call(combine_kernel, [jax.ShapeDtypeStruct((rows, 512), bf16)], 1, 4)(
        came, o0, l0, r1, r2
    )

    own_part = lax.dynamic_slice_in_dim(pair, c * rows, rows, 0)
    other_part = lax.dynamic_slice_in_dim(other[0][0], c * rows, rows, 0)
    keys_fresh = jnp.where(c == 0, own_part, other_part)
    values_fresh = jnp.where(c == 0, other_part, own_part)
    return keys_fresh, values_fresh, context


def solution(mesh):
    fine = Mesh(mesh.devices.reshape(4, 8, 2, 4, 2), ("x", "z", "c", "y", "w"))
    ctx, head = ("x", "z", "c"), ("y", "w")
    in_specs = (P(ctx, head), P(), P(), P(), P(ctx, head), P(ctx), P())
    out_specs = (P(ctx, head), P(ctx, head), P(ctx, head))
    return jax.shard_map(body, mesh=fine, in_specs=in_specs, out_specs=out_specs, check_vma=False)
```

```python
import functools
import math

import jax
import jax.numpy as jnp
from jax import lax
from jax.experimental import pallas as pl
from jax.experimental.pallas import tpu as pltpu
from jax.sharding import Mesh
from jax.sharding import PartitionSpec as P

epsilon = 1e-06
rope_base = 1000000.0
NEG = -1e30
MASKED = -3e38
KEY_BLOCK = 1024
NO_SEGMENT = 100.0
VMEM_LIMIT = 20 * 1024 * 1024


def call(kernel, out_shape, n_smem, n_vmem, scratch=(), flops=0, n_hbm=0, out_hbm=False):
    specs = [pl.BlockSpec(memory_space=pltpu.SMEM)] * n_smem
    specs += [pl.BlockSpec(memory_space=pltpu.HBM)] * n_hbm
    specs += [pl.BlockSpec(memory_space=pltpu.VMEM)] * n_vmem
    out = pl.BlockSpec(memory_space=pltpu.HBM if out_hbm else pltpu.VMEM)
    return pl.pallas_call(
        kernel,
        out_shape=out_shape,
        in_specs=specs,
        out_specs=[out] * len(out_shape),
        scratch_shapes=list(scratch),
        compiler_params=pltpu.CompilerParams(vmem_limit_bytes=VMEM_LIMIT),
        cost_estimate=pl.CostEstimate(flops=flops, bytes_accessed=4 << 20, transcendentals=0),
    )


PEER = (0, 4, 2, 6, 1, 5, 3, 7)


def head_norm_rope(v, gain, cosine, sine):
    mean = jnp.mean(v * v, axis=-1, keepdims=True)
    v = v * lax.rsqrt(mean + epsilon) * gain
    return v * cosine + pltpu.roll(v, 64, 1) * sine


def collect(offsets, where, blocks, weights, panel):
    nx, nz = blocks.shape[:2]
    for s in range(nx):
        for k, peer in enumerate(PEER):
            for c in range(2):
                slot = s * (2 * nz) + (where[1] ^ peer) * 2 + c
                first = pl.multiple_of(offsets[slot], 16)
                weights[pl.ds(first, panel), :] = blocks[s, k, c * panel : (c + 1) * panel, :]


def norm_kernel(where, norm_gain, *refs):
    hidden, out, normed, sem = refs[:-3], refs[-3], refs[-2], refs[-1]
    ny, rows, width = hidden[0].shape
    for side in range(2):
        first = pl.multiple_of(rows * (where[0] if side == 0 else 1 - where[0]), rows)
        total = jnp.zeros((rows, 128), jnp.float32)
        for half in range(2):
            for s in range(ny):
                v = hidden[side * 2 + half][s].astype(jnp.float32)
                v = v * v
                for k in range(width // 128):
                    total = total + v[:, k * 128 : (k + 1) * 128]
        mean = jnp.sum(total, axis=-1, keepdims=True) * (1.0 / (2 * ny * width))
        scale = lax.rsqrt(mean + epsilon)
        for half in range(2):
            for s in range(ny):
                source = s * 2 + (where[2] ^ half)
                cols = pl.ds(pl.multiple_of(source * width, 128), width)
                v = hidden[side * 2 + half][s].astype(jnp.float32)
                v = v * scale * norm_gain[:, cols]
                normed[pl.ds(first, rows), cols] = v.astype(jnp.bfloat16)
    copy = pltpu.make_async_copy(normed, out, sem)
    copy.start()
    copy.wait()


def pair_kernel(panel, offsets, where, source, gain, cosine, sine, blocks, out, normed, weights, sem):
    copy = pltpu.make_async_copy(source, normed, sem)
    copy.start()
    collect(offsets, where, blocks, weights, panel)
    copy.wait()
    v = jnp.dot(normed[...], weights[...], preferred_element_type=jnp.float32)
    keys = head_norm_rope(v, gain[...], cosine[...], sine[...])
    out[...] = jnp.where(where[0] == 0, keys, v).astype(jnp.bfloat16)


def query_kernel(panel, offsets, where, source, gain, cosine, sine, blocks, out, normed, weights, sem):
    copy = pltpu.make_async_copy(source, normed, sem)
    copy.start()
    collect(offsets, where, blocks, weights, panel)
    copy.wait()
    rows = out.shape[2]
    for side in range(2):
        span = pl.ds(side * rows, rows)
        v = jnp.dot(normed[span, :], weights[...], preferred_element_type=jnp.float32)
        for h in range(2):
            q = head_norm_rope(
                v[:, h * 128 : (h + 1) * 128], gain[...], cosine[span, :], sine[span, :]
            )
            out[side, h] = q.astype(jnp.bfloat16)


def identity_mask():
    shape = (128, 128)
    return lax.broadcasted_iota(jnp.int32, shape, 0) == lax.broadcasted_iota(jnp.int32, shape, 1)


def attend(query, keys, values, begin, index, low, high, clear, acc, top):
    rows = begin.shape[0]
    scale = math.log2(math.e) / math.sqrt(128)
    acc[...] = jnp.zeros_like(acc)
    top[...] = jnp.full(top.shape, NEG, jnp.float32)

    def block(base, masked):
        key = keys[pl.ds(base, KEY_BLOCK), :]
        value = values[pl.ds(base, KEY_BLOCK), :]
        if masked:
            col = base + lax.broadcasted_iota(jnp.int32, (rows, KEY_BLOCK), 1)
            allowed = col >= begin
            if index is not None:
                allowed = allowed & (col <= index)
        for h in range(query.shape[0] // rows):
            span = pl.ds(h * rows, rows)
            raw = lax.dot_general(
                query[span, :], key, (((1,), (1,)), ((), ())), preferred_element_type=jnp.float32
            )
            if masked:
                raw = jnp.where(allowed, raw, MASKED)
            old = top[span, :]
            new = jnp.maximum(old, jnp.max(raw, axis=-1, keepdims=True))
            terms = jnp.exp2(raw * scale - new * scale)
            decay = jnp.exp2((old - new) * scale)
            top[span, :] = new
            acc[span, :] = acc[span, :] * decay + jnp.dot(
                terms.astype(jnp.bfloat16), value, preferred_element_type=jnp.float32
            )

    def step(b, carry):
        base = pl.multiple_of(b * KEY_BLOCK, KEY_BLOCK)
        plain = base >= clear
        if index is not None:
            plain = plain & (base + KEY_BLOCK <= high - rows)

        @pl.when(plain)
        def _():
            block(base, False)

        @pl.when(jnp.logical_not(plain))
        def _():
            block(base, True)

        return carry

    lax.fori_loop(low // KEY_BLOCK, (high + KEY_BLOCK - 1) // KEY_BLOCK, step, 0)
    summed = acc[:, 128:]
    safe = jnp.where(summed > 0, summed, 1.0)
    one = safe[:, 0:1]
    return acc[:, :128] / safe, jnp.where(one > 0, top[...] * scale + jnp.log2(one), NEG)


def own_kernel(where, begins, query, keys, values, out, log, acc, top):
    rows = begins.shape[1]
    index = where[2] + lax.broadcasted_iota(jnp.int32, (rows, 1), 0)
    limits = [where[3 + i] for i in range(3)]
    result, level = attend(query, keys, values, begins[0], index, *limits, acc, top)
    out[...] = result
    log[...] = level


def remote_kernel(where, begins, near, far, *refs):
    mine, other = refs[:2], refs[2:4]
    out1, out2, keys, values, acc, top = refs[4:]
    block = mine[0].shape[1]
    values[:, 128:] = jnp.ones((values.shape[0], 128), values.dtype)
    for core, (first, second) in enumerate(((mine, other), (other, mine))):

        @pl.when(where[0] == core)
        def _(first=first, second=second):
            for k in range(8):
                spot = pl.ds(pl.multiple_of((where[1] ^ PEER[k]) * block, block), block)
                keys[spot, :] = first[k // 4][k % 4]
                values[spot, :128] = second[k // 4][k % 4]

    eye = identity_mask()
    size = near.shape[0]
    for s, query, out in ((1, near, out1), (2, far, out2)):
        limits = [where[3 + 3 * s + i] for i in range(3)]
        result, log = attend(query, keys, values, begins[s], None, *limits, acc, top)
        out[0:size, :] = result.astype(jnp.bfloat16)
        rest = jnp.concatenate(
            [
                jnp.sum(jnp.where(eye, log[g * 128 : (g + 1) * 128, :], 0.0), axis=0, keepdims=True)
                for g in range(size // 128)
            ]
            + [jnp.zeros((16 - size // 128, 128), jnp.float32)],
            axis=0,
        )
        for part in range(3):
            piece = rest.astype(jnp.bfloat16)
            out[size + 16 * part : size + 16 * (part + 1), :] = piece
            rest = rest - piece.astype(jnp.float32)


def combine_kernel(where, o0, l0, r1, r2, out):
    rows = out.shape[0]
    size = o0.shape[0]
    eye = identity_mask()

    def column(ref):
        level = sum(
            ref[size + 16 * part : size + 16 * (part + 1), :].astype(jnp.float32)
            for part in (2, 1, 0)
        )
        pieces = [
            jnp.sum(jnp.where(eye, level[g : g + 1, :], 0.0), axis=1, keepdims=True)
            for g in range(size // 128)
        ]
        return jnp.concatenate(pieces, axis=0)

    a = l0[...]
    b = jnp.where(where[1] == 1, column(r1), NEG)
    c = jnp.where(where[2] == 1, column(r2), NEG)
    top = jnp.maximum(jnp.maximum(a, b), c)
    a, b, c = jnp.exp2(a - top), jnp.exp2(b - top), jnp.exp2(c - top)
    summed = a * o0[...]
    summed = summed + b * r1[0:size, :].astype(jnp.float32) + c * r2[0:size, :].astype(jnp.float32)
    result = (summed / (a + b + c)).astype(jnp.bfloat16)
    for side in range(2):
        first = 256 * (where[0] if side == 0 else 1 - where[0])
        for h in range(2):
            k = side * 2 + h
            cols = pl.ds(pl.multiple_of(first + h * 128, 128), 128)
            out[:, cols] = result[k * rows : (k + 1) * rows, :]


def across(v, bit):
    return lax.ppermute(v, "z", [(i, i ^ bit) for i in range(8)])


def after(v, *earlier):
    return lax.optimization_barrier((v, *earlier))[0]


def body(hidden, norm_gain, query_gain, key_gain, weight_store, documents, owners):
    x, z, c, w = (lax.axis_index(a) for a in ("x", "z", "c", "w"))
    nx, nz = (lax.axis_size(a) for a in ("x", "z"))
    rows = hidden.shape[0]
    slots = owners.shape[0]
    panel = weight_store.shape[0]
    swap = [(0, 1), (1, 0)]
    bf16, f32 = jnp.bfloat16, jnp.float32
    table = jnp.arange(slots, dtype=jnp.int32)

    riders = jnp.pad(documents.astype(bf16), (0, 256 - rows), constant_values=NO_SEGMENT)
    riders = jnp.pad(riders[None], ((0, 15), (0, weight_store.shape[1] - 256)))
    both = lax.all_gather(jnp.concatenate([weight_store, riders], axis=0), "c", axis=0)
    pair_docs = both[:, panel, :256]
    columns = both[:, :panel].reshape(2 * panel, -1)
    columns = jnp.concatenate(
        [
            lax.dynamic_slice_in_dim(columns, 512 + 128 * c, 128, 1),
            lax.dynamic_slice_in_dim(columns, 256 * c, 256, 1),
        ],
        axis=1,
    )
    tail = jnp.pad(pair_docs.reshape(4, 128), ((0, 12), (0, 256)))
    line = jnp.concatenate([columns, tail], axis=0)
    pair_docs = pair_docs[:, :rows].astype(jnp.int32)

    line = line[None]
    step = across(line, 4)
    far = lax.ppermute(hidden, "w", swap)
    own_near = lax.all_gather(hidden, "y", axis=0)
    step, far, own_near = lax.optimization_barrier((step, far, own_near))

    line = jnp.concatenate([line, step], axis=0)
    step = across(line, 2)
    other_near = lax.ppermute(own_near, "c", swap)
    own_far = lax.all_gather(far, "y", axis=0)
    step, other_near, own_far = lax.optimization_barrier((step, other_near, own_far))

    line = jnp.concatenate([line, step], axis=0)
    step = across(line, 1)
    other_far = lax.ppermute(own_far, "c", swap)
    line = jnp.concatenate([line, step], axis=0)

    def along_x(v):
        return lax.all_to_all(jnp.broadcast_to(v[None], (nx, *v.shape)), "x", 0, 0)

    pair_blocks = along_x(line[:, :, :128])
    query_blocks = along_x(after(line[:, : 2 * panel, 128:], pair_blocks))

    spot = jnp.stack([c, z, w]).astype(jnp.int32)
    features = norm_gain.shape[0]
    (normed,) = call(
        norm_kernel,
        [jax.ShapeDtypeStruct((2 * rows, features), bf16)],
        1,
        5,
        [pltpu.VMEM((2 * rows, features), bf16), pltpu.SemaphoreType.DMA],
        4 * 10**9,
        out_hbm=True,
    )(spot, norm_gain.astype(f32)[None, :], own_near, own_far, other_near, other_far)

    riding = pair_blocks[:, :, 2 * panel : 2 * panel + 4, :].astype(f32)
    starts = jnp.sum(
        (riding.reshape(-1, 1) < table.astype(f32)[None, :]).astype(f32), axis=0
    ).astype(jnp.int32)

    def begin_of(docs):
        return jnp.sum(
            (docs[:, None] == table[None, :]).astype(jnp.int32) * starts[None, :], axis=1
        )

    pair_begin = begin_of(pair_docs.reshape(-1))
    plane = nz * 2 * rows
    token = x * plane + z * 2 * rows + jnp.arange(2 * rows, dtype=jnp.int32)
    positions = token - pair_begin
    exponent = jnp.arange(64, dtype=f32) * (2.0 / 128)
    frequency = jnp.exp(exponent * -math.log(rope_base))
    angles = positions.astype(f32)[:, None] * frequency[None, :]
    cosine, sine = jnp.cos(angles), jnp.sin(angles)
    cosine = jnp.concatenate([cosine, cosine], axis=1)
    sine = jnp.concatenate([-sine, sine], axis=1)
    spread = [lax.dynamic_slice_in_dim(pair_begin, c * rows, rows, 0)]
    for s in (1, 2):
        place = (jnp.minimum(x + s, nx - 1), 0, 2 * c, 0)
        docs = lax.dynamic_slice(riding, place, (1, 1, 2, 128)).reshape(-1)[:rows]
        spread.append(begin_of(docs.astype(jnp.int32)))
    spread = jnp.stack(spread) - x * plane

    offsets = panel * jnp.sum(
        table[:, None] * (owners[:, None] == table[None, :]).astype(jnp.int32), axis=0
    )
    (pair,) = call(
        functools.partial(pair_kernel, panel),
        [jax.ShapeDtypeStruct((2 * rows, 128), bf16)],
        2,
        4,
        [
            pltpu.VMEM((2 * rows, features), bf16),
            pltpu.VMEM((features, 128), bf16),
            pltpu.SemaphoreType.DMA,
        ],
        2 * 10**9,
        n_hbm=1,
    )(offsets, spot, normed, key_gain[None, :], cosine, sine, pair_blocks)

    inside = z * 2 * rows + c * rows
    low = [jnp.clip(spread[s, 0], 0, plane) for s in range(3)]
    high = [inside + rows] + [jnp.where(x + s < nx, plane, 0) for s in (1, 2)]
    limits = [v for s in range(3) for v in (low[s], high[s], spread[s, rows - 1])]
    ranges = jnp.stack([c, z, inside] + limits).astype(jnp.int32)
    begins = spread[:, :, None]

    mine0 = jnp.stack([pair, across(pair, 4)])
    mine0, ranges, begins, query_blocks = lax.optimization_barrier(
        (mine0, ranges, begins, query_blocks)
    )
    mine0 = jnp.concatenate([mine0, across(mine0, 2)], axis=0)
    mine1 = across(mine0, 1)
    mine = [mine0, mine1]
    other = [lax.ppermute(v, "c", swap) for v in mine]

    (query,) = call(
        functools.partial(query_kernel, panel),
        [jax.ShapeDtypeStruct((2, 2, rows, 128), bf16)],
        2,
        4,
        [
            pltpu.VMEM((2 * rows, features), bf16),
            pltpu.VMEM((features, 256), bf16),
            pltpu.SemaphoreType.DMA,
        ],
        4 * 10**9,
        n_hbm=1,
    )(offsets, spot, normed, query_gain[None, :], cosine, sine, query_blocks)

    own_query = lax.dynamic_index_in_dim(query, c, 0, keepdims=False)
    sent_query = lax.dynamic_index_in_dim(query, 1 - c, 0, keepdims=False)
    q0 = jnp.concatenate([own_query, lax.ppermute(sent_query, "c", swap)], axis=0)
    q0 = q0.reshape(4 * rows, 128)
    q1 = lax.ppermute(q0, "x", [(i, i - 1) for i in range(1, nx)])
    q2 = lax.ppermute(q0, "x", [(i, i - 2) for i in range(2, nx)])

    state = [pltpu.VMEM((4 * rows, 256), f32), pltpu.VMEM((4 * rows, 1), f32)]
    r1, r2, keys, values = call(
        remote_kernel,
        [jax.ShapeDtypeStruct((4 * rows + 48, 128), bf16)] * 2
        + [jax.ShapeDtypeStruct((plane, 128 * k), bf16) for k in (1, 2)],
        1,
        7,
        state,
        10**10,
    )(ranges, begins, q1, q2, *mine, *other)
    r1 = lax.ppermute(r1, "x", [(i, i + 1) for i in range(nx - 1)])
    r2 = lax.ppermute(r2, "x", [(i, i + 2) for i in range(nx - 2)])
    o0, l0 = call(
        own_kernel,
        [
            jax.ShapeDtypeStruct((4 * rows, 128), f32),
            jax.ShapeDtypeStruct((4 * rows, 1), f32),
        ],
        1,
        4,
        state,
        10**10,
    )(ranges, begins, q0, keys, values)
    came = jnp.stack([c, (x >= 1).astype(jnp.int32), (x >= 2).astype(jnp.int32)]).astype(jnp.int32)
    (context,) = call(combine_kernel, [jax.ShapeDtypeStruct((rows, 512), bf16)], 1, 4)(
        came, o0, l0, r1, r2
    )

    own_part = lax.dynamic_slice_in_dim(pair, c * rows, rows, 0)
    other_part = lax.dynamic_slice_in_dim(other[0][0], c * rows, rows, 0)
    keys_fresh = jnp.where(c == 0, own_part, other_part)
    values_fresh = jnp.where(c == 0, other_part, own_part)
    return keys_fresh, values_fresh, context


def solution(mesh):
    fine = Mesh(mesh.devices.reshape(4, 8, 2, 4, 2), ("x", "z", "c", "y", "w"))
    ctx, head = ("x", "z", "c"), ("y", "w")
    in_specs = (P(ctx, head), P(), P(), P(), P(ctx, head), P(ctx), P())
    out_specs = (P(ctx, head), P(ctx, head), P(ctx, head))
    return jax.shard_map(body, mesh=fine, in_specs=in_specs, out_specs=out_specs, check_vma=False)
```

```python
import functools
import math

import jax
import jax.numpy as jnp
from jax import lax
from jax.experimental import pallas as pl
from jax.experimental.pallas import tpu as pltpu
from jax.sharding import Mesh
from jax.sharding import PartitionSpec as P

epsilon = 1e-06
rope_base = 1000000.0
NEG = -1e30
MASKED = -3e38
KEY_BLOCK = 1024
NO_SEGMENT = 100.0
VMEM_LIMIT = 20 * 1024 * 1024


def call(kernel, out_shape, n_smem, n_vmem, scratch=(), flops=0, n_hbm=0, out_hbm=False):
    specs = [pl.BlockSpec(memory_space=pltpu.SMEM)] * n_smem
    specs += [pl.BlockSpec(memory_space=pltpu.HBM)] * n_hbm
    specs += [pl.BlockSpec(memory_space=pltpu.VMEM)] * n_vmem
    out = pl.BlockSpec(memory_space=pltpu.HBM if out_hbm else pltpu.VMEM)
    return pl.pallas_call(
        kernel,
        out_shape=out_shape,
        in_specs=specs,
        out_specs=[out] * len(out_shape),
        scratch_shapes=list(scratch),
        compiler_params=pltpu.CompilerParams(vmem_limit_bytes=VMEM_LIMIT),
        cost_estimate=pl.CostEstimate(flops=flops, bytes_accessed=4 << 20, transcendentals=0),
    )


PEER = (0, 4, 2, 6, 1, 5, 3, 7)


def head_norm_rope(v, gain, cosine, sine):
    mean = jnp.mean(v * v, axis=-1, keepdims=True)
    v = v * lax.rsqrt(mean + epsilon) * gain
    return v * cosine + pltpu.roll(v, 64, 1) * sine


def collect(offsets, blocks, weights, panel):
    nx, nz = blocks.shape[:2]
    for s in range(nx):
        for k in range(nz):
            for c in range(2):
                first = pl.multiple_of(offsets[(s * nz + k) * 2 + c], 16)
                weights[pl.ds(first, panel), :] = blocks[s, k, c * panel : (c + 1) * panel, :]


def norm_kernel(where, norm_gain, *refs):
    hidden, out, normed, sem = refs[:-3], refs[-3], refs[-2], refs[-1]
    ny, rows, width = hidden[0].shape
    for side in range(2):
        first = pl.multiple_of(rows * (where[0] if side == 0 else 1 - where[0]), rows)
        total = jnp.zeros((rows, 128), jnp.float32)
        for half in range(2):
            for s in range(ny):
                v = hidden[side * 2 + half][s].astype(jnp.float32)
                v = v * v
                for k in range(width // 128):
                    total = total + v[:, k * 128 : (k + 1) * 128]
        mean = jnp.sum(total, axis=-1, keepdims=True) * (1.0 / (2 * ny * width))
        scale = lax.rsqrt(mean + epsilon)
        for half in range(2):
            for s in range(ny):
                cols = pl.ds((s * 2 + half) * width, width)
                v = hidden[side * 2 + half][s].astype(jnp.float32)
                v = v * scale * norm_gain[:, cols]
                normed[pl.ds(first, rows), cols] = v.astype(jnp.bfloat16)
    copy = pltpu.make_async_copy(normed, out, sem)
    copy.start()
    copy.wait()


def pair_kernel(panel, offsets, where, source, gain, cosine, sine, blocks, out, normed, weights, sem):
    copy = pltpu.make_async_copy(source, normed, sem)
    copy.start()
    collect(offsets, blocks, weights, panel)
    copy.wait()
    v = jnp.dot(normed[...], weights[...], preferred_element_type=jnp.float32)
    keys = head_norm_rope(v, gain[...], cosine[...], sine[...])
    out[...] = jnp.where(where[0] == 0, keys, v).astype(jnp.bfloat16)


def query_kernel(panel, offsets, where, source, gain, cosine, sine, blocks, out, normed, weights, sem):
    copy = pltpu.make_async_copy(source, normed, sem)
    copy.start()
    collect(offsets, blocks, weights, panel)
    copy.wait()
    rows = out.shape[2]
    for side in range(2):
        span = pl.ds(side * rows, rows)
        v = jnp.dot(normed[span, :], weights[...], preferred_element_type=jnp.float32)
        for h in range(2):
            q = head_norm_rope(
                v[:, h * 128 : (h + 1) * 128], gain[...], cosine[span, :], sine[span, :]
            )
            out[side, h] = q.astype(jnp.bfloat16)


def identity_mask():
    shape = (128, 128)
    return lax.broadcasted_iota(jnp.int32, shape, 0) == lax.broadcasted_iota(jnp.int32, shape, 1)


def attend(query, keys, values, begin, index, low, high, clear, acc, top):
    rows = begin.shape[0]
    scale = math.log2(math.e) / math.sqrt(128)
    acc[...] = jnp.zeros_like(acc)
    top[...] = jnp.full(top.shape, NEG, jnp.float32)

    def block(base, masked):
        key = keys[pl.ds(base, KEY_BLOCK), :]
        value = values[pl.ds(base, KEY_BLOCK), :]
        if masked:
            col = base + lax.broadcasted_iota(jnp.int32, (rows, KEY_BLOCK), 1)
            allowed = col >= begin
            if index is not None:
                allowed = allowed & (col <= index)
        for h in range(query.shape[0] // rows):
            span = pl.ds(h * rows, rows)
            raw = lax.dot_general(
                query[span, :], key, (((1,), (1,)), ((), ())), preferred_element_type=jnp.float32
            )
            if masked:
                raw = jnp.where(allowed, raw, MASKED)
            old = top[span, :]
            new = jnp.maximum(old, jnp.max(raw, axis=-1, keepdims=True))
            terms = jnp.exp2(raw * scale - new * scale)
            decay = jnp.exp2((old - new) * scale)
            top[span, :] = new
            acc[span, :] = acc[span, :] * decay + jnp.dot(
                terms.astype(jnp.bfloat16), value, preferred_element_type=jnp.float32
            )

    def step(b, carry):
        base = pl.multiple_of(b * KEY_BLOCK, KEY_BLOCK)
        plain = base >= clear
        if index is not None:
            plain = plain & (base + KEY_BLOCK <= high - rows)

        @pl.when(plain)
        def _():
            block(base, False)

        @pl.when(jnp.logical_not(plain))
        def _():
            block(base, True)

        return carry

    lax.fori_loop(low // KEY_BLOCK, (high + KEY_BLOCK - 1) // KEY_BLOCK, step, 0)
    summed = acc[:, 128:]
    safe = jnp.where(summed > 0, summed, 1.0)
    one = safe[:, 0:1]
    return acc[:, :128] / safe, jnp.where(one > 0, top[...] * scale + jnp.log2(one), NEG)


def own_kernel(where, begins, query, keys, values, out, log, acc, top):
    rows = begins.shape[1]
    index = where[2] + lax.broadcasted_iota(jnp.int32, (rows, 1), 0)
    limits = [where[3 + i] for i in range(3)]
    result, level = attend(query, keys, values, begins[0], index, *limits, acc, top)
    out[...] = result
    log[...] = level


def remote_kernel(where, begins, near, far, *refs):
    mine, other = refs[:2], refs[2:4]
    out1, out2, keys, values, acc, top = refs[4:]
    block = mine[0].shape[1]
    values[:, 128:] = jnp.ones((values.shape[0], 128), values.dtype)
    for core, (first, second) in enumerate(((mine, other), (other, mine))):

        @pl.when(where[0] == core)
        def _(first=first, second=second):
            for k in range(8):
                spot = pl.ds(pl.multiple_of((where[1] ^ PEER[k]) * block, block), block)
                keys[spot, :] = first[k // 4][k % 4]
                values[spot, :128] = second[k // 4][k % 4]

    eye = identity_mask()
    size = near.shape[0]
    for s, query, out in ((1, near, out1), (2, far, out2)):
        limits = [where[3 + 3 * s + i] for i in range(3)]
        result, log = attend(query, keys, values, begins[s], None, *limits, acc, top)
        out[0:size, :] = result.astype(jnp.bfloat16)
        rest = jnp.concatenate(
            [
                jnp.sum(jnp.where(eye, log[g * 128 : (g + 1) * 128, :], 0.0), axis=0, keepdims=True)
                for g in range(size // 128)
            ]
            + [jnp.zeros((16 - size // 128, 128), jnp.float32)],
            axis=0,
        )
        for part in range(3):
            piece = rest.astype(jnp.bfloat16)
            out[size + 16 * part : size + 16 * (part + 1), :] = piece
            rest = rest - piece.astype(jnp.float32)


def combine_kernel(where, o0, l0, r1, r2, out):
    rows = out.shape[0]
    size = o0.shape[0]
    eye = identity_mask()

    def column(ref):
        level = sum(
            ref[size + 16 * part : size + 16 * (part + 1), :].astype(jnp.float32)
            for part in (2, 1, 0)
        )
        pieces = [
            jnp.sum(jnp.where(eye, level[g : g + 1, :], 0.0), axis=1, keepdims=True)
            for g in range(size // 128)
        ]
        return jnp.concatenate(pieces, axis=0)

    a = l0[...]
    b = jnp.where(where[1] == 1, column(r1), NEG)
    c = jnp.where(where[2] == 1, column(r2), NEG)
    top = jnp.maximum(jnp.maximum(a, b), c)
    a, b, c = jnp.exp2(a - top), jnp.exp2(b - top), jnp.exp2(c - top)
    summed = a * o0[...]
    summed = summed + b * r1[0:size, :].astype(jnp.float32) + c * r2[0:size, :].astype(jnp.float32)
    result = (summed / (a + b + c)).astype(jnp.bfloat16)
    for side in range(2):
        first = 256 * (where[0] if side == 0 else 1 - where[0])
        for h in range(2):
            k = side * 2 + h
            cols = pl.ds(pl.multiple_of(first + h * 128, 128), 128)
            out[:, cols] = result[k * rows : (k + 1) * rows, :]


def across(v, bit):
    return lax.ppermute(v, "z", [(i, i ^ bit) for i in range(8)])


def after(v, *earlier):
    return lax.optimization_barrier((v, *earlier))[0]


def body(hidden, norm_gain, query_gain, key_gain, weight_store, documents, owners):
    x, z, c = (lax.axis_index(a) for a in ("x", "z", "c"))
    nx, nz = (lax.axis_size(a) for a in ("x", "z"))
    rows = hidden.shape[0]
    slots = owners.shape[0]
    panel = weight_store.shape[0]
    swap = [(0, 1), (1, 0)]
    bf16, f32 = jnp.bfloat16, jnp.float32
    table = jnp.arange(slots, dtype=jnp.int32)

    riders = jnp.pad(documents.astype(bf16), (0, 256 - rows), constant_values=NO_SEGMENT)
    riders = jnp.pad(riders[None], ((0, 15), (0, weight_store.shape[1] - 256)))
    both = lax.all_gather(jnp.concatenate([weight_store, riders], axis=0), "c", axis=0)
    pair_docs = both[:, panel, :256]
    columns = both[:, :panel].reshape(2 * panel, -1)
    columns = jnp.concatenate(
        [
            lax.dynamic_slice_in_dim(columns, 512 + 128 * c, 128, 1),
            lax.dynamic_slice_in_dim(columns, 256 * c, 256, 1),
        ],
        axis=1,
    )
    tail = jnp.pad(pair_docs.reshape(4, 128), ((0, 12), (0, 256)))
    line = jnp.concatenate([columns, tail], axis=0)
    pair_docs = pair_docs[:, :rows].astype(jnp.int32)

    hidden, line = lax.optimization_barrier((hidden, line))
    line = lax.all_gather(line, "z", axis=0)

    halves = lax.all_gather(hidden, "w", axis=0)
    own = [lax.all_gather(halves[i], "y", axis=0) for i in range(2)]
    other = [lax.ppermute(v, "c", swap) for v in own]

    pair_line = jnp.broadcast_to(line[None, :, :, :128], (nx, nz, *line.shape[1:2], 128))
    query_line = jnp.broadcast_to(line[None, :, : 2 * panel, 128:], (nx, nz, 2 * panel, 256))
    pair_blocks = lax.all_to_all(pair_line, "x", 0, 0)
    query_blocks = lax.all_to_all(after(query_line, pair_blocks), "x", 0, 0)

    spot = jnp.stack([c, z]).astype(jnp.int32)
    features = norm_gain.shape[0]
    (normed,) = call(
        norm_kernel,
        [jax.ShapeDtypeStruct((2 * rows, features), bf16)],
        1,
        5,
        [pltpu.VMEM((2 * rows, features), bf16), pltpu.SemaphoreType.DMA],
        4 * 10**9,
        out_hbm=True,
    )(spot, norm_gain.astype(f32)[None, :], *own, *other)

    riding = pair_blocks[:, :, 2 * panel : 2 * panel + 4, :].astype(f32)
    starts = jnp.sum(
        (riding.reshape(-1, 1) < table.astype(f32)[None, :]).astype(f32), axis=0
    ).astype(jnp.int32)

    def begin_of(docs):
        return jnp.sum(
            (docs[:, None] == table[None, :]).astype(jnp.int32) * starts[None, :], axis=1
        )

    pair_begin = begin_of(pair_docs.reshape(-1))
    plane = nz * 2 * rows
    token = x * plane + z * 2 * rows + jnp.arange(2 * rows, dtype=jnp.int32)
    positions = token - pair_begin
    exponent = jnp.arange(64, dtype=f32) * (2.0 / 128)
    frequency = jnp.exp(exponent * -math.log(rope_base))
    angles = positions.astype(f32)[:, None] * frequency[None, :]
    cosine, sine = jnp.cos(angles), jnp.sin(angles)
    cosine = jnp.concatenate([cosine, cosine], axis=1)
    sine = jnp.concatenate([-sine, sine], axis=1)
    spread = [lax.dynamic_slice_in_dim(pair_begin, c * rows, rows, 0)]
    for s in (1, 2):
        place = (jnp.minimum(x + s, nx - 1), z, 2 * c, 0)
        docs = lax.dynamic_slice(riding, place, (1, 1, 2, 128)).reshape(-1)[:rows]
        spread.append(begin_of(docs.astype(jnp.int32)))
    spread = jnp.stack(spread) - x * plane

    offsets = panel * jnp.sum(
        table[:, None] * (owners[:, None] == table[None, :]).astype(jnp.int32), axis=0
    )
    (pair,) = call(
        functools.partial(pair_kernel, panel),
        [jax.ShapeDtypeStruct((2 * rows, 128), bf16)],
        2,
        4,
        [
            pltpu.VMEM((2 * rows, features), bf16),
            pltpu.VMEM((features, 128), bf16),
            pltpu.SemaphoreType.DMA,
        ],
        2 * 10**9,
        n_hbm=1,
    )(offsets, spot, normed, key_gain[None, :], cosine, sine, pair_blocks)

    inside = z * 2 * rows + c * rows
    low = [jnp.clip(spread[s, 0], 0, plane) for s in range(3)]
    high = [inside + rows] + [jnp.where(x + s < nx, plane, 0) for s in (1, 2)]
    limits = [v for s in range(3) for v in (low[s], high[s], spread[s, rows - 1])]
    ranges = jnp.stack([c, z, inside] + limits).astype(jnp.int32)
    begins = spread[:, :, None]

    mine0 = jnp.stack([pair, across(pair, 4)])
    mine0, ranges, begins = lax.optimization_barrier((mine0, ranges, begins))
    mine0 = jnp.concatenate([mine0, across(mine0, 2)], axis=0)
    mine0, query_blocks = lax.optimization_barrier((mine0, query_blocks))
    mine1 = across(mine0, 1)
    mine = [mine0, mine1]
    other = [lax.ppermute(v, "c", swap) for v in mine]

    (query,) = call(
        functools.partial(query_kernel, panel),
        [jax.ShapeDtypeStruct((2, 2, rows, 128), bf16)],
        2,
        4,
        [
            pltpu.VMEM((2 * rows, features), bf16),
            pltpu.VMEM((features, 256), bf16),
            pltpu.SemaphoreType.DMA,
        ],
        4 * 10**9,
        n_hbm=1,
    )(offsets, spot, normed, query_gain[None, :], cosine, sine, query_blocks)

    own_query = lax.dynamic_index_in_dim(query, c, 0, keepdims=False)
    sent_query = lax.dynamic_index_in_dim(query, 1 - c, 0, keepdims=False)
    q0 = jnp.concatenate([own_query, lax.ppermute(sent_query, "c", swap)], axis=0)
    q0 = q0.reshape(4 * rows, 128)
    q1 = lax.ppermute(q0, "x", [(i, i - 1) for i in range(1, nx)])
    q2 = lax.ppermute(q0, "x", [(i, i - 2) for i in range(2, nx)])

    state = [pltpu.VMEM((4 * rows, 256), f32), pltpu.VMEM((4 * rows, 1), f32)]
    r1, r2, keys, values = call(
        remote_kernel,
        [jax.ShapeDtypeStruct((4 * rows + 48, 128), bf16)] * 2
        + [jax.ShapeDtypeStruct((plane, 128 * k), bf16) for k in (1, 2)],
        1,
        7,
        state,
        10**10,
    )(ranges, begins, q1, q2, *mine, *other)
    r1 = lax.ppermute(r1, "x", [(i, i + 1) for i in range(nx - 1)])
    r2 = lax.ppermute(r2, "x", [(i, i + 2) for i in range(nx - 2)])
    o0, l0 = call(
        own_kernel,
        [
            jax.ShapeDtypeStruct((4 * rows, 128), f32),
            jax.ShapeDtypeStruct((4 * rows, 1), f32),
        ],
        1,
        4,
        state,
        10**10,
    )(ranges, begins, q0, keys, values)
    came = jnp.stack([c, (x >= 1).astype(jnp.int32), (x >= 2).astype(jnp.int32)]).astype(jnp.int32)
    (context,) = call(combine_kernel, [jax.ShapeDtypeStruct((rows, 512), bf16)], 1, 4)(
        came, o0, l0, r1, r2
    )

    own_part = lax.dynamic_slice_in_dim(pair, c * rows, rows, 0)
    other_part = lax.dynamic_slice_in_dim(other[0][0], c * rows, rows, 0)
    keys_fresh = jnp.where(c == 0, own_part, other_part)
    values_fresh = jnp.where(c == 0, other_part, own_part)
    return keys_fresh, values_fresh, context


def solution(mesh):
    fine = Mesh(mesh.devices.reshape(4, 8, 2, 4, 2), ("x", "z", "c", "y", "w"))
    ctx, head = ("x", "z", "c"), ("y", "w")
    in_specs = (P(ctx, head), P(), P(), P(), P(ctx, head), P(ctx), P())
    out_specs = (P(ctx, head), P(ctx, head), P(ctx, head))
    return jax.shard_map(body, mesh=fine, in_specs=in_specs, out_specs=out_specs, check_vma=False)
```

```python
import functools
import math

import jax
import jax.numpy as jnp
from jax import lax
from jax.experimental import pallas as pl
from jax.experimental.pallas import tpu as pltpu
from jax.sharding import Mesh
from jax.sharding import PartitionSpec as P

epsilon = 1e-06
rope_base = 1000000.0
NEG = -1e30
MASKED = -3e38
KEY_BLOCK = 1024
NO_SEGMENT = 100.0
VMEM_LIMIT = 20 * 1024 * 1024


def call(kernel, out_shape, n_smem, n_vmem, scratch=(), flops=0, n_hbm=0, out_hbm=False):
    specs = [pl.BlockSpec(memory_space=pltpu.SMEM)] * n_smem
    specs += [pl.BlockSpec(memory_space=pltpu.HBM)] * n_hbm
    specs += [pl.BlockSpec(memory_space=pltpu.VMEM)] * n_vmem
    out = pl.BlockSpec(memory_space=pltpu.HBM if out_hbm else pltpu.VMEM)
    return pl.pallas_call(
        kernel,
        out_shape=out_shape,
        in_specs=specs,
        out_specs=[out] * len(out_shape),
        scratch_shapes=list(scratch),
        compiler_params=pltpu.CompilerParams(vmem_limit_bytes=VMEM_LIMIT),
        cost_estimate=pl.CostEstimate(flops=flops, bytes_accessed=4 << 20, transcendentals=0),
    )


def head_norm_rope(v, gain, cosine, sine):
    mean = jnp.mean(v * v, axis=-1, keepdims=True)
    v = v * lax.rsqrt(mean + epsilon) * gain
    return v * cosine + pltpu.roll(v, 64, 1) * sine


def collect(offsets, blocks, weights, panel):
    nx, nz = blocks.shape[:2]
    for s in range(nx):
        for k in range(nz):
            for c in range(2):
                first = pl.multiple_of(offsets[(s * nz + k) * 2 + c], 16)
                weights[pl.ds(first, panel), :] = blocks[s, k, c * panel : (c + 1) * panel, :]


def norm_kernel(where, norm_gain, *refs):
    hidden, out, normed, sem = refs[:-3], refs[-3], refs[-2], refs[-1]
    ny, rows, width = hidden[0].shape
    for side in range(2):
        first = pl.multiple_of(rows * (where[0] if side == 0 else 1 - where[0]), rows)
        total = jnp.zeros((rows, 128), jnp.float32)
        for half in range(2):
            for s in range(ny):
                v = hidden[side * 2 + half][s].astype(jnp.float32)
                v = v * v
                for k in range(width // 128):
                    total = total + v[:, k * 128 : (k + 1) * 128]
        mean = jnp.sum(total, axis=-1, keepdims=True) * (1.0 / (2 * ny * width))
        scale = lax.rsqrt(mean + epsilon)
        for half in range(2):
            for s in range(ny):
                cols = pl.ds((s * 2 + half) * width, width)
                v = hidden[side * 2 + half][s].astype(jnp.float32)
                v = v * scale * norm_gain[:, cols]
                normed[pl.ds(first, rows), cols] = v.astype(jnp.bfloat16)
    copy = pltpu.make_async_copy(normed, out, sem)
    copy.start()
    copy.wait()


def pair_kernel(panel, offsets, where, source, gain, cosine, sine, blocks, out, normed, weights, sem):
    copy = pltpu.make_async_copy(source, normed, sem)
    copy.start()
    collect(offsets, blocks, weights, panel)
    copy.wait()
    v = jnp.dot(normed[...], weights[...], preferred_element_type=jnp.float32)
    keys = head_norm_rope(v, gain[...], cosine[...], sine[...])
    out[...] = jnp.where(where[0] == 0, keys, v).astype(jnp.bfloat16)


def query_kernel(panel, offsets, where, source, gain, cosine, sine, blocks, out, normed, weights, sem):
    copy = pltpu.make_async_copy(source, normed, sem)
    copy.start()
    collect(offsets, blocks, weights, panel)
    copy.wait()
    rows = out.shape[2]
    for side in range(2):
        span = pl.ds(side * rows, rows)
        v = jnp.dot(normed[span, :], weights[...], preferred_element_type=jnp.float32)
        for h in range(2):
            q = head_norm_rope(
                v[:, h * 128 : (h + 1) * 128], gain[...], cosine[span, :], sine[span, :]
            )
            out[side, h] = q.astype(jnp.bfloat16)


def identity_mask():
    shape = (128, 128)
    return lax.broadcasted_iota(jnp.int32, shape, 0) == lax.broadcasted_iota(jnp.int32, shape, 1)


def attend(query, keys, values, begin, index, low, high, clear, acc, top):
    rows = begin.shape[0]
    scale = math.log2(math.e) / math.sqrt(128)
    acc[...] = jnp.zeros_like(acc)
    top[...] = jnp.full(top.shape, NEG, jnp.float32)

    def block(base, masked):
        key = keys[pl.ds(base, KEY_BLOCK), :]
        value = values[pl.ds(base, KEY_BLOCK), :]
        if masked:
            col = base + lax.broadcasted_iota(jnp.int32, (rows, KEY_BLOCK), 1)
            allowed = col >= begin
            if index is not None:
                allowed = allowed & (col <= index)
        for h in range(query.shape[0] // rows):
            span = pl.ds(h * rows, rows)
            raw = lax.dot_general(
                query[span, :], key, (((1,), (1,)), ((), ())), preferred_element_type=jnp.float32
            )
            if masked:
                raw = jnp.where(allowed, raw, MASKED)
            old = top[span, :]
            new = jnp.maximum(old, jnp.max(raw, axis=-1, keepdims=True))
            terms = jnp.exp2(raw * scale - new * scale)
            decay = jnp.exp2((old - new) * scale)
            top[span, :] = new
            acc[span, :] = acc[span, :] * decay + jnp.dot(
                terms.astype(jnp.bfloat16), value, preferred_element_type=jnp.float32
            )

    def step(b, carry):
        base = pl.multiple_of(b * KEY_BLOCK, KEY_BLOCK)
        plain = base >= clear
        if index is not None:
            plain = plain & (base + KEY_BLOCK <= high - rows)

        @pl.when(plain)
        def _():
            block(base, False)

        @pl.when(jnp.logical_not(plain))
        def _():
            block(base, True)

        return carry

    lax.fori_loop(low // KEY_BLOCK, (high + KEY_BLOCK - 1) // KEY_BLOCK, step, 0)
    summed = acc[:, 128:]
    safe = jnp.where(summed > 0, summed, 1.0)
    one = safe[:, 0:1]
    return acc[:, :128] / safe, jnp.where(one > 0, top[...] * scale + jnp.log2(one), NEG)


def own_kernel(where, begins, query, keys, values, out, log, acc, top):
    rows = begins.shape[1]
    index = where[1] + lax.broadcasted_iota(jnp.int32, (rows, 1), 0)
    limits = [where[2 + i] for i in range(3)]
    result, level = attend(query, keys, values, begins[0], index, *limits, acc, top)
    out[...] = result
    log[...] = level


def remote_kernel(where, begins, near, far, *refs):
    mine, other, out1, out2, keys, values, acc, top = refs
    values[:, 128:] = jnp.ones((values.shape[0], 128), values.dtype)
    for core, (first, second) in enumerate(((mine, other), (other, mine))):

        @pl.when(where[0] == core)
        def _(first=first, second=second):
            keys[...] = first[...]
            values[:, :128] = second[...]

    eye = identity_mask()
    size = near.shape[0]
    for s, query, out in ((1, near, out1), (2, far, out2)):
        limits = [where[2 + 3 * s + i] for i in range(3)]
        result, log = attend(query, keys, values, begins[s], None, *limits, acc, top)
        out[0:size, :] = result.astype(jnp.bfloat16)
        rest = jnp.concatenate(
            [
                jnp.sum(jnp.where(eye, log[g * 128 : (g + 1) * 128, :], 0.0), axis=0, keepdims=True)
                for g in range(size // 128)
            ]
            + [jnp.zeros((16 - size // 128, 128), jnp.float32)],
            axis=0,
        )
        for part in range(3):
            piece = rest.astype(jnp.bfloat16)
            out[size + 16 * part : size + 16 * (part + 1), :] = piece
            rest = rest - piece.astype(jnp.float32)


def combine_kernel(where, o0, l0, r1, r2, out):
    rows = out.shape[0]
    size = o0.shape[0]
    eye = identity_mask()

    def column(ref):
        level = sum(
            ref[size + 16 * part : size + 16 * (part + 1), :].astype(jnp.float32)
            for part in (2, 1, 0)
        )
        pieces = [
            jnp.sum(jnp.where(eye, level[g : g + 1, :], 0.0), axis=1, keepdims=True)
            for g in range(size // 128)
        ]
        return jnp.concatenate(pieces, axis=0)

    a = l0[...]
    b = jnp.where(where[1] == 1, column(r1), NEG)
    c = jnp.where(where[2] == 1, column(r2), NEG)
    top = jnp.maximum(jnp.maximum(a, b), c)
    a, b, c = jnp.exp2(a - top), jnp.exp2(b - top), jnp.exp2(c - top)
    summed = a * o0[...]
    summed = summed + b * r1[0:size, :].astype(jnp.float32) + c * r2[0:size, :].astype(jnp.float32)
    result = (summed / (a + b + c)).astype(jnp.bfloat16)
    for side in range(2):
        first = 256 * (where[0] if side == 0 else 1 - where[0])
        for h in range(2):
            k = side * 2 + h
            cols = pl.ds(pl.multiple_of(first + h * 128, 128), 128)
            out[:, cols] = result[k * rows : (k + 1) * rows, :]


def gather(v, axis):
    return lax.all_to_all(jnp.broadcast_to(v[None], (lax.axis_size(axis), *v.shape)), axis, 0, 0)


def after(v, *earlier):
    return lax.optimization_barrier((v, *earlier))[0]


def body(hidden, norm_gain, query_gain, key_gain, weight_store, documents, owners):
    x, z, c = (lax.axis_index(a) for a in ("x", "z", "c"))
    nx, nz = (lax.axis_size(a) for a in ("x", "z"))
    rows = hidden.shape[0]
    slots = owners.shape[0]
    panel = weight_store.shape[0]
    swap = [(0, 1), (1, 0)]
    bf16, f32 = jnp.bfloat16, jnp.float32
    table = jnp.arange(slots, dtype=jnp.int32)

    riders = jnp.pad(documents.astype(bf16), (0, 256 - rows), constant_values=NO_SEGMENT)
    riders = jnp.pad(riders[None], ((0, 15), (0, weight_store.shape[1] - 256)))
    both = lax.all_gather(jnp.concatenate([weight_store, riders], axis=0), "c", axis=0)
    pair_docs = both[:, panel, :256]
    columns = both[:, :panel].reshape(2 * panel, -1)
    pair_line = jnp.concatenate(
        [
            lax.dynamic_slice_in_dim(columns, 512 + 128 * c, 128, 1),
            jnp.pad(pair_docs.reshape(4, 128), ((0, 12), (0, 0))),
        ],
        axis=0,
    )
    query_line = lax.dynamic_slice_in_dim(columns, 256 * c, 256, 1)
    pair_docs = pair_docs[:, :rows].astype(jnp.int32)

    hidden, pair_line, query_line = lax.optimization_barrier((hidden, pair_line, query_line))
    pair_line = gather(pair_line, "z")
    halves = lax.all_gather(hidden, "w", axis=0)
    halves, pair_line, query_line = lax.optimization_barrier((halves, pair_line, query_line))
    pair_blocks = gather(pair_line, "x")
    query_line = gather(query_line, "z")
    own = [lax.all_gather(halves[i], "y", axis=0) for i in range(2)]
    other = [lax.ppermute(v, "c", swap) for v in own]
    own, other, pair_blocks, query_line = lax.optimization_barrier(
        (own, other, pair_blocks, query_line)
    )
    query_blocks = gather(query_line, "x")

    spot = jnp.stack([c]).astype(jnp.int32)
    features = norm_gain.shape[0]
    (normed,) = call(
        norm_kernel,
        [jax.ShapeDtypeStruct((2 * rows, features), bf16)],
        1,
        5,
        [pltpu.VMEM((2 * rows, features), bf16), pltpu.SemaphoreType.DMA],
        4 * 10**9,
        out_hbm=True,
    )(spot, norm_gain.astype(f32)[None, :], *own, *other)

    riding = pair_blocks[:, :, 2 * panel : 2 * panel + 4, :].astype(f32)
    starts = jnp.sum(
        (riding.reshape(-1, 1) < table.astype(f32)[None, :]).astype(f32), axis=0
    ).astype(jnp.int32)

    def begin_of(docs):
        return jnp.sum(
            (docs[:, None] == table[None, :]).astype(jnp.int32) * starts[None, :], axis=1
        )

    pair_begin = begin_of(pair_docs.reshape(-1))
    plane = nz * 2 * rows
    token = x * plane + z * 2 * rows + jnp.arange(2 * rows, dtype=jnp.int32)
    positions = token - pair_begin
    exponent = jnp.arange(64, dtype=f32) * (2.0 / 128)
    frequency = jnp.exp(exponent * -math.log(rope_base))
    angles = positions.astype(f32)[:, None] * frequency[None, :]
    cosine, sine = jnp.cos(angles), jnp.sin(angles)
    cosine = jnp.concatenate([cosine, cosine], axis=1)
    sine = jnp.concatenate([-sine, sine], axis=1)
    spread = [lax.dynamic_slice_in_dim(pair_begin, c * rows, rows, 0)]
    for s in (1, 2):
        place = (jnp.minimum(x + s, nx - 1), z, 2 * c, 0)
        docs = lax.dynamic_slice(riding, place, (1, 1, 2, 128)).reshape(-1)[:rows]
        spread.append(begin_of(docs.astype(jnp.int32)))
    spread = jnp.stack(spread) - x * plane

    offsets = panel * jnp.sum(
        table[:, None] * (owners[:, None] == table[None, :]).astype(jnp.int32), axis=0
    )
    (pair,) = call(
        functools.partial(pair_kernel, panel),
        [jax.ShapeDtypeStruct((2 * rows, 128), bf16)],
        2,
        4,
        [
            pltpu.VMEM((2 * rows, features), bf16),
            pltpu.VMEM((features, 128), bf16),
            pltpu.SemaphoreType.DMA,
        ],
        2 * 10**9,
        n_hbm=1,
    )(offsets, spot, normed, key_gain[None, :], cosine, sine, pair_blocks)

    inside = z * 2 * rows + c * rows
    low = [jnp.clip(spread[s, 0], 0, plane) for s in range(3)]
    high = [inside + rows] + [jnp.where(x + s < nx, plane, 0) for s in (1, 2)]
    limits = [v for s in range(3) for v in (low[s], high[s], spread[s, rows - 1])]
    ranges = jnp.stack([c, inside] + limits).astype(jnp.int32)
    begins = spread[:, :, None]

    mine = gather(pair, "z").reshape(plane, 128)
    other = lax.ppermute(mine, "c", swap)

    (query,) = call(
        functools.partial(query_kernel, panel),
        [jax.ShapeDtypeStruct((2, 2, rows, 128), bf16)],
        2,
        4,
        [
            pltpu.VMEM((2 * rows, features), bf16),
            pltpu.VMEM((features, 256), bf16),
            pltpu.SemaphoreType.DMA,
        ],
        4 * 10**9,
        n_hbm=1,
    )(offsets, spot, normed, query_gain[None, :], cosine, sine, query_blocks)

    query, ranges, begins = lax.optimization_barrier((query, ranges, begins))
    own_query = lax.dynamic_index_in_dim(query, c, 0, keepdims=False)
    sent_query = lax.dynamic_index_in_dim(query, 1 - c, 0, keepdims=False)
    q0 = jnp.concatenate([own_query, lax.ppermute(sent_query, "c", swap)], axis=0)
    q0 = q0.reshape(4 * rows, 128)
    q1 = lax.ppermute(q0, "x", [(i, i - 1) for i in range(1, nx)])
    q2 = lax.ppermute(q0, "x", [(i, i - 2) for i in range(2, nx)])

    state = [pltpu.VMEM((4 * rows, 256), f32), pltpu.VMEM((4 * rows, 1), f32)]
    r1, r2, keys, values = call(
        remote_kernel,
        [jax.ShapeDtypeStruct((4 * rows + 48, 128), bf16)] * 2
        + [jax.ShapeDtypeStruct((plane, 128 * k), bf16) for k in (1, 2)],
        1,
        5,
        state,
        10**10,
    )(ranges, begins, q1, q2, mine, other)
    r1 = lax.ppermute(r1, "x", [(i, i + 1) for i in range(nx - 1)])
    r2 = lax.ppermute(r2, "x", [(i, i + 2) for i in range(nx - 2)])
    o0, l0 = call(
        own_kernel,
        [
            jax.ShapeDtypeStruct((4 * rows, 128), f32),
            jax.ShapeDtypeStruct((4 * rows, 1), f32),
        ],
        1,
        4,
        state,
        10**10,
    )(ranges, begins, q0, keys, values)
    came = jnp.stack([c, (x >= 1).astype(jnp.int32), (x >= 2).astype(jnp.int32)]).astype(jnp.int32)
    (context,) = call(combine_kernel, [jax.ShapeDtypeStruct((rows, 512), bf16)], 1, 4)(
        came, o0, l0, r1, r2
    )

    own_part = lax.dynamic_slice_in_dim(pair, c * rows, rows, 0)
    other_part = lax.dynamic_slice_in_dim(other, inside, rows, 0)
    keys_fresh = jnp.where(c == 0, own_part, other_part)
    values_fresh = jnp.where(c == 0, other_part, own_part)
    return keys_fresh, values_fresh, context


def solution(mesh):
    fine = Mesh(mesh.devices.reshape(4, 8, 2, 4, 2), ("x", "z", "c", "y", "w"))
    ctx, head = ("x", "z", "c"), ("y", "w")
    in_specs = (P(ctx, head), P(), P(), P(), P(ctx, head), P(ctx), P())
    out_specs = (P(ctx, head), P(ctx, head), P(ctx, head))
    return jax.shard_map(body, mesh=fine, in_specs=in_specs, out_specs=out_specs, check_vma=False)
```

```python
import functools
import math

import jax
import jax.numpy as jnp
from jax import lax
from jax.experimental import pallas as pl
from jax.experimental.pallas import tpu as pltpu
from jax.sharding import Mesh
from jax.sharding import PartitionSpec as P

epsilon = 1e-06
rope_base = 1000000.0
NEG = -1e30
MASKED = -3e38
KEY_BLOCK = 1024
NO_SEGMENT = 100.0
VMEM_LIMIT = 14 * 1024 * 1024


def call(kernel, out_shape, n_smem, n_vmem, scratch=(), flops=0, n_hbm=0, out_hbm=False):
    specs = [pl.BlockSpec(memory_space=pltpu.SMEM)] * n_smem
    specs += [pl.BlockSpec(memory_space=pltpu.HBM)] * n_hbm
    specs += [pl.BlockSpec(memory_space=pltpu.VMEM)] * n_vmem
    out = pl.BlockSpec(memory_space=pltpu.HBM if out_hbm else pltpu.VMEM)
    return pl.pallas_call(
        kernel,
        out_shape=out_shape,
        in_specs=specs,
        out_specs=[out] * len(out_shape),
        scratch_shapes=list(scratch),
        compiler_params=pltpu.CompilerParams(vmem_limit_bytes=VMEM_LIMIT),
        cost_estimate=pl.CostEstimate(flops=flops, bytes_accessed=4 << 20, transcendentals=0),
    )


PEER = (0, 4, 2, 6, 1, 5, 3, 7)


def head_norm_rope(v, gain, cosine, sine):
    mean = jnp.mean(v * v, axis=-1, keepdims=True)
    v = v * lax.rsqrt(mean + epsilon) * gain
    return v * cosine + pltpu.roll(v, 64, 1) * sine


def collect(offsets, blocks, weights, panel):
    nx, nz = blocks.shape[:2]
    for s in range(nx):
        for k in range(nz):
            for c in range(2):
                first = pl.multiple_of(offsets[(s * nz + k) * 2 + c], 16)
                weights[pl.ds(first, panel), :] = blocks[s, k, c * panel : (c + 1) * panel, :]


def norm_kernel(where, norm_gain, *refs):
    hidden, out, normed, sem = refs[:-3], refs[-3], refs[-2], refs[-1]
    ny, rows, width = hidden[0].shape
    for side in range(2):
        first = pl.multiple_of(rows * (where[0] if side == 0 else 1 - where[0]), rows)
        total = jnp.zeros((rows, 128), jnp.float32)
        for half in range(2):
            for s in range(ny):
                v = hidden[side * 2 + half][s].astype(jnp.float32)
                v = v * v
                for k in range(width // 128):
                    total = total + v[:, k * 128 : (k + 1) * 128]
        mean = jnp.sum(total, axis=-1, keepdims=True) * (1.0 / (2 * ny * width))
        scale = lax.rsqrt(mean + epsilon)
        for half in range(2):
            for s in range(ny):
                cols = pl.ds((s * 2 + half) * width, width)
                v = hidden[side * 2 + half][s].astype(jnp.float32)
                v = v * scale * norm_gain[:, cols]
                normed[pl.ds(first, rows), cols] = v.astype(jnp.bfloat16)
    copy = pltpu.make_async_copy(normed, out, sem)
    copy.start()
    copy.wait()


def pair_kernel(panel, offsets, where, source, gain, cosine, sine, blocks, out, normed, weights, sem):
    copy = pltpu.make_async_copy(source, normed, sem)
    copy.start()
    collect(offsets, blocks, weights, panel)
    copy.wait()
    v = jnp.dot(normed[...], weights[...], preferred_element_type=jnp.float32)
    keys = head_norm_rope(v, gain[...], cosine[...], sine[...])
    out[...] = jnp.where(where[0] == 0, keys, v).astype(jnp.bfloat16)


def query_kernel(panel, offsets, where, source, gain, cosine, sine, blocks, out, normed, weights, sem):
    copy = pltpu.make_async_copy(source, normed, sem)
    copy.start()
    collect(offsets, blocks, weights, panel)
    copy.wait()
    rows = out.shape[2]
    for side in range(2):
        span = pl.ds(side * rows, rows)
        v = jnp.dot(normed[span, :], weights[...], preferred_element_type=jnp.float32)
        for h in range(2):
            q = head_norm_rope(
                v[:, h * 128 : (h + 1) * 128], gain[...], cosine[span, :], sine[span, :]
            )
            out[side, h] = q.astype(jnp.bfloat16)


def identity_mask():
    shape = (128, 128)
    return lax.broadcasted_iota(jnp.int32, shape, 0) == lax.broadcasted_iota(jnp.int32, shape, 1)


def attend(query, keys, values, begin, index, low, high, clear, acc, top):
    rows = begin.shape[0]
    scale = math.log2(math.e) / math.sqrt(128)
    acc[...] = jnp.zeros_like(acc)
    top[...] = jnp.full(top.shape, NEG, jnp.float32)

    def block(base, masked):
        key = keys[pl.ds(base, KEY_BLOCK), :]
        value = values[pl.ds(base, KEY_BLOCK), :]
        if masked:
            col = base + lax.broadcasted_iota(jnp.int32, (rows, KEY_BLOCK), 1)
            allowed = col >= begin
            if index is not None:
                allowed = allowed & (col <= index)
        for h in range(query.shape[0] // rows):
            span = pl.ds(h * rows, rows)
            raw = lax.dot_general(
                query[span, :], key, (((1,), (1,)), ((), ())), preferred_element_type=jnp.float32
            )
            if masked:
                raw = jnp.where(allowed, raw, MASKED)
            old = top[span, :]
            new = jnp.maximum(old, jnp.max(raw, axis=-1, keepdims=True))
            terms = jnp.exp2(raw * scale - new * scale)
            decay = jnp.exp2((old - new) * scale)
            top[span, :] = new
            acc[span, :] = acc[span, :] * decay + jnp.dot(
                terms.astype(jnp.bfloat16), value, preferred_element_type=jnp.float32
            )

    def step(b, carry):
        base = pl.multiple_of(b * KEY_BLOCK, KEY_BLOCK)
        plain = base >= clear
        if index is not None:
            plain = plain & (base + KEY_BLOCK <= high - rows)

        @pl.when(plain)
        def _():
            block(base, False)

        @pl.when(jnp.logical_not(plain))
        def _():
            block(base, True)

        return carry

    lax.fori_loop(low // KEY_BLOCK, (high + KEY_BLOCK - 1) // KEY_BLOCK, step, 0)
    summed = acc[:, 128:]
    safe = jnp.where(summed > 0, summed, 1.0)
    one = safe[:, 0:1]
    return acc[:, :128] / safe, jnp.where(one > 0, top[...] * scale + jnp.log2(one), NEG)


def own_kernel(where, begins, query, keys, values, out, log, acc, top):
    rows = begins.shape[1]
    index = where[2] + lax.broadcasted_iota(jnp.int32, (rows, 1), 0)
    limits = [where[3 + i] for i in range(3)]
    result, level = attend(query, keys, values, begins[0], index, *limits, acc, top)
    out[...] = result
    log[...] = level


def remote_kernel(where, begins, near, far, *refs):
    mine, other = refs[:2], refs[2:4]
    out1, out2, keys, values, acc, top = refs[4:]
    block = mine[0].shape[1]
    values[:, 128:] = jnp.ones((values.shape[0], 128), values.dtype)
    for core, (first, second) in enumerate(((mine, other), (other, mine))):

        @pl.when(where[0] == core)
        def _(first=first, second=second):
            for k in range(8):
                spot = pl.ds(pl.multiple_of((where[1] ^ PEER[k]) * block, block), block)
                keys[spot, :] = first[k // 4][k % 4]
                values[spot, :128] = second[k // 4][k % 4]

    eye = identity_mask()
    size = near.shape[0]
    for s, query, out in ((1, near, out1), (2, far, out2)):
        limits = [where[3 + 3 * s + i] for i in range(3)]
        result, log = attend(query, keys, values, begins[s], None, *limits, acc, top)
        out[0:size, :] = result.astype(jnp.bfloat16)
        rest = jnp.concatenate(
            [
                jnp.sum(jnp.where(eye, log[g * 128 : (g + 1) * 128, :], 0.0), axis=0, keepdims=True)
                for g in range(size // 128)
            ]
            + [jnp.zeros((16 - size // 128, 128), jnp.float32)],
            axis=0,
        )
        for part in range(3):
            piece = rest.astype(jnp.bfloat16)
            out[size + 16 * part : size + 16 * (part + 1), :] = piece
            rest = rest - piece.astype(jnp.float32)


def combine_kernel(where, o0, l0, r1, r2, out):
    rows = out.shape[0]
    size = o0.shape[0]
    eye = identity_mask()

    def column(ref):
        level = sum(
            ref[size + 16 * part : size + 16 * (part + 1), :].astype(jnp.float32)
            for part in (2, 1, 0)
        )
        pieces = [
            jnp.sum(jnp.where(eye, level[g : g + 1, :], 0.0), axis=1, keepdims=True)
            for g in range(size // 128)
        ]
        return jnp.concatenate(pieces, axis=0)

    a = l0[...]
    b = jnp.where(where[1] == 1, column(r1), NEG)
    c = jnp.where(where[2] == 1, column(r2), NEG)
    top = jnp.maximum(jnp.maximum(a, b), c)
    a, b, c = jnp.exp2(a - top), jnp.exp2(b - top), jnp.exp2(c - top)
    summed = a * o0[...]
    summed = summed + b * r1[0:size, :].astype(jnp.float32) + c * r2[0:size, :].astype(jnp.float32)
    result = (summed / (a + b + c)).astype(jnp.bfloat16)
    for side in range(2):
        first = 256 * (where[0] if side == 0 else 1 - where[0])
        for h in range(2):
            k = side * 2 + h
            cols = pl.ds(pl.multiple_of(first + h * 128, 128), 128)
            out[:, cols] = result[k * rows : (k + 1) * rows, :]


def across(v, bit):
    return lax.ppermute(v, "z", [(i, i ^ bit) for i in range(8)])


def after(v, *earlier):
    return lax.optimization_barrier((v, *earlier))[0]


def body(hidden, norm_gain, query_gain, key_gain, weight_store, documents, owners):
    x, z, c = (lax.axis_index(a) for a in ("x", "z", "c"))
    nx, nz = (lax.axis_size(a) for a in ("x", "z"))
    rows = hidden.shape[0]
    slots = owners.shape[0]
    panel = weight_store.shape[0]
    swap = [(0, 1), (1, 0)]
    bf16, f32 = jnp.bfloat16, jnp.float32
    table = jnp.arange(slots, dtype=jnp.int32)

    riders = jnp.pad(documents.astype(bf16), (0, 256 - rows), constant_values=NO_SEGMENT)
    riders = jnp.pad(riders[None], ((0, 15), (0, weight_store.shape[1] - 256)))
    both = lax.all_gather(jnp.concatenate([weight_store, riders], axis=0), "c", axis=0)
    pair_docs = both[:, panel, :256]
    columns = both[:, :panel].reshape(2 * panel, -1)
    columns = jnp.concatenate(
        [
            lax.dynamic_slice_in_dim(columns, 512 + 128 * c, 128, 1),
            lax.dynamic_slice_in_dim(columns, 256 * c, 256, 1),
        ],
        axis=1,
    )
    tail = jnp.pad(pair_docs.reshape(4, 128), ((0, 12), (0, 256)))
    line = jnp.concatenate([columns, tail], axis=0)
    pair_docs = pair_docs[:, :rows].astype(jnp.int32)

    hidden, line = lax.optimization_barrier((hidden, line))
    line = lax.all_to_all(jnp.broadcast_to(line[None], (nz, *line.shape)), "z", 0, 0)

    halves = lax.all_gather(hidden, "w", axis=0)
    own = [lax.all_gather(halves[i], "y", axis=0) for i in range(2)]
    other = [lax.ppermute(v, "c", swap) for v in own]

    pair_line = jnp.broadcast_to(line[None, :, :, :128], (nx, nz, *line.shape[1:2], 128))
    query_line = jnp.broadcast_to(line[None, :, : 2 * panel, 128:], (nx, nz, 2 * panel, 256))
    pair_blocks = lax.all_to_all(pair_line, "x", 0, 0)
    query_blocks = lax.all_to_all(after(query_line, pair_blocks), "x", 0, 0)

    spot = jnp.stack([c, z]).astype(jnp.int32)
    features = norm_gain.shape[0]
    (normed,) = call(
        norm_kernel,
        [jax.ShapeDtypeStruct((2 * rows, features), bf16)],
        1,
        5,
        [pltpu.VMEM((2 * rows, features), bf16), pltpu.SemaphoreType.DMA],
        4 * 10**9,
        out_hbm=True,
    )(spot, norm_gain.astype(f32)[None, :], *own, *other)

    riding = pair_blocks[:, :, 2 * panel : 2 * panel + 4, :].astype(f32)
    starts = jnp.sum(
        (riding.reshape(-1, 1) < table.astype(f32)[None, :]).astype(f32), axis=0
    ).astype(jnp.int32)

    def begin_of(docs):
        return jnp.sum(
            (docs[:, None] == table[None, :]).astype(jnp.int32) * starts[None, :], axis=1
        )

    pair_begin = begin_of(pair_docs.reshape(-1))
    plane = nz * 2 * rows
    token = x * plane + z * 2 * rows + jnp.arange(2 * rows, dtype=jnp.int32)
    positions = token - pair_begin
    exponent = jnp.arange(64, dtype=f32) * (2.0 / 128)
    frequency = jnp.exp(exponent * -math.log(rope_base))
    angles = positions.astype(f32)[:, None] * frequency[None, :]
    cosine, sine = jnp.cos(angles), jnp.sin(angles)
    cosine = jnp.concatenate([cosine, cosine], axis=1)
    sine = jnp.concatenate([-sine, sine], axis=1)
    spread = [lax.dynamic_slice_in_dim(pair_begin, c * rows, rows, 0)]
    for s in (1, 2):
        place = (jnp.minimum(x + s, nx - 1), z, 2 * c, 0)
        docs = lax.dynamic_slice(riding, place, (1, 1, 2, 128)).reshape(-1)[:rows]
        spread.append(begin_of(docs.astype(jnp.int32)))
    spread = jnp.stack(spread) - x * plane

    offsets = panel * jnp.sum(
        table[:, None] * (owners[:, None] == table[None, :]).astype(jnp.int32), axis=0
    )
    (pair,) = call(
        functools.partial(pair_kernel, panel),
        [jax.ShapeDtypeStruct((2 * rows, 128), bf16)],
        2,
        4,
        [
            pltpu.VMEM((2 * rows, features), bf16),
            pltpu.VMEM((features, 128), bf16),
            pltpu.SemaphoreType.DMA,
        ],
        2 * 10**9,
        n_hbm=1,
    )(offsets, spot, normed, key_gain[None, :], cosine, sine, pair_blocks)

    inside = z * 2 * rows + c * rows
    low = [jnp.clip(spread[s, 0], 0, plane) for s in range(3)]
    high = [inside + rows] + [jnp.where(x + s < nx, plane, 0) for s in (1, 2)]
    limits = [v for s in range(3) for v in (low[s], high[s], spread[s, rows - 1])]
    ranges = jnp.stack([c, z, inside] + limits).astype(jnp.int32)
    begins = spread[:, :, None]

    mine0 = jnp.stack([pair, across(pair, 4)])
    mine0, ranges, begins = lax.optimization_barrier((mine0, ranges, begins))
    mine0 = jnp.concatenate([mine0, across(mine0, 2)], axis=0)
    mine0, query_blocks = lax.optimization_barrier((mine0, query_blocks))
    mine1 = across(mine0, 1)
    mine = [mine0, mine1]
    other = [lax.ppermute(v, "c", swap) for v in mine]

    (query,) = call(
        functools.partial(query_kernel, panel),
        [jax.ShapeDtypeStruct((2, 2, rows, 128), bf16)],
        2,
        4,
        [
            pltpu.VMEM((2 * rows, features), bf16),
            pltpu.VMEM((features, 256), bf16),
            pltpu.SemaphoreType.DMA,
        ],
        4 * 10**9,
        n_hbm=1,
    )(offsets, spot, normed, query_gain[None, :], cosine, sine, query_blocks)

    own_query = lax.dynamic_index_in_dim(query, c, 0, keepdims=False)
    sent_query = lax.dynamic_index_in_dim(query, 1 - c, 0, keepdims=False)
    q0 = jnp.concatenate([own_query, lax.ppermute(sent_query, "c", swap)], axis=0)
    q0 = q0.reshape(4 * rows, 128)
    q1 = lax.ppermute(q0, "x", [(i, i - 1) for i in range(1, nx)])
    q2 = lax.ppermute(q0, "x", [(i, i - 2) for i in range(2, nx)])

    state = [pltpu.VMEM((4 * rows, 256), f32), pltpu.VMEM((4 * rows, 1), f32)]
    r1, r2, keys, values = call(
        remote_kernel,
        [jax.ShapeDtypeStruct((4 * rows + 48, 128), bf16)] * 2
        + [jax.ShapeDtypeStruct((plane, 128 * k), bf16) for k in (1, 2)],
        1,
        7,
        state,
        10**10,
    )(ranges, begins, q1, q2, *mine, *other)
    r1 = lax.ppermute(r1, "x", [(i, i + 1) for i in range(nx - 1)])
    r2 = lax.ppermute(r2, "x", [(i, i + 2) for i in range(nx - 2)])
    o0, l0 = call(
        own_kernel,
        [
            jax.ShapeDtypeStruct((4 * rows, 128), f32),
            jax.ShapeDtypeStruct((4 * rows, 1), f32),
        ],
        1,
        4,
        state,
        10**10,
    )(ranges, begins, q0, keys, values)
    came = jnp.stack([c, (x >= 1).astype(jnp.int32), (x >= 2).astype(jnp.int32)]).astype(jnp.int32)
    (context,) = call(combine_kernel, [jax.ShapeDtypeStruct((rows, 512), bf16)], 1, 4)(
        came, o0, l0, r1, r2
    )

    own_part = lax.dynamic_slice_in_dim(pair, c * rows, rows, 0)
    other_part = lax.dynamic_slice_in_dim(other[0][0], c * rows, rows, 0)
    keys_fresh = jnp.where(c == 0, own_part, other_part)
    values_fresh = jnp.where(c == 0, other_part, own_part)
    return keys_fresh, values_fresh, context


def solution(mesh):
    fine = Mesh(mesh.devices.reshape(4, 8, 2, 4, 2), ("x", "z", "c", "y", "w"))
    ctx, head = ("x", "z", "c"), ("y", "w")
    in_specs = (P(ctx, head), P(), P(), P(), P(ctx, head), P(ctx), P())
    out_specs = (P(ctx, head), P(ctx, head), P(ctx, head))
    return jax.shard_map(body, mesh=fine, in_specs=in_specs, out_specs=out_specs, check_vma=False)
```

```python
import functools
import math

import jax
import jax.numpy as jnp
from jax import lax
from jax.experimental import pallas as pl
from jax.experimental.pallas import tpu as pltpu
from jax.sharding import Mesh
from jax.sharding import PartitionSpec as P

epsilon = 1e-06
rope_base = 1000000.0
NEG = -1e30
MASKED = -3e38
KEY_BLOCK = 1024
NO_SEGMENT = 100.0
VMEM_LIMIT = 14 * 1024 * 1024


def call(kernel, out_shape, n_smem, n_vmem, scratch=(), flops=0, n_hbm=0, out_hbm=False):
    specs = [pl.BlockSpec(memory_space=pltpu.SMEM)] * n_smem
    specs += [pl.BlockSpec(memory_space=pltpu.HBM)] * n_hbm
    specs += [pl.BlockSpec(memory_space=pltpu.VMEM)] * n_vmem
    out = pl.BlockSpec(memory_space=pltpu.HBM if out_hbm else pltpu.VMEM)
    return pl.pallas_call(
        kernel,
        out_shape=out_shape,
        in_specs=specs,
        out_specs=[out] * len(out_shape),
        scratch_shapes=list(scratch),
        compiler_params=pltpu.CompilerParams(vmem_limit_bytes=VMEM_LIMIT),
        cost_estimate=pl.CostEstimate(flops=flops, bytes_accessed=4 << 20, transcendentals=0),
    )


PEER = (0, 4, 2, 6, 1, 5, 3, 7)


def head_norm_rope(v, gain, cosine, sine):
    mean = jnp.mean(v * v, axis=-1, keepdims=True)
    v = v * lax.rsqrt(mean + epsilon) * gain
    return v * cosine + pltpu.roll(v, 64, 1) * sine


def collect(offsets, where, blocks, weights, panel):
    nx, nz = blocks.shape[:2]
    for s in range(nx):
        for k, peer in enumerate(PEER):
            for c in range(2):
                slot = s * (2 * nz) + (where[1] ^ peer) * 2 + c
                first = pl.multiple_of(offsets[slot], 16)
                weights[pl.ds(first, panel), :] = blocks[s, k, c * panel : (c + 1) * panel, :]


def norm_kernel(where, norm_gain, *refs):
    hidden, out, normed, sem = refs[:-3], refs[-3], refs[-2], refs[-1]
    ny, rows, width = hidden[0].shape
    for side in range(2):
        first = pl.multiple_of(rows * (where[0] if side == 0 else 1 - where[0]), rows)
        total = jnp.zeros((rows, 128), jnp.float32)
        for half in range(2):
            for s in range(ny):
                v = hidden[side * 2 + half][s].astype(jnp.float32)
                v = v * v
                for k in range(width // 128):
                    total = total + v[:, k * 128 : (k + 1) * 128]
        mean = jnp.sum(total, axis=-1, keepdims=True) * (1.0 / (2 * ny * width))
        scale = lax.rsqrt(mean + epsilon)
        for half in range(2):
            for s in range(ny):
                source = s * 2 + (where[2] ^ half)
                cols = pl.ds(pl.multiple_of(source * width, 128), width)
                v = hidden[side * 2 + half][s].astype(jnp.float32)
                v = v * scale * norm_gain[:, cols]
                normed[pl.ds(first, rows), cols] = v.astype(jnp.bfloat16)
    copy = pltpu.make_async_copy(normed, out, sem)
    copy.start()
    copy.wait()


def pair_kernel(panel, offsets, where, source, gain, cosine, sine, blocks, out, normed, weights, sem):
    copy = pltpu.make_async_copy(source, normed, sem)
    copy.start()
    collect(offsets, where, blocks, weights, panel)
    copy.wait()
    v = jnp.dot(normed[...], weights[...], preferred_element_type=jnp.float32)
    keys = head_norm_rope(v, gain[...], cosine[...], sine[...])
    out[...] = jnp.where(where[0] == 0, keys, v).astype(jnp.bfloat16)


def query_kernel(panel, offsets, where, source, gain, cosine, sine, blocks, out, normed, weights, sem):
    copy = pltpu.make_async_copy(source, normed, sem)
    copy.start()
    collect(offsets, where, blocks, weights, panel)
    copy.wait()
    rows = out.shape[2]
    for side in range(2):
        span = pl.ds(side * rows, rows)
        v = jnp.dot(normed[span, :], weights[...], preferred_element_type=jnp.float32)
        for h in range(2):
            q = head_norm_rope(
                v[:, h * 128 : (h + 1) * 128], gain[...], cosine[span, :], sine[span, :]
            )
            out[side, h] = q.astype(jnp.bfloat16)


def identity_mask():
    shape = (128, 128)
    return lax.broadcasted_iota(jnp.int32, shape, 0) == lax.broadcasted_iota(jnp.int32, shape, 1)


def attend(query, keys, values, begin, index, low, high, clear, acc, top):
    rows = begin.shape[0]
    scale = math.log2(math.e) / math.sqrt(128)
    acc[...] = jnp.zeros_like(acc)
    top[...] = jnp.full(top.shape, NEG, jnp.float32)

    def block(base, masked):
        key = keys[pl.ds(base, KEY_BLOCK), :]
        value = values[pl.ds(base, KEY_BLOCK), :]
        if masked:
            col = base + lax.broadcasted_iota(jnp.int32, (rows, KEY_BLOCK), 1)
            allowed = col >= begin
            if index is not None:
                allowed = allowed & (col <= index)
        for h in range(query.shape[0] // rows):
            span = pl.ds(h * rows, rows)
            raw = lax.dot_general(
                query[span, :], key, (((1,), (1,)), ((), ())), preferred_element_type=jnp.float32
            )
            if masked:
                raw = jnp.where(allowed, raw, MASKED)
            old = top[span, :]
            new = jnp.maximum(old, jnp.max(raw, axis=-1, keepdims=True))
            terms = jnp.exp2(raw * scale - new * scale)
            decay = jnp.exp2((old - new) * scale)
            top[span, :] = new
            acc[span, :] = acc[span, :] * decay + jnp.dot(
                terms.astype(jnp.bfloat16), value, preferred_element_type=jnp.float32
            )

    def step(b, carry):
        base = pl.multiple_of(b * KEY_BLOCK, KEY_BLOCK)
        plain = base >= clear
        if index is not None:
            plain = plain & (base + KEY_BLOCK <= high - rows)

        @pl.when(plain)
        def _():
            block(base, False)

        @pl.when(jnp.logical_not(plain))
        def _():
            block(base, True)

        return carry

    lax.fori_loop(low // KEY_BLOCK, (high + KEY_BLOCK - 1) // KEY_BLOCK, step, 0)
    summed = acc[:, 128:]
    safe = jnp.where(summed > 0, summed, 1.0)
    one = safe[:, 0:1]
    return acc[:, :128] / safe, jnp.where(one > 0, top[...] * scale + jnp.log2(one), NEG)


def own_kernel(where, begins, query, keys, values, out, log, acc, top):
    rows = begins.shape[1]
    index = where[2] + lax.broadcasted_iota(jnp.int32, (rows, 1), 0)
    limits = [where[3 + i] for i in range(3)]
    result, level = attend(query, keys, values, begins[0], index, *limits, acc, top)
    out[...] = result
    log[...] = level


def remote_kernel(where, begins, near, far, *refs):
    mine, other = refs[:2], refs[2:4]
    out1, out2, keys, values, acc, top = refs[4:]
    block = mine[0].shape[1]
    values[:, 128:] = jnp.ones((values.shape[0], 128), values.dtype)
    for core, (first, second) in enumerate(((mine, other), (other, mine))):

        @pl.when(where[0] == core)
        def _(first=first, second=second):
            for k in range(8):
                spot = pl.ds(pl.multiple_of((where[1] ^ PEER[k]) * block, block), block)
                keys[spot, :] = first[k // 4][k % 4]
                values[spot, :128] = second[k // 4][k % 4]

    eye = identity_mask()
    size = near.shape[0]
    for s, query, out in ((1, near, out1), (2, far, out2)):
        limits = [where[3 + 3 * s + i] for i in range(3)]
        result, log = attend(query, keys, values, begins[s], None, *limits, acc, top)
        out[0:size, :] = result.astype(jnp.bfloat16)
        rest = jnp.concatenate(
            [
                jnp.sum(jnp.where(eye, log[g * 128 : (g + 1) * 128, :], 0.0), axis=0, keepdims=True)
                for g in range(size // 128)
            ]
            + [jnp.zeros((16 - size // 128, 128), jnp.float32)],
            axis=0,
        )
        for part in range(3):
            piece = rest.astype(jnp.bfloat16)
            out[size + 16 * part : size + 16 * (part + 1), :] = piece
            rest = rest - piece.astype(jnp.float32)


def combine_kernel(where, o0, l0, r1, r2, out):
    rows = out.shape[0]
    size = o0.shape[0]
    eye = identity_mask()

    def column(ref):
        level = sum(
            ref[size + 16 * part : size + 16 * (part + 1), :].astype(jnp.float32)
            for part in (2, 1, 0)
        )
        pieces = [
            jnp.sum(jnp.where(eye, level[g : g + 1, :], 0.0), axis=1, keepdims=True)
            for g in range(size // 128)
        ]
        return jnp.concatenate(pieces, axis=0)

    a = l0[...]
    b = jnp.where(where[1] == 1, column(r1), NEG)
    c = jnp.where(where[2] == 1, column(r2), NEG)
    top = jnp.maximum(jnp.maximum(a, b), c)
    a, b, c = jnp.exp2(a - top), jnp.exp2(b - top), jnp.exp2(c - top)
    summed = a * o0[...]
    summed = summed + b * r1[0:size, :].astype(jnp.float32) + c * r2[0:size, :].astype(jnp.float32)
    result = (summed / (a + b + c)).astype(jnp.bfloat16)
    for side in range(2):
        first = 256 * (where[0] if side == 0 else 1 - where[0])
        for h in range(2):
            k = side * 2 + h
            cols = pl.ds(pl.multiple_of(first + h * 128, 128), 128)
            out[:, cols] = result[k * rows : (k + 1) * rows, :]


def across(v, bit):
    return lax.ppermute(v, "z", [(i, i ^ bit) for i in range(8)])


def after(v, *earlier):
    return lax.optimization_barrier((v, *earlier))[0]


def body(hidden, norm_gain, query_gain, key_gain, weight_store, documents, owners):
    x, z, c, w = (lax.axis_index(a) for a in ("x", "z", "c", "w"))
    nx, nz = (lax.axis_size(a) for a in ("x", "z"))
    rows = hidden.shape[0]
    slots = owners.shape[0]
    panel = weight_store.shape[0]
    swap = [(0, 1), (1, 0)]
    bf16, f32 = jnp.bfloat16, jnp.float32
    table = jnp.arange(slots, dtype=jnp.int32)

    riders = jnp.pad(documents.astype(bf16), (0, 256 - rows), constant_values=NO_SEGMENT)
    riders = jnp.pad(riders[None], ((0, 15), (0, weight_store.shape[1] - 256)))
    both = lax.all_gather(jnp.concatenate([weight_store, riders], axis=0), "c", axis=0)
    pair_docs = both[:, panel, :256]
    columns = both[:, :panel].reshape(2 * panel, -1)
    columns = jnp.concatenate(
        [
            lax.dynamic_slice_in_dim(columns, 512 + 128 * c, 128, 1),
            lax.dynamic_slice_in_dim(columns, 256 * c, 256, 1),
        ],
        axis=1,
    )
    tail = jnp.pad(pair_docs.reshape(4, 128), ((0, 12), (0, 256)))
    line = jnp.concatenate([columns, tail], axis=0)
    pair_docs = pair_docs[:, :rows].astype(jnp.int32)

    line = line[None]
    step = across(line, 4)
    far = lax.ppermute(hidden, "w", swap)
    own_near = lax.all_gather(hidden, "y", axis=0)
    step, far, own_near = lax.optimization_barrier((step, far, own_near))

    line = jnp.concatenate([line, step], axis=0)
    step = across(line, 2)
    other_near = lax.ppermute(own_near, "c", swap)
    own_far = lax.all_gather(far, "y", axis=0)
    step, other_near, own_far = lax.optimization_barrier((step, other_near, own_far))

    line = jnp.concatenate([line, step], axis=0)
    step = across(line, 1)
    other_far = lax.ppermute(own_far, "c", swap)
    line = jnp.concatenate([line, step], axis=0)

    def copies(v):
        return jnp.broadcast_to(v[None], (nx, *v.shape))

    pair_blocks = lax.all_to_all(copies(line[:, :, :128]), "x", 0, 0)
    query_line = copies(line[:, : 2 * panel, 128:])
    other_far, query_line = lax.optimization_barrier((other_far, query_line))
    query_blocks = lax.all_to_all(after(query_line, pair_blocks), "x", 0, 0)

    spot = jnp.stack([c, z, w]).astype(jnp.int32)
    features = norm_gain.shape[0]
    (normed,) = call(
        norm_kernel,
        [jax.ShapeDtypeStruct((2 * rows, features), bf16)],
        1,
        5,
        [pltpu.VMEM((2 * rows, features), bf16), pltpu.SemaphoreType.DMA],
        4 * 10**9,
        out_hbm=True,
    )(spot, norm_gain.astype(f32)[None, :], own_near, own_far, other_near, other_far)

    riding = pair_blocks[:, :, 2 * panel : 2 * panel + 4, :].astype(f32)
    starts = jnp.sum(
        (riding.reshape(-1, 1) < table.astype(f32)[None, :]).astype(f32), axis=0
    ).astype(jnp.int32)

    def begin_of(docs):
        return jnp.sum(
            (docs[:, None] == table[None, :]).astype(jnp.int32) * starts[None, :], axis=1
        )

    pair_begin = begin_of(pair_docs.reshape(-1))
    plane = nz * 2 * rows
    token = x * plane + z * 2 * rows + jnp.arange(2 * rows, dtype=jnp.int32)
    positions = token - pair_begin
    exponent = jnp.arange(64, dtype=f32) * (2.0 / 128)
    frequency = jnp.exp(exponent * -math.log(rope_base))
    angles = positions.astype(f32)[:, None] * frequency[None, :]
    cosine, sine = jnp.cos(angles), jnp.sin(angles)
    cosine = jnp.concatenate([cosine, cosine], axis=1)
    sine = jnp.concatenate([-sine, sine], axis=1)
    spread = [lax.dynamic_slice_in_dim(pair_begin, c * rows, rows, 0)]
    for s in (1, 2):
        place = (jnp.minimum(x + s, nx - 1), 0, 2 * c, 0)
        docs = lax.dynamic_slice(riding, place, (1, 1, 2, 128)).reshape(-1)[:rows]
        spread.append(begin_of(docs.astype(jnp.int32)))
    spread = jnp.stack(spread) - x * plane

    offsets = panel * jnp.sum(
        table[:, None] * (owners[:, None] == table[None, :]).astype(jnp.int32), axis=0
    )
    (pair,) = call(
        functools.partial(pair_kernel, panel),
        [jax.ShapeDtypeStruct((2 * rows, 128), bf16)],
        2,
        4,
        [
            pltpu.VMEM((2 * rows, features), bf16),
            pltpu.VMEM((features, 128), bf16),
            pltpu.SemaphoreType.DMA,
        ],
        2 * 10**9,
        n_hbm=1,
    )(offsets, spot, normed, key_gain[None, :], cosine, sine, pair_blocks)

    inside = z * 2 * rows + c * rows
    low = [jnp.clip(spread[s, 0], 0, plane) for s in range(3)]
    high = [inside + rows] + [jnp.where(x + s < nx, plane, 0) for s in (1, 2)]
    limits = [v for s in range(3) for v in (low[s], high[s], spread[s, rows - 1])]
    ranges = jnp.stack([c, z, inside] + limits).astype(jnp.int32)
    begins = spread[:, :, None]

    mine0 = jnp.stack([pair, across(pair, 4)])
    mine0, ranges, begins = lax.optimization_barrier((mine0, ranges, begins))
    mine0 = jnp.concatenate([mine0, across(mine0, 2)], axis=0)
    mine0, query_blocks = lax.optimization_barrier((mine0, query_blocks))
    mine1 = across(mine0, 1)
    mine = [mine0, mine1]
    other = [lax.ppermute(v, "c", swap) for v in mine]

    (query,) = call(
        functools.partial(query_kernel, panel),
        [jax.ShapeDtypeStruct((2, 2, rows, 128), bf16)],
        2,
        4,
        [
            pltpu.VMEM((2 * rows, features), bf16),
            pltpu.VMEM((features, 256), bf16),
            pltpu.SemaphoreType.DMA,
        ],
        4 * 10**9,
        n_hbm=1,
    )(offsets, spot, normed, query_gain[None, :], cosine, sine, query_blocks)

    own_query = lax.dynamic_index_in_dim(query, c, 0, keepdims=False)
    sent_query = lax.dynamic_index_in_dim(query, 1 - c, 0, keepdims=False)
    q0 = jnp.concatenate([own_query, lax.ppermute(sent_query, "c", swap)], axis=0)
    q0 = q0.reshape(4 * rows, 128)
    q1 = lax.ppermute(q0, "x", [(i, i - 1) for i in range(1, nx)])
    q2 = lax.ppermute(q0, "x", [(i, i - 2) for i in range(2, nx)])

    state = [pltpu.VMEM((4 * rows, 256), f32), pltpu.VMEM((4 * rows, 1), f32)]
    r1, r2, keys, values = call(
        remote_kernel,
        [jax.ShapeDtypeStruct((4 * rows + 48, 128), bf16)] * 2
        + [jax.ShapeDtypeStruct((plane, 128 * k), bf16) for k in (1, 2)],
        1,
        7,
        state,
        10**10,
    )(ranges, begins, q1, q2, *mine, *other)
    r1 = lax.ppermute(r1, "x", [(i, i + 1) for i in range(nx - 1)])
    r2 = lax.ppermute(r2, "x", [(i, i + 2) for i in range(nx - 2)])
    o0, l0 = call(
        own_kernel,
        [
            jax.ShapeDtypeStruct((4 * rows, 128), f32),
            jax.ShapeDtypeStruct((4 * rows, 1), f32),
        ],
        1,
        4,
        state,
        10**10,
    )(ranges, begins, q0, keys, values)
    came = jnp.stack([c, (x >= 1).astype(jnp.int32), (x >= 2).astype(jnp.int32)]).astype(jnp.int32)
    (context,) = call(combine_kernel, [jax.ShapeDtypeStruct((rows, 512), bf16)], 1, 4)(
        came, o0, l0, r1, r2
    )

    own_part = lax.dynamic_slice_in_dim(pair, c * rows, rows, 0)
    other_part = lax.dynamic_slice_in_dim(other[0][0], c * rows, rows, 0)
    keys_fresh = jnp.where(c == 0, own_part, other_part)
    values_fresh = jnp.where(c == 0, other_part, own_part)
    return keys_fresh, values_fresh, context


def solution(mesh):
    fine = Mesh(mesh.devices.reshape(4, 8, 2, 4, 2), ("x", "z", "c", "y", "w"))
    ctx, head = ("x", "z", "c"), ("y", "w")
    in_specs = (P(ctx, head), P(), P(), P(), P(ctx, head), P(ctx), P())
    out_specs = (P(ctx, head), P(ctx, head), P(ctx, head))
    return jax.shard_map(body, mesh=fine, in_specs=in_specs, out_specs=out_specs, check_vma=False)
```

```python
import functools
import math

import jax
import jax.numpy as jnp
from jax import lax
from jax.experimental import pallas as pl
from jax.experimental.pallas import tpu as pltpu
from jax.sharding import Mesh
from jax.sharding import PartitionSpec as P

epsilon = 1e-06
rope_base = 1000000.0
NEG = -1e30
MASKED = -3e38
KEY_BLOCK = 1024
NO_SEGMENT = 100.0
VMEM_LIMIT = 14 * 1024 * 1024


def call(kernel, out_shape, n_smem, n_vmem, scratch=(), flops=0, n_hbm=0, out_hbm=False):
    specs = [pl.BlockSpec(memory_space=pltpu.SMEM)] * n_smem
    specs += [pl.BlockSpec(memory_space=pltpu.HBM)] * n_hbm
    specs += [pl.BlockSpec(memory_space=pltpu.VMEM)] * n_vmem
    out = pl.BlockSpec(memory_space=pltpu.HBM if out_hbm else pltpu.VMEM)
    return pl.pallas_call(
        kernel,
        out_shape=out_shape,
        in_specs=specs,
        out_specs=[out] * len(out_shape),
        scratch_shapes=list(scratch),
        compiler_params=pltpu.CompilerParams(vmem_limit_bytes=VMEM_LIMIT),
        cost_estimate=pl.CostEstimate(flops=flops, bytes_accessed=4 << 20, transcendentals=0),
    )


PEER = (0, 4, 2, 6, 1, 5, 3, 7)


def head_norm_rope(v, gain, cosine, sine):
    mean = jnp.mean(v * v, axis=-1, keepdims=True)
    v = v * lax.rsqrt(mean + epsilon) * gain
    return v * cosine + pltpu.roll(v, 64, 1) * sine


def collect(offsets, where, parts, weights, panel):
    peers = iter(PEER)
    for blocks in parts:
        for k in range(blocks.shape[1]):
            peer = next(peers)
            for s in range(blocks.shape[0]):
                for c in range(2):
                    slot = s * (2 * len(PEER)) + (where[1] ^ peer) * 2 + c
                    first = pl.multiple_of(offsets[slot], 16)
                    weights[pl.ds(first, panel), :] = blocks[s, k, c * panel : (c + 1) * panel, :]


def norm_kernel(where, norm_gain, *refs):
    hidden, out, normed, sem = refs[:-3], refs[-3], refs[-2], refs[-1]
    ny, rows, width = hidden[0].shape
    for side in range(2):
        first = pl.multiple_of(rows * (where[0] if side == 0 else 1 - where[0]), rows)
        total = jnp.zeros((rows, 128), jnp.float32)
        for half in range(2):
            for s in range(ny):
                v = hidden[side * 2 + half][s].astype(jnp.float32)
                v = v * v
                for k in range(width // 128):
                    total = total + v[:, k * 128 : (k + 1) * 128]
        mean = jnp.sum(total, axis=-1, keepdims=True) * (1.0 / (2 * ny * width))
        scale = lax.rsqrt(mean + epsilon)
        for half in range(2):
            for s in range(ny):
                source = s * 2 + (where[2] ^ half)
                cols = pl.ds(pl.multiple_of(source * width, 128), width)
                v = hidden[side * 2 + half][s].astype(jnp.float32)
                v = v * scale * norm_gain[:, cols]
                normed[pl.ds(first, rows), cols] = v.astype(jnp.bfloat16)
    copy = pltpu.make_async_copy(normed, out, sem)
    copy.start()
    copy.wait()


def pair_kernel(panel, offsets, where, source, gain, cosine, sine, near, far, out, normed, weights, sem):
    copy = pltpu.make_async_copy(source, normed, sem)
    copy.start()
    collect(offsets, where, (near, far), weights, panel)
    copy.wait()
    v = jnp.dot(normed[...], weights[...], preferred_element_type=jnp.float32)
    keys = head_norm_rope(v, gain[...], cosine[...], sine[...])
    out[...] = jnp.where(where[0] == 0, keys, v).astype(jnp.bfloat16)


def query_kernel(panel, offsets, where, source, gain, cosine, sine, blocks, out, normed, weights, sem):
    copy = pltpu.make_async_copy(source, normed, sem)
    copy.start()
    collect(offsets, where, (blocks,), weights, panel)
    copy.wait()
    rows = out.shape[2]
    for side in range(2):
        span = pl.ds(side * rows, rows)
        v = jnp.dot(normed[span, :], weights[...], preferred_element_type=jnp.float32)
        for h in range(2):
            q = head_norm_rope(
                v[:, h * 128 : (h + 1) * 128], gain[...], cosine[span, :], sine[span, :]
            )
            out[side, h] = q.astype(jnp.bfloat16)


def identity_mask():
    shape = (128, 128)
    return lax.broadcasted_iota(jnp.int32, shape, 0) == lax.broadcasted_iota(jnp.int32, shape, 1)


def attend(query, keys, values, begin, index, low, high, clear, acc, top):
    rows = begin.shape[0]
    scale = math.log2(math.e) / math.sqrt(128)
    acc[...] = jnp.zeros_like(acc)
    top[...] = jnp.full(top.shape, NEG, jnp.float32)

    def block(base, masked):
        key = keys[pl.ds(base, KEY_BLOCK), :]
        value = values[pl.ds(base, KEY_BLOCK), :]
        if masked:
            col = base + lax.broadcasted_iota(jnp.int32, (rows, KEY_BLOCK), 1)
            allowed = col >= begin
            if index is not None:
                allowed = allowed & (col <= index)
        for h in range(query.shape[0] // rows):
            span = pl.ds(h * rows, rows)
            raw = lax.dot_general(
                query[span, :], key, (((1,), (1,)), ((), ())), preferred_element_type=jnp.float32
            )
            if masked:
                raw = jnp.where(allowed, raw, MASKED)
            old = top[span, :]
            new = jnp.maximum(old, jnp.max(raw, axis=-1, keepdims=True))
            terms = jnp.exp2(raw * scale - new * scale)
            decay = jnp.exp2((old - new) * scale)
            top[span, :] = new
            acc[span, :] = acc[span, :] * decay + jnp.dot(
                terms.astype(jnp.bfloat16), value, preferred_element_type=jnp.float32
            )

    def step(b, carry):
        base = pl.multiple_of(b * KEY_BLOCK, KEY_BLOCK)
        plain = base >= clear
        if index is not None:
            plain = plain & (base + KEY_BLOCK <= high - rows)

        @pl.when(plain)
        def _():
            block(base, False)

        @pl.when(jnp.logical_not(plain))
        def _():
            block(base, True)

        return carry

    lax.fori_loop(low // KEY_BLOCK, (high + KEY_BLOCK - 1) // KEY_BLOCK, step, 0)
    summed = acc[:, 128:]
    safe = jnp.where(summed > 0, summed, 1.0)
    one = safe[:, 0:1]
    return acc[:, :128] / safe, jnp.where(one > 0, top[...] * scale + jnp.log2(one), NEG)


def own_kernel(where, begins, query, keys, values, out, log, acc, top):
    rows = begins.shape[1]
    index = where[2] + lax.broadcasted_iota(jnp.int32, (rows, 1), 0)
    limits = [where[3 + i] for i in range(3)]
    result, level = attend(query, keys, values, begins[0], index, *limits, acc, top)
    out[...] = result
    log[...] = level


def remote_kernel(where, begins, near, far, *refs):
    mine, other = refs[:2], refs[2:4]
    out1, out2, keys, values, acc, top = refs[4:]
    block = mine[0].shape[1]
    values[:, 128:] = jnp.ones((values.shape[0], 128), values.dtype)
    for core, (first, second) in enumerate(((mine, other), (other, mine))):

        @pl.when(where[0] == core)
        def _(first=first, second=second):
            for k in range(8):
                spot = pl.ds(pl.multiple_of((where[1] ^ PEER[k]) * block, block), block)
                keys[spot, :] = first[k // 4][k % 4]
                values[spot, :128] = second[k // 4][k % 4]

    eye = identity_mask()
    size = near.shape[0]
    for s, query, out in ((1, near, out1), (2, far, out2)):
        limits = [where[3 + 3 * s + i] for i in range(3)]
        result, log = attend(query, keys, values, begins[s], None, *limits, acc, top)
        out[0:size, :] = result.astype(jnp.bfloat16)
        rest = jnp.concatenate(
            [
                jnp.sum(jnp.where(eye, log[g * 128 : (g + 1) * 128, :], 0.0), axis=0, keepdims=True)
                for g in range(size // 128)
            ]
            + [jnp.zeros((16 - size // 128, 128), jnp.float32)],
            axis=0,
        )
        for part in range(3):
            piece = rest.astype(jnp.bfloat16)
            out[size + 16 * part : size + 16 * (part + 1), :] = piece
            rest = rest - piece.astype(jnp.float32)


def combine_kernel(where, o0, l0, r1, r2, out):
    rows = out.shape[0]
    size = o0.shape[0]
    eye = identity_mask()

    def column(ref):
        level = sum(
            ref[size + 16 * part : size + 16 * (part + 1), :].astype(jnp.float32)
            for part in (2, 1, 0)
        )
        pieces = [
            jnp.sum(jnp.where(eye, level[g : g + 1, :], 0.0), axis=1, keepdims=True)
            for g in range(size // 128)
        ]
        return jnp.concatenate(pieces, axis=0)

    a = l0[...]
    b = jnp.where(where[1] == 1, column(r1), NEG)
    c = jnp.where(where[2] == 1, column(r2), NEG)
    top = jnp.maximum(jnp.maximum(a, b), c)
    a, b, c = jnp.exp2(a - top), jnp.exp2(b - top), jnp.exp2(c - top)
    summed = a * o0[...]
    summed = summed + b * r1[0:size, :].astype(jnp.float32) + c * r2[0:size, :].astype(jnp.float32)
    result = (summed / (a + b + c)).astype(jnp.bfloat16)
    for side in range(2):
        first = 256 * (where[0] if side == 0 else 1 - where[0])
        for h in range(2):
            k = side * 2 + h
            cols = pl.ds(pl.multiple_of(first + h * 128, 128), 128)
            out[:, cols] = result[k * rows : (k + 1) * rows, :]


def across(v, bit):
    return lax.ppermute(v, "z", [(i, i ^ bit) for i in range(8)])


def after(v, *earlier):
    return lax.optimization_barrier((v, *earlier))[0]


def body(hidden, norm_gain, query_gain, key_gain, weight_store, documents, owners):
    x, z, c, w = (lax.axis_index(a) for a in ("x", "z", "c", "w"))
    nx, nz = (lax.axis_size(a) for a in ("x", "z"))
    rows = hidden.shape[0]
    slots = owners.shape[0]
    panel = weight_store.shape[0]
    swap = [(0, 1), (1, 0)]
    bf16, f32 = jnp.bfloat16, jnp.float32
    table = jnp.arange(slots, dtype=jnp.int32)

    riders = jnp.pad(documents.astype(bf16), (0, 256 - rows), constant_values=NO_SEGMENT)
    riders = jnp.pad(riders[None], ((0, 15), (0, weight_store.shape[1] - 256)))
    both = lax.all_gather(jnp.concatenate([weight_store, riders], axis=0), "c", axis=0)
    pair_docs = both[:, panel, :256]
    columns = both[:, :panel].reshape(2 * panel, -1)
    columns = jnp.concatenate(
        [
            lax.dynamic_slice_in_dim(columns, 512 + 128 * c, 128, 1),
            lax.dynamic_slice_in_dim(columns, 256 * c, 256, 1),
        ],
        axis=1,
    )
    tail = jnp.pad(pair_docs.reshape(4, 128), ((0, 12), (0, 256)))
    line = jnp.concatenate([columns, tail], axis=0)
    pair_docs = pair_docs[:, :rows].astype(jnp.int32)

    line = line[None]
    step = across(line, 4)
    far = lax.ppermute(hidden, "w", swap)
    own_near = lax.all_gather(hidden, "y", axis=0)
    step, far, own_near = lax.optimization_barrier((step, far, own_near))

    line = jnp.concatenate([line, step], axis=0)
    step = across(line, 2)
    other_near = lax.ppermute(own_near, "c", swap)
    own_far = lax.all_gather(far, "y", axis=0)
    step, other_near, own_far = lax.optimization_barrier((step, other_near, own_far))

    def copies(v):
        return jnp.broadcast_to(v[None], (nx, *v.shape))

    line = jnp.concatenate([line, step], axis=0)
    step = across(line, 1)
    other_far = lax.ppermute(own_far, "c", swap)
    pair_near = lax.all_to_all(copies(line[:, :, :128]), "x", 0, 0)
    step, pair_near = lax.optimization_barrier((step, pair_near))

    pair_far = lax.all_to_all(copies(step[:, :, :128]), "x", 0, 0)
    line = jnp.concatenate([line, step], axis=0)
    query_line = copies(line[:, : 2 * panel, 128:])
    other_far, query_line = lax.optimization_barrier((other_far, query_line))
    query_blocks = lax.all_to_all(after(query_line, pair_far), "x", 0, 0)

    spot = jnp.stack([c, z, w]).astype(jnp.int32)
    features = norm_gain.shape[0]
    (normed,) = call(
        norm_kernel,
        [jax.ShapeDtypeStruct((2 * rows, features), bf16)],
        1,
        5,
        [pltpu.VMEM((2 * rows, features), bf16), pltpu.SemaphoreType.DMA],
        4 * 10**9,
        out_hbm=True,
    )(spot, norm_gain.astype(f32)[None, :], own_near, own_far, other_near, other_far)

    riding = [v[:, :, 2 * panel : 2 * panel + 4, :] for v in (pair_near, pair_far)]
    riding = jnp.concatenate(riding, axis=1).astype(f32)
    starts = jnp.sum(
        (riding.reshape(-1, 1) < table.astype(f32)[None, :]).astype(f32), axis=0
    ).astype(jnp.int32)

    def begin_of(docs):
        return jnp.sum(
            (docs[:, None] == table[None, :]).astype(jnp.int32) * starts[None, :], axis=1
        )

    pair_begin = begin_of(pair_docs.reshape(-1))
    plane = nz * 2 * rows
    token = x * plane + z * 2 * rows + jnp.arange(2 * rows, dtype=jnp.int32)
    positions = token - pair_begin
    exponent = jnp.arange(64, dtype=f32) * (2.0 / 128)
    frequency = jnp.exp(exponent * -math.log(rope_base))
    angles = positions.astype(f32)[:, None] * frequency[None, :]
    cosine, sine = jnp.cos(angles), jnp.sin(angles)
    cosine = jnp.concatenate([cosine, cosine], axis=1)
    sine = jnp.concatenate([-sine, sine], axis=1)
    spread = [lax.dynamic_slice_in_dim(pair_begin, c * rows, rows, 0)]
    for s in (1, 2):
        place = (jnp.minimum(x + s, nx - 1), 0, 2 * c, 0)
        docs = lax.dynamic_slice(riding, place, (1, 1, 2, 128)).reshape(-1)[:rows]
        spread.append(begin_of(docs.astype(jnp.int32)))
    spread = jnp.stack(spread) - x * plane

    offsets = panel * jnp.sum(
        table[:, None] * (owners[:, None] == table[None, :]).astype(jnp.int32), axis=0
    )
    (pair,) = call(
        functools.partial(pair_kernel, panel),
        [jax.ShapeDtypeStruct((2 * rows, 128), bf16)],
        2,
        5,
        [
            pltpu.VMEM((2 * rows, features), bf16),
            pltpu.VMEM((features, 128), bf16),
            pltpu.SemaphoreType.DMA,
        ],
        2 * 10**9,
        n_hbm=1,
    )(offsets, spot, normed, key_gain[None, :], cosine, sine, pair_near, pair_far)

    inside = z * 2 * rows + c * rows
    low = [jnp.clip(spread[s, 0], 0, plane) for s in range(3)]
    high = [inside + rows] + [jnp.where(x + s < nx, plane, 0) for s in (1, 2)]
    limits = [v for s in range(3) for v in (low[s], high[s], spread[s, rows - 1])]
    ranges = jnp.stack([c, z, inside] + limits).astype(jnp.int32)
    begins = spread[:, :, None]

    mine0 = jnp.stack([pair, across(pair, 4)])
    mine0, ranges, begins = lax.optimization_barrier((mine0, ranges, begins))
    mine0 = jnp.concatenate([mine0, across(mine0, 2)], axis=0)
    (query,) = call(
        functools.partial(query_kernel, panel),
        [jax.ShapeDtypeStruct((2, 2, rows, 128), bf16)],
        2,
        4,
        [
            pltpu.VMEM((2 * rows, features), bf16),
            pltpu.VMEM((features, 256), bf16),
            pltpu.SemaphoreType.DMA,
        ],
        4 * 10**9,
        n_hbm=1,
    )(offsets, spot, normed, query_gain[None, :], cosine, sine, query_blocks)

    mine0, query = lax.optimization_barrier((mine0, query))
    mine1 = across(mine0, 1)
    mine = [mine0, mine1]
    other = [lax.ppermute(v, "c", swap) for v in mine]
    own_query = lax.dynamic_index_in_dim(query, c, 0, keepdims=False)
    sent_query = lax.dynamic_index_in_dim(query, 1 - c, 0, keepdims=False)
    q0 = jnp.concatenate([own_query, lax.ppermute(sent_query, "c", swap)], axis=0)
    q0 = q0.reshape(4 * rows, 128)
    q1 = lax.ppermute(q0, "x", [(i, i - 1) for i in range(1, nx)])
    q2 = lax.ppermute(q0, "x", [(i, i - 2) for i in range(2, nx)])

    state = [pltpu.VMEM((4 * rows, 256), f32), pltpu.VMEM((4 * rows, 1), f32)]
    r1, r2, keys, values = call(
        remote_kernel,
        [jax.ShapeDtypeStruct((4 * rows + 48, 128), bf16)] * 2
        + [jax.ShapeDtypeStruct((plane, 128 * k), bf16) for k in (1, 2)],
        1,
        7,
        state,
        10**10,
    )(ranges, begins, q1, q2, *mine, *other)
    r1 = lax.ppermute(r1, "x", [(i, i + 1) for i in range(nx - 1)])
    r2 = lax.ppermute(r2, "x", [(i, i + 2) for i in range(nx - 2)])
    o0, l0 = call(
        own_kernel,
        [
            jax.ShapeDtypeStruct((4 * rows, 128), f32),
            jax.ShapeDtypeStruct((4 * rows, 1), f32),
        ],
        1,
        4,
        state,
        10**10,
    )(ranges, begins, q0, keys, values)
    came = jnp.stack([c, (x >= 1).astype(jnp.int32), (x >= 2).astype(jnp.int32)]).astype(jnp.int32)
    (context,) = call(combine_kernel, [jax.ShapeDtypeStruct((rows, 512), bf16)], 1, 4)(
        came, o0, l0, r1, r2
    )

    own_part = lax.dynamic_slice_in_dim(pair, c * rows, rows, 0)
    other_part = lax.dynamic_slice_in_dim(other[0][0], c * rows, rows, 0)
    keys_fresh = jnp.where(c == 0, own_part, other_part)
    values_fresh = jnp.where(c == 0, other_part, own_part)
    return keys_fresh, values_fresh, context


def solution(mesh):
    fine = Mesh(mesh.devices.reshape(4, 8, 2, 4, 2), ("x", "z", "c", "y", "w"))
    ctx, head = ("x", "z", "c"), ("y", "w")
    in_specs = (P(ctx, head), P(), P(), P(), P(ctx, head), P(ctx), P())
    out_specs = (P(ctx, head), P(ctx, head), P(ctx, head))
    return jax.shard_map(body, mesh=fine, in_specs=in_specs, out_specs=out_specs, check_vma=False)
```

```python
import functools
import math

import jax
import jax.numpy as jnp
from jax import lax
from jax.experimental import pallas as pl
from jax.experimental.pallas import tpu as pltpu
from jax.sharding import Mesh
from jax.sharding import PartitionSpec as P

epsilon = 1e-06
rope_base = 1000000.0
NEG = -1e30
MASKED = -3e38
KEY_BLOCK = 1024
NO_SEGMENT = 100.0
VMEM_LIMIT = 14 * 1024 * 1024


def call(kernel, out_shape, n_smem, n_vmem, scratch=(), flops=0, n_hbm=0, out_hbm=False):
    specs = [pl.BlockSpec(memory_space=pltpu.SMEM)] * n_smem
    specs += [pl.BlockSpec(memory_space=pltpu.HBM)] * n_hbm
    specs += [pl.BlockSpec(memory_space=pltpu.VMEM)] * n_vmem
    out = pl.BlockSpec(memory_space=pltpu.HBM if out_hbm else pltpu.VMEM)
    return pl.pallas_call(
        kernel,
        out_shape=out_shape,
        in_specs=specs,
        out_specs=[out] * len(out_shape),
        scratch_shapes=list(scratch),
        compiler_params=pltpu.CompilerParams(vmem_limit_bytes=VMEM_LIMIT),
        cost_estimate=pl.CostEstimate(flops=flops, bytes_accessed=4 << 20, transcendentals=0),
    )


PEER = (0, 4, 2, 6, 1, 5, 3, 7)


def head_norm_rope(v, gain, cosine, sine):
    mean = jnp.mean(v * v, axis=-1, keepdims=True)
    v = v * lax.rsqrt(mean + epsilon) * gain
    return v * cosine + pltpu.roll(v, 64, 1) * sine


def collect(offsets, where, blocks, weights, panel):
    nx, nz = blocks.shape[:2]
    for s in range(nx):
        for k, peer in enumerate(PEER):
            for c in range(2):
                slot = s * (2 * nz) + (where[1] ^ peer) * 2 + c
                first = pl.multiple_of(offsets[slot], 16)
                weights[pl.ds(first, panel), :] = blocks[s, k, c * panel : (c + 1) * panel, :]


def norm_kernel(where, norm_gain, *refs):
    hidden, out, normed, sem = refs[:-3], refs[-3], refs[-2], refs[-1]
    ny, rows, width = hidden[0].shape
    for side in range(2):
        first = pl.multiple_of(rows * (where[0] if side == 0 else 1 - where[0]), rows)
        total = jnp.zeros((rows, 128), jnp.float32)
        for half in range(2):
            for s in range(ny):
                v = hidden[side * 2 + half][s].astype(jnp.float32)
                v = v * v
                for k in range(width // 128):
                    total = total + v[:, k * 128 : (k + 1) * 128]
        mean = jnp.sum(total, axis=-1, keepdims=True) * (1.0 / (2 * ny * width))
        scale = lax.rsqrt(mean + epsilon)
        for half in range(2):
            for s in range(ny):
                source = s * 2 + (where[2] ^ half)
                cols = pl.ds(pl.multiple_of(source * width, 128), width)
                v = hidden[side * 2 + half][s].astype(jnp.float32)
                v = v * scale * norm_gain[:, cols]
                normed[pl.ds(first, rows), cols] = v.astype(jnp.bfloat16)
    copy = pltpu.make_async_copy(normed, out, sem)
    copy.start()
    copy.wait()


def pair_kernel(panel, offsets, where, source, gain, cosine, sine, blocks, out, normed, weights, sem):
    copy = pltpu.make_async_copy(source, normed, sem)
    copy.start()
    collect(offsets, where, blocks, weights, panel)
    copy.wait()
    v = jnp.dot(normed[...], weights[...], preferred_element_type=jnp.float32)
    keys = head_norm_rope(v, gain[...], cosine[...], sine[...])
    out[...] = jnp.where(where[0] == 0, keys, v).astype(jnp.bfloat16)


def query_kernel(panel, offsets, where, source, gain, cosine, sine, blocks, out, normed, weights, sem):
    copy = pltpu.make_async_copy(source, normed, sem)
    copy.start()
    collect(offsets, where, blocks, weights, panel)
    copy.wait()
    rows = out.shape[2]
    for side in range(2):
        span = pl.ds(side * rows, rows)
        v = jnp.dot(normed[span, :], weights[...], preferred_element_type=jnp.float32)
        for h in range(2):
            q = head_norm_rope(
                v[:, h * 128 : (h + 1) * 128], gain[...], cosine[span, :], sine[span, :]
            )
            out[side, h] = q.astype(jnp.bfloat16)


def identity_mask():
    shape = (128, 128)
    return lax.broadcasted_iota(jnp.int32, shape, 0) == lax.broadcasted_iota(jnp.int32, shape, 1)


def attend(query, keys, values, begin, index, low, high, clear, acc, top):
    rows = begin.shape[0]
    scale = math.log2(math.e) / math.sqrt(128)
    acc[...] = jnp.zeros_like(acc)
    top[...] = jnp.full(top.shape, NEG, jnp.float32)

    def block(base, masked):
        key = keys[pl.ds(base, KEY_BLOCK), :]
        value = values[pl.ds(base, KEY_BLOCK), :]
        if masked:
            col = base + lax.broadcasted_iota(jnp.int32, (rows, KEY_BLOCK), 1)
            allowed = col >= begin
            if index is not None:
                allowed = allowed & (col <= index)
        for h in range(query.shape[0] // rows):
            span = pl.ds(h * rows, rows)
            raw = lax.dot_general(
                query[span, :], key, (((1,), (1,)), ((), ())), preferred_element_type=jnp.float32
            )
            if masked:
                raw = jnp.where(allowed, raw, MASKED)
            old = top[span, :]
            new = jnp.maximum(old, jnp.max(raw, axis=-1, keepdims=True))
            terms = jnp.exp2(raw * scale - new * scale)
            decay = jnp.exp2((old - new) * scale)
            top[span, :] = new
            acc[span, :] = acc[span, :] * decay + jnp.dot(
                terms.astype(jnp.bfloat16), value, preferred_element_type=jnp.float32
            )

    def step(b, carry):
        base = pl.multiple_of(b * KEY_BLOCK, KEY_BLOCK)
        plain = base >= clear
        if index is not None:
            plain = plain & (base + KEY_BLOCK <= high - rows)

        @pl.when(plain)
        def _():
            block(base, False)

        @pl.when(jnp.logical_not(plain))
        def _():
            block(base, True)

        return carry

    lax.fori_loop(low // KEY_BLOCK, (high + KEY_BLOCK - 1) // KEY_BLOCK, step, 0)
    summed = acc[:, 128:]
    safe = jnp.where(summed > 0, summed, 1.0)
    one = safe[:, 0:1]
    return acc[:, :128] / safe, jnp.where(one > 0, top[...] * scale + jnp.log2(one), NEG)


def own_kernel(where, begins, query, keys, values, out, log, acc, top):
    rows = begins.shape[1]
    index = where[2] + lax.broadcasted_iota(jnp.int32, (rows, 1), 0)
    limits = [where[3 + i] for i in range(3)]
    result, level = attend(query, keys, values, begins[0], index, *limits, acc, top)
    out[...] = result
    log[...] = level


def remote_kernel(where, begins, near, far, *refs):
    mine, other = refs[:2], refs[2:4]
    out1, out2, keys, values, acc, top = refs[4:]
    block = mine[0].shape[1]
    values[:, 128:] = jnp.ones((values.shape[0], 128), values.dtype)
    for core, (first, second) in enumerate(((mine, other), (other, mine))):

        @pl.when(where[0] == core)
        def _(first=first, second=second):
            for k in range(8):
                spot = pl.ds(pl.multiple_of((where[1] ^ PEER[k]) * block, block), block)
                keys[spot, :] = first[k // 4][k % 4]
                values[spot, :128] = second[k // 4][k % 4]

    eye = identity_mask()
    size = near.shape[0]
    for s, query, out in ((1, near, out1), (2, far, out2)):
        limits = [where[3 + 3 * s + i] for i in range(3)]
        result, log = attend(query, keys, values, begins[s], None, *limits, acc, top)
        out[0:size, :] = result.astype(jnp.bfloat16)
        rest = jnp.concatenate(
            [
                jnp.sum(jnp.where(eye, log[g * 128 : (g + 1) * 128, :], 0.0), axis=0, keepdims=True)
                for g in range(size // 128)
            ]
            + [jnp.zeros((16 - size // 128, 128), jnp.float32)],
            axis=0,
        )
        for part in range(3):
            piece = rest.astype(jnp.bfloat16)
            out[size + 16 * part : size + 16 * (part + 1), :] = piece
            rest = rest - piece.astype(jnp.float32)


def combine_kernel(where, o0, l0, r1, r2, out):
    rows = out.shape[0]
    size = o0.shape[0]
    eye = identity_mask()

    def column(ref):
        level = sum(
            ref[size + 16 * part : size + 16 * (part + 1), :].astype(jnp.float32)
            for part in (2, 1, 0)
        )
        pieces = [
            jnp.sum(jnp.where(eye, level[g : g + 1, :], 0.0), axis=1, keepdims=True)
            for g in range(size // 128)
        ]
        return jnp.concatenate(pieces, axis=0)

    a = l0[...]
    b = jnp.where(where[1] == 1, column(r1), NEG)
    c = jnp.where(where[2] == 1, column(r2), NEG)
    top = jnp.maximum(jnp.maximum(a, b), c)
    a, b, c = jnp.exp2(a - top), jnp.exp2(b - top), jnp.exp2(c - top)
    summed = a * o0[...]
    summed = summed + b * r1[0:size, :].astype(jnp.float32) + c * r2[0:size, :].astype(jnp.float32)
    result = (summed / (a + b + c)).astype(jnp.bfloat16)
    for side in range(2):
        first = 256 * (where[0] if side == 0 else 1 - where[0])
        for h in range(2):
            k = side * 2 + h
            cols = pl.ds(pl.multiple_of(first + h * 128, 128), 128)
            out[:, cols] = result[k * rows : (k + 1) * rows, :]


def across(v, bit):
    return lax.ppermute(v, "z", [(i, i ^ bit) for i in range(8)])


def after(v, *earlier):
    return lax.optimization_barrier((v, *earlier))[0]


def body(hidden, norm_gain, query_gain, key_gain, weight_store, documents, owners):
    x, z, c, w = (lax.axis_index(a) for a in ("x", "z", "c", "w"))
    nx, nz = (lax.axis_size(a) for a in ("x", "z"))
    rows = hidden.shape[0]
    slots = owners.shape[0]
    panel = weight_store.shape[0]
    swap = [(0, 1), (1, 0)]
    bf16, f32 = jnp.bfloat16, jnp.float32
    table = jnp.arange(slots, dtype=jnp.int32)

    riders = jnp.pad(documents.astype(bf16), (0, 256 - rows), constant_values=NO_SEGMENT)
    riders = jnp.pad(riders[None], ((0, 15), (0, weight_store.shape[1] - 256)))
    both = lax.all_gather(jnp.concatenate([weight_store, riders], axis=0), "c", axis=0)
    pair_docs = both[:, panel, :256]
    columns = both[:, :panel].reshape(2 * panel, -1)
    columns = jnp.concatenate(
        [
            lax.dynamic_slice_in_dim(columns, 512 + 128 * c, 128, 1),
            lax.dynamic_slice_in_dim(columns, 256 * c, 256, 1),
        ],
        axis=1,
    )
    tail = jnp.pad(pair_docs.reshape(4, 128), ((0, 12), (0, 256)))
    line = jnp.concatenate([columns, tail], axis=0)
    pair_docs = pair_docs[:, :rows].astype(jnp.int32)

    line = line[None]
    step = across(line, 4)
    far = lax.ppermute(hidden, "w", swap)
    own_near = lax.all_gather(hidden, "y", axis=0)
    step, far, own_near = lax.optimization_barrier((step, far, own_near))

    line = jnp.concatenate([line, step], axis=0)
    step = across(line, 2)
    other_near = lax.ppermute(own_near, "c", swap)
    own_far = lax.all_gather(far, "y", axis=0)
    step, other_near, own_far = lax.optimization_barrier((step, other_near, own_far))

    line = jnp.concatenate([line, step], axis=0)
    step = across(line, 1)
    other_far = lax.ppermute(own_far, "c", swap)
    line = jnp.concatenate([line, step], axis=0)

    def copies(v):
        return jnp.broadcast_to(v[None], (nx, *v.shape))

    pair_blocks = lax.all_to_all(copies(line[:, :, :128]), "x", 0, 0)
    query_line = copies(line[:, : 2 * panel, 128:])
    other_far, query_line = lax.optimization_barrier((other_far, query_line))
    query_blocks = lax.all_to_all(after(query_line, pair_blocks), "x", 0, 0)

    spot = jnp.stack([c, z, w]).astype(jnp.int32)
    features = norm_gain.shape[0]
    (normed,) = call(
        norm_kernel,
        [jax.ShapeDtypeStruct((2 * rows, features), bf16)],
        1,
        5,
        [pltpu.VMEM((2 * rows, features), bf16), pltpu.SemaphoreType.DMA],
        4 * 10**9,
        out_hbm=True,
    )(spot, norm_gain.astype(f32)[None, :], own_near, own_far, other_near, other_far)

    riding = pair_blocks[:, :, 2 * panel : 2 * panel + 4, :].astype(f32)
    starts = jnp.sum(
        (riding.reshape(-1, 1) < table.astype(f32)[None, :]).astype(f32), axis=0
    ).astype(jnp.int32)

    def begin_of(docs):
        return jnp.sum(
            (docs[:, None] == table[None, :]).astype(jnp.int32) * starts[None, :], axis=1
        )

    pair_begin = begin_of(pair_docs.reshape(-1))
    plane = nz * 2 * rows
    token = x * plane + z * 2 * rows + jnp.arange(2 * rows, dtype=jnp.int32)
    positions = token - pair_begin
    exponent = jnp.arange(64, dtype=f32) * (2.0 / 128)
    frequency = jnp.exp(exponent * -math.log(rope_base))
    angles = positions.astype(f32)[:, None] * frequency[None, :]
    cosine, sine = jnp.cos(angles), jnp.sin(angles)
    cosine = jnp.concatenate([cosine, cosine], axis=1)
    sine = jnp.concatenate([-sine, sine], axis=1)
    spread = [lax.dynamic_slice_in_dim(pair_begin, c * rows, rows, 0)]
    for s in (1, 2):
        place = (jnp.minimum(x + s, nx - 1), 0, 2 * c, 0)
        docs = lax.dynamic_slice(riding, place, (1, 1, 2, 128)).reshape(-1)[:rows]
        spread.append(begin_of(docs.astype(jnp.int32)))
    spread = jnp.stack(spread) - x * plane

    offsets = panel * jnp.sum(
        table[:, None] * (owners[:, None] == table[None, :]).astype(jnp.int32), axis=0
    )
    (pair,) = call(
        functools.partial(pair_kernel, panel),
        [jax.ShapeDtypeStruct((2 * rows, 128), bf16)],
        2,
        4,
        [
            pltpu.VMEM((2 * rows, features), bf16),
            pltpu.VMEM((features, 128), bf16),
            pltpu.SemaphoreType.DMA,
        ],
        2 * 10**9,
        n_hbm=1,
    )(offsets, spot, normed, key_gain[None, :], cosine, sine, pair_blocks)

    inside = z * 2 * rows + c * rows
    low = [jnp.clip(spread[s, 0], 0, plane) for s in range(3)]
    high = [inside + rows] + [jnp.where(x + s < nx, plane, 0) for s in (1, 2)]
    limits = [v for s in range(3) for v in (low[s], high[s], spread[s, rows - 1])]
    ranges = jnp.stack([c, z, inside] + limits).astype(jnp.int32)
    begins = spread[:, :, None]

    mine0 = jnp.stack([pair, across(pair, 4)])
    mine0, ranges, begins = lax.optimization_barrier((mine0, ranges, begins))
    mine0 = jnp.concatenate([mine0, across(mine0, 2)], axis=0)
    (query,) = call(
        functools.partial(query_kernel, panel),
        [jax.ShapeDtypeStruct((2, 2, rows, 128), bf16)],
        2,
        4,
        [
            pltpu.VMEM((2 * rows, features), bf16),
            pltpu.VMEM((features, 256), bf16),
            pltpu.SemaphoreType.DMA,
        ],
        4 * 10**9,
        n_hbm=1,
    )(offsets, spot, normed, query_gain[None, :], cosine, sine, query_blocks)

    mine0, query = lax.optimization_barrier((mine0, query))
    mine1 = across(mine0, 1)
    own_query = lax.dynamic_index_in_dim(query, c, 0, keepdims=False)
    sent_query = lax.dynamic_index_in_dim(query, 1 - c, 0, keepdims=False)
    q0 = jnp.concatenate([own_query, lax.ppermute(sent_query, "c", swap)], axis=0)
    q0 = q0.reshape(4 * rows, 128)
    mine = [mine0, mine1]
    other = [lax.ppermute(v, "c", swap) for v in (after(mine0, q0), mine1)]
    q1 = lax.ppermute(q0, "x", [(i, i - 1) for i in range(1, nx)])
    q2 = lax.ppermute(q0, "x", [(i, i - 2) for i in range(2, nx)])

    state = [pltpu.VMEM((4 * rows, 256), f32), pltpu.VMEM((4 * rows, 1), f32)]
    r1, r2, keys, values = call(
        remote_kernel,
        [jax.ShapeDtypeStruct((4 * rows + 48, 128), bf16)] * 2
        + [jax.ShapeDtypeStruct((plane, 128 * k), bf16) for k in (1, 2)],
        1,
        7,
        state,
        10**10,
    )(ranges, begins, q1, q2, *mine, *other)
    r1 = lax.ppermute(r1, "x", [(i, i + 1) for i in range(nx - 1)])
    r2 = lax.ppermute(r2, "x", [(i, i + 2) for i in range(nx - 2)])
    o0, l0 = call(
        own_kernel,
        [
            jax.ShapeDtypeStruct((4 * rows, 128), f32),
            jax.ShapeDtypeStruct((4 * rows, 1), f32),
        ],
        1,
        4,
        state,
        10**10,
    )(ranges, begins, q0, keys, values)
    came = jnp.stack([c, (x >= 1).astype(jnp.int32), (x >= 2).astype(jnp.int32)]).astype(jnp.int32)
    (context,) = call(combine_kernel, [jax.ShapeDtypeStruct((rows, 512), bf16)], 1, 4)(
        came, o0, l0, r1, r2
    )

    own_part = lax.dynamic_slice_in_dim(pair, c * rows, rows, 0)
    other_part = lax.dynamic_slice_in_dim(other[0][0], c * rows, rows, 0)
    keys_fresh = jnp.where(c == 0, own_part, other_part)
    values_fresh = jnp.where(c == 0, other_part, own_part)
    return keys_fresh, values_fresh, context


def solution(mesh):
    fine = Mesh(mesh.devices.reshape(4, 8, 2, 4, 2), ("x", "z", "c", "y", "w"))
    ctx, head = ("x", "z", "c"), ("y", "w")
    in_specs = (P(ctx, head), P(), P(), P(), P(ctx, head), P(ctx), P())
    out_specs = (P(ctx, head), P(ctx, head), P(ctx, head))
    return jax.shard_map(body, mesh=fine, in_specs=in_specs, out_specs=out_specs, check_vma=False)
```

```python
import functools
import math

import jax
import jax.numpy as jnp
from jax import lax
from jax.experimental import pallas as pl
from jax.experimental.pallas import tpu as pltpu
from jax.sharding import Mesh
from jax.sharding import PartitionSpec as P

epsilon = 1e-06
rope_base = 1000000.0
NEG = -1e30
MASKED = -3e38
KEY_BLOCK = 1024
NO_SEGMENT = 100.0
VMEM_LIMIT = 14 * 1024 * 1024
WIDE_LIMIT = 44 * 1024 * 1024


def call(kernel, out_shape, n_smem, n_vmem, scratch=(), flops=0, n_hbm=0, out_hbm=False, limit=VMEM_LIMIT):
    specs = [pl.BlockSpec(memory_space=pltpu.SMEM)] * n_smem
    specs += [pl.BlockSpec(memory_space=pltpu.HBM)] * n_hbm
    specs += [pl.BlockSpec(memory_space=pltpu.VMEM)] * n_vmem
    out = pl.BlockSpec(memory_space=pltpu.HBM if out_hbm else pltpu.VMEM)
    return pl.pallas_call(
        kernel,
        out_shape=out_shape,
        in_specs=specs,
        out_specs=[out] * len(out_shape),
        scratch_shapes=list(scratch),
        compiler_params=pltpu.CompilerParams(vmem_limit_bytes=limit),
        cost_estimate=pl.CostEstimate(flops=flops, bytes_accessed=4 << 20, transcendentals=0),
    )


PEER = (0, 4, 2, 6, 1, 5, 3, 7)


def head_norm_rope(v, gain, cosine, sine):
    mean = jnp.mean(v * v, axis=-1, keepdims=True)
    v = v * lax.rsqrt(mean + epsilon) * gain
    return v * cosine + pltpu.roll(v, 64, 1) * sine


def collect(offsets, where, blocks, weights, panel):
    nx, nz = blocks.shape[:2]
    for s in range(nx):
        for k, peer in enumerate(PEER):
            for c in range(2):
                slot = s * (2 * nz) + (where[1] ^ peer) * 2 + c
                first = pl.multiple_of(offsets[slot], 16)
                weights[pl.ds(first, panel), :] = blocks[s, k, c * panel : (c + 1) * panel, :]


def norm_kernel(where, norm_gain, *refs):
    hidden, out, normed, sem = refs[:-3], refs[-3], refs[-2], refs[-1]
    ny, rows, width = hidden[0].shape
    for side in range(2):
        first = pl.multiple_of(rows * (where[0] if side == 0 else 1 - where[0]), rows)
        total = jnp.zeros((rows, 128), jnp.float32)
        for half in range(2):
            for s in range(ny):
                v = hidden[side * 2 + half][s].astype(jnp.float32)
                v = v * v
                for k in range(width // 128):
                    total = total + v[:, k * 128 : (k + 1) * 128]
        mean = jnp.sum(total, axis=-1, keepdims=True) * (1.0 / (2 * ny * width))
        scale = lax.rsqrt(mean + epsilon)
        for half in range(2):
            for s in range(ny):
                source = s * 2 + (where[2] ^ half)
                cols = pl.ds(pl.multiple_of(source * width, 128), width)
                v = hidden[side * 2 + half][s].astype(jnp.float32)
                v = v * scale * norm_gain[:, cols]
                normed[pl.ds(first, rows), cols] = v.astype(jnp.bfloat16)
    copy = pltpu.make_async_copy(normed, out, sem)
    copy.start()
    copy.wait()


def fetch(offsets, where, sources, buffers, weights, sems, panel):
    copies = [
        pltpu.make_async_copy(source, buffer, sems.at[i])
        for i, (source, buffer) in enumerate(zip(sources, buffers, strict=True))
    ]
    for copy in copies[::-1]:
        copy.start()
    copies[3].wait()
    collect(offsets, where, buffers[3], weights, panel)
    for copy in copies[:3]:
        copy.wait()


def pair_kernel(panel, offsets, where, *refs):
    sources, (gain, out, weights, sems), buffers = refs[:4], refs[4:8], refs[8:]
    fetch(offsets, where, sources, buffers, weights, sems, panel)
    normed, cosine, sine, _ = buffers
    v = jnp.dot(normed[...], weights[...], preferred_element_type=jnp.float32)
    keys = head_norm_rope(v, gain[...], cosine[...], sine[...])
    out[...] = jnp.where(where[0] == 0, keys, v).astype(jnp.bfloat16)


def query_kernel(panel, offsets, where, *refs):
    sources, (gain, out, weights, sems), buffers = refs[:4], refs[4:8], refs[8:]
    fetch(offsets, where, sources, buffers, weights, sems, panel)
    normed, cosine, sine, _ = buffers
    rows = out.shape[2]
    for side in range(2):
        span = pl.ds(side * rows, rows)
        v = jnp.dot(normed[span, :], weights[...], preferred_element_type=jnp.float32)
        for h in range(2):
            q = head_norm_rope(
                v[:, h * 128 : (h + 1) * 128], gain[...], cosine[span, :], sine[span, :]
            )
            out[side, h] = q.astype(jnp.bfloat16)


def identity_mask():
    shape = (128, 128)
    return lax.broadcasted_iota(jnp.int32, shape, 0) == lax.broadcasted_iota(jnp.int32, shape, 1)


def attend(query, keys, values, begin, index, low, high, clear, acc, top):
    rows = begin.shape[0]
    scale = math.log2(math.e) / math.sqrt(128)
    acc[...] = jnp.zeros_like(acc)
    top[...] = jnp.full(top.shape, NEG, jnp.float32)

    def block(base, masked):
        key = keys[pl.ds(base, KEY_BLOCK), :]
        value = values[pl.ds(base, KEY_BLOCK), :]
        if masked:
            col = base + lax.broadcasted_iota(jnp.int32, (rows, KEY_BLOCK), 1)
            allowed = col >= begin
            if index is not None:
                allowed = allowed & (col <= index)
        for h in range(query.shape[0] // rows):
            span = pl.ds(h * rows, rows)
            raw = lax.dot_general(
                query[span, :], key, (((1,), (1,)), ((), ())), preferred_element_type=jnp.float32
            )
            if masked:
                raw = jnp.where(allowed, raw, MASKED)
            old = top[span, :]
            new = jnp.maximum(old, jnp.max(raw, axis=-1, keepdims=True))
            terms = jnp.exp2(raw * scale - new * scale)
            decay = jnp.exp2((old - new) * scale)
            top[span, :] = new
            acc[span, :] = acc[span, :] * decay + jnp.dot(
                terms.astype(jnp.bfloat16), value, preferred_element_type=jnp.float32
            )

    def step(b, carry):
        base = pl.multiple_of(b * KEY_BLOCK, KEY_BLOCK)
        plain = base >= clear
        if index is not None:
            plain = plain & (base + KEY_BLOCK <= high - rows)

        @pl.when(plain)
        def _():
            block(base, False)

        @pl.when(jnp.logical_not(plain))
        def _():
            block(base, True)

        return carry

    lax.fori_loop(low // KEY_BLOCK, (high + KEY_BLOCK - 1) // KEY_BLOCK, step, 0)
    summed = acc[:, 128:]
    safe = jnp.where(summed > 0, summed, 1.0)
    one = safe[:, 0:1]
    return acc[:, :128] / safe, jnp.where(one > 0, top[...] * scale + jnp.log2(one), NEG)


def own_kernel(where, begins, query, keys, values, out, log, acc, top):
    rows = begins.shape[1]
    index = where[2] + lax.broadcasted_iota(jnp.int32, (rows, 1), 0)
    limits = [where[3 + i] for i in range(3)]
    result, level = attend(query, keys, values, begins[0], index, *limits, acc, top)
    out[...] = result
    log[...] = level


def remote_kernel(where, begins, near, far, *refs):
    mine, other = refs[:2], refs[2:4]
    out1, out2, keys, values, acc, top = refs[4:]
    block = mine[0].shape[1]
    values[:, 128:] = jnp.ones((values.shape[0], 128), values.dtype)
    for core, (first, second) in enumerate(((mine, other), (other, mine))):

        @pl.when(where[0] == core)
        def _(first=first, second=second):
            for k in range(8):
                spot = pl.ds(pl.multiple_of((where[1] ^ PEER[k]) * block, block), block)
                keys[spot, :] = first[k // 4][k % 4]
                values[spot, :128] = second[k // 4][k % 4]

    eye = identity_mask()
    size = near.shape[0]
    for s, query, out in ((1, near, out1), (2, far, out2)):
        limits = [where[3 + 3 * s + i] for i in range(3)]
        result, log = attend(query, keys, values, begins[s], None, *limits, acc, top)
        out[0:size, :] = result.astype(jnp.bfloat16)
        rest = jnp.concatenate(
            [
                jnp.sum(jnp.where(eye, log[g * 128 : (g + 1) * 128, :], 0.0), axis=0, keepdims=True)
                for g in range(size // 128)
            ]
            + [jnp.zeros((16 - size // 128, 128), jnp.float32)],
            axis=0,
        )
        for part in range(3):
            piece = rest.astype(jnp.bfloat16)
            out[size + 16 * part : size + 16 * (part + 1), :] = piece
            rest = rest - piece.astype(jnp.float32)


def combine_kernel(where, o0, l0, r1, r2, out):
    rows = out.shape[0]
    size = o0.shape[0]
    eye = identity_mask()

    def column(ref):
        level = sum(
            ref[size + 16 * part : size + 16 * (part + 1), :].astype(jnp.float32)
            for part in (2, 1, 0)
        )
        pieces = [
            jnp.sum(jnp.where(eye, level[g : g + 1, :], 0.0), axis=1, keepdims=True)
            for g in range(size // 128)
        ]
        return jnp.concatenate(pieces, axis=0)

    a = l0[...]
    b = jnp.where(where[1] == 1, column(r1), NEG)
    c = jnp.where(where[2] == 1, column(r2), NEG)
    top = jnp.maximum(jnp.maximum(a, b), c)
    a, b, c = jnp.exp2(a - top), jnp.exp2(b - top), jnp.exp2(c - top)
    summed = a * o0[...]
    summed = summed + b * r1[0:size, :].astype(jnp.float32) + c * r2[0:size, :].astype(jnp.float32)
    result = (summed / (a + b + c)).astype(jnp.bfloat16)
    for side in range(2):
        first = 256 * (where[0] if side == 0 else 1 - where[0])
        for h in range(2):
            k = side * 2 + h
            cols = pl.ds(pl.multiple_of(first + h * 128, 128), 128)
            out[:, cols] = result[k * rows : (k + 1) * rows, :]


def across(v, bit):
    return lax.ppermute(v, "z", [(i, i ^ bit) for i in range(8)])


def after(v, *earlier):
    return lax.optimization_barrier((v, *earlier))[0]


def body(hidden, norm_gain, query_gain, key_gain, weight_store, documents, owners):
    x, z, c, w = (lax.axis_index(a) for a in ("x", "z", "c", "w"))
    nx, nz = (lax.axis_size(a) for a in ("x", "z"))
    rows = hidden.shape[0]
    slots = owners.shape[0]
    panel = weight_store.shape[0]
    swap = [(0, 1), (1, 0)]
    bf16, f32 = jnp.bfloat16, jnp.float32
    table = jnp.arange(slots, dtype=jnp.int32)

    riders = jnp.pad(documents.astype(bf16), (0, 256 - rows), constant_values=NO_SEGMENT)
    riders = jnp.pad(riders[None], ((0, 15), (0, weight_store.shape[1] - 256)))
    both = lax.all_gather(jnp.concatenate([weight_store, riders], axis=0), "c", axis=0)
    pair_docs = both[:, panel, :256]
    columns = both[:, :panel].reshape(2 * panel, -1)
    columns = jnp.concatenate(
        [
            lax.dynamic_slice_in_dim(columns, 512 + 128 * c, 128, 1),
            lax.dynamic_slice_in_dim(columns, 256 * c, 256, 1),
        ],
        axis=1,
    )
    tail = jnp.pad(pair_docs.reshape(4, 128), ((0, 12), (0, 256)))
    line = jnp.concatenate([columns, tail], axis=0)
    pair_docs = pair_docs[:, :rows].astype(jnp.int32)

    line = line[None]
    step = across(line, 4)
    far = lax.ppermute(hidden, "w", swap)
    own_near = lax.all_gather(hidden, "y", axis=0)
    step, far, own_near = lax.optimization_barrier((step, far, own_near))

    line = jnp.concatenate([line, step], axis=0)
    step = across(line, 2)
    other_near = lax.ppermute(own_near, "c", swap)
    own_far = lax.all_gather(far, "y", axis=0)
    step, other_near, own_far = lax.optimization_barrier((step, other_near, own_far))

    line = jnp.concatenate([line, step], axis=0)
    step = across(line, 1)
    other_far = lax.ppermute(own_far, "c", swap)
    line = jnp.concatenate([line, step], axis=0)

    def copies(v):
        return jnp.broadcast_to(v[None], (nx, *v.shape))

    pair_blocks = lax.all_to_all(copies(line[:, :, :128]), "x", 0, 0)
    query_line = copies(line[:, : 2 * panel, 128:])
    other_far, query_line = lax.optimization_barrier((other_far, query_line))
    query_blocks = lax.all_to_all(after(query_line, pair_blocks), "x", 0, 0)

    spot = jnp.stack([c, z, w]).astype(jnp.int32)
    features = norm_gain.shape[0]
    (normed,) = call(
        norm_kernel,
        [jax.ShapeDtypeStruct((2 * rows, features), bf16)],
        1,
        5,
        [pltpu.VMEM((2 * rows, features), bf16), pltpu.SemaphoreType.DMA],
        4 * 10**9,
        out_hbm=True,
    )(spot, norm_gain.astype(f32)[None, :], own_near, own_far, other_near, other_far)

    riding = pair_blocks[:, :, 2 * panel : 2 * panel + 4, :].astype(f32)
    starts = jnp.sum(
        (riding.reshape(-1, 1) < table.astype(f32)[None, :]).astype(f32), axis=0
    ).astype(jnp.int32)

    def begin_of(docs):
        return jnp.sum(
            (docs[:, None] == table[None, :]).astype(jnp.int32) * starts[None, :], axis=1
        )

    pair_begin = begin_of(pair_docs.reshape(-1))
    plane = nz * 2 * rows
    token = x * plane + z * 2 * rows + jnp.arange(2 * rows, dtype=jnp.int32)
    positions = token - pair_begin
    exponent = jnp.arange(64, dtype=f32) * (2.0 / 128)
    frequency = jnp.exp(exponent * -math.log(rope_base))
    angles = positions.astype(f32)[:, None] * frequency[None, :]
    cosine, sine = jnp.cos(angles), jnp.sin(angles)
    cosine = jnp.concatenate([cosine, cosine], axis=1)
    sine = jnp.concatenate([-sine, sine], axis=1)
    spread = [lax.dynamic_slice_in_dim(pair_begin, c * rows, rows, 0)]
    for s in (1, 2):
        place = (jnp.minimum(x + s, nx - 1), 0, 2 * c, 0)
        docs = lax.dynamic_slice(riding, place, (1, 1, 2, 128)).reshape(-1)[:rows]
        spread.append(begin_of(docs.astype(jnp.int32)))
    spread = jnp.stack(spread) - x * plane

    offsets = panel * jnp.sum(
        table[:, None] * (owners[:, None] == table[None, :]).astype(jnp.int32), axis=0
    )
    def project(kernel, out_shape, gain, blocks):
        scratch = [
            pltpu.VMEM((features, blocks.shape[-1]), bf16),
            pltpu.SemaphoreType.DMA((4,)),
            pltpu.VMEM(normed.shape, bf16),
            pltpu.VMEM(cosine.shape, f32),
            pltpu.VMEM(sine.shape, f32),
            pltpu.VMEM(blocks.shape, bf16),
        ]
        (result,) = call(
            functools.partial(kernel, panel),
            [jax.ShapeDtypeStruct(out_shape, bf16)],
            2,
            1,
            scratch,
            3 * 10**9,
            n_hbm=4,
            limit=WIDE_LIMIT,
        )(offsets, spot, normed, cosine, sine, blocks, gain[None, :])
        return result

    pair = project(pair_kernel, (2 * rows, 128), key_gain, pair_blocks)

    inside = z * 2 * rows + c * rows
    low = [jnp.clip(spread[s, 0], 0, plane) for s in range(3)]
    high = [inside + rows] + [jnp.where(x + s < nx, plane, 0) for s in (1, 2)]
    limits = [v for s in range(3) for v in (low[s], high[s], spread[s, rows - 1])]
    ranges = jnp.stack([c, z, inside] + limits).astype(jnp.int32)
    begins = spread[:, :, None]

    mine0 = jnp.stack([pair, across(pair, 4)])
    mine0, ranges, begins = lax.optimization_barrier((mine0, ranges, begins))
    mine0 = jnp.concatenate([mine0, across(mine0, 2)], axis=0)
    query = project(query_kernel, (2, 2, rows, 128), query_gain, query_blocks)

    mine0, query = lax.optimization_barrier((mine0, query))
    mine1 = across(mine0, 1)
    own_query = lax.dynamic_index_in_dim(query, c, 0, keepdims=False)
    sent_query = lax.dynamic_index_in_dim(query, 1 - c, 0, keepdims=False)
    q0 = jnp.concatenate([own_query, lax.ppermute(sent_query, "c", swap)], axis=0)
    q0 = q0.reshape(4 * rows, 128)
    mine = [mine0, mine1]
    q1 = lax.ppermute(q0, "x", [(i, i - 1) for i in range(1, nx)])
    q2 = lax.ppermute(q0, "x", [(i, i - 2) for i in range(2, nx)])
    other = [lax.ppermute(v, "c", swap) for v in (after(mine0, q0), after(mine1, q1, q2))]

    state = [pltpu.VMEM((4 * rows, 256), f32), pltpu.VMEM((4 * rows, 1), f32)]
    r1, r2, keys, values = call(
        remote_kernel,
        [jax.ShapeDtypeStruct((4 * rows + 48, 128), bf16)] * 2
        + [jax.ShapeDtypeStruct((plane, 128 * k), bf16) for k in (1, 2)],
        1,
        7,
        state,
        10**10,
    )(ranges, begins, q1, q2, *mine, *other)
    r1 = lax.ppermute(r1, "x", [(i, i + 1) for i in range(nx - 1)])
    r2 = lax.ppermute(r2, "x", [(i, i + 2) for i in range(nx - 2)])
    o0, l0 = call(
        own_kernel,
        [
            jax.ShapeDtypeStruct((4 * rows, 128), f32),
            jax.ShapeDtypeStruct((4 * rows, 1), f32),
        ],
        1,
        4,
        state,
        10**10,
    )(ranges, begins, q0, keys, values)
    came = jnp.stack([c, (x >= 1).astype(jnp.int32), (x >= 2).astype(jnp.int32)]).astype(jnp.int32)
    (context,) = call(combine_kernel, [jax.ShapeDtypeStruct((rows, 512), bf16)], 1, 4)(
        came, o0, l0, r1, r2
    )

    own_part = lax.dynamic_slice_in_dim(pair, c * rows, rows, 0)
    other_part = lax.dynamic_slice_in_dim(other[0][0], c * rows, rows, 0)
    keys_fresh = jnp.where(c == 0, own_part, other_part)
    values_fresh = jnp.where(c == 0, other_part, own_part)
    return keys_fresh, values_fresh, context


def solution(mesh):
    fine = Mesh(mesh.devices.reshape(4, 8, 2, 4, 2), ("x", "z", "c", "y", "w"))
    ctx, head = ("x", "z", "c"), ("y", "w")
    in_specs = (P(ctx, head), P(), P(), P(), P(ctx, head), P(ctx), P())
    out_specs = (P(ctx, head), P(ctx, head), P(ctx, head))
    return jax.shard_map(body, mesh=fine, in_specs=in_specs, out_specs=out_specs, check_vma=False)
```

```python
import functools
import math

import jax
import jax.numpy as jnp
from jax import lax
from jax.experimental import pallas as pl
from jax.experimental.pallas import tpu as pltpu
from jax.sharding import Mesh
from jax.sharding import PartitionSpec as P

epsilon = 1e-06
rope_base = 1000000.0
NEG = -1e30
MASKED = -3e38
KEY_BLOCK = 1024
NO_SEGMENT = 100.0
VMEM_LIMIT = 14 * 1024 * 1024
WIDE_LIMIT = 60 * 1024 * 1024


def call(kernel, out_shape, n_smem, n_vmem, scratch=(), flops=0, n_hbm=0, out_hbm=False, limit=VMEM_LIMIT):
    specs = [pl.BlockSpec(memory_space=pltpu.SMEM)] * n_smem
    specs += [pl.BlockSpec(memory_space=pltpu.HBM)] * n_hbm
    specs += [pl.BlockSpec(memory_space=pltpu.VMEM)] * n_vmem
    out = pl.BlockSpec(memory_space=pltpu.HBM if out_hbm else pltpu.VMEM)
    return pl.pallas_call(
        kernel,
        out_shape=out_shape,
        in_specs=specs,
        out_specs=[out] * len(out_shape),
        scratch_shapes=list(scratch),
        compiler_params=pltpu.CompilerParams(vmem_limit_bytes=limit),
        cost_estimate=pl.CostEstimate(flops=flops, bytes_accessed=4 << 20, transcendentals=0),
    )


PEER = (0, 4, 2, 6, 1, 5, 3, 7)


def head_norm_rope(v, gain, cosine, sine):
    mean = jnp.mean(v * v, axis=-1, keepdims=True)
    v = v * lax.rsqrt(mean + epsilon) * gain
    return v * cosine + pltpu.roll(v, 64, 1) * sine


def collect(offsets, where, blocks, weights, panel):
    nx, nz = blocks.shape[:2]
    for s in range(nx):
        for k, peer in enumerate(PEER):
            for c in range(2):
                slot = s * (2 * nz) + (where[1] ^ peer) * 2 + c
                first = pl.multiple_of(offsets[slot], 16)
                weights[pl.ds(first, panel), :] = blocks[s, k, c * panel : (c + 1) * panel, :]


def norm_kernel(where, norm_gain, *refs):
    hidden, out, normed, sem = refs[:-3], refs[-3], refs[-2], refs[-1]
    ny, rows, width = hidden[0].shape
    for side in range(2):
        first = pl.multiple_of(rows * (where[0] if side == 0 else 1 - where[0]), rows)
        total = jnp.zeros((rows, 128), jnp.float32)
        for half in range(2):
            for s in range(ny):
                v = hidden[side * 2 + half][s].astype(jnp.float32)
                v = v * v
                for k in range(width // 128):
                    total = total + v[:, k * 128 : (k + 1) * 128]
        mean = jnp.sum(total, axis=-1, keepdims=True) * (1.0 / (2 * ny * width))
        scale = lax.rsqrt(mean + epsilon)
        for half in range(2):
            for s in range(ny):
                source = s * 2 + (where[2] ^ half)
                cols = pl.ds(pl.multiple_of(source * width, 128), width)
                v = hidden[side * 2 + half][s].astype(jnp.float32)
                v = v * scale * norm_gain[:, cols]
                normed[pl.ds(first, rows), cols] = v.astype(jnp.bfloat16)
    copy = pltpu.make_async_copy(normed, out, sem)
    copy.start()
    copy.wait()


def fetch(offsets, where, sources, buffers, weights, sems, panel):
    copies = [
        pltpu.make_async_copy(source, buffer, sems.at[i])
        for i, (source, buffer) in enumerate(zip(sources, buffers, strict=True))
    ]
    for copy in copies[::-1]:
        copy.start()
    copies[3].wait()
    collect(offsets, where, buffers[3], weights, panel)
    for copy in copies[:3]:
        copy.wait()


def pair_kernel(panel, offsets, where, *refs):
    sources, (gain, out, weights, sems), buffers = refs[:4], refs[4:8], refs[8:]
    fetch(offsets, where, sources, buffers, weights, sems, panel)
    normed, cosine, sine, _ = buffers
    v = jnp.dot(normed[...], weights[...], preferred_element_type=jnp.float32)
    keys = head_norm_rope(v, gain[...], cosine[...], sine[...])
    out[...] = jnp.where(where[0] == 0, keys, v).astype(jnp.bfloat16)


def query_kernel(panel, offsets, where, *refs):
    sources, (gain, out, weights, sems), buffers = refs[:4], refs[4:8], refs[8:]
    fetch(offsets, where, sources, buffers, weights, sems, panel)
    normed, cosine, sine, _ = buffers
    rows = out.shape[2]
    for side in range(2):
        span = pl.ds(side * rows, rows)
        v = jnp.dot(normed[span, :], weights[...], preferred_element_type=jnp.float32)
        for h in range(2):
            q = head_norm_rope(
                v[:, h * 128 : (h + 1) * 128], gain[...], cosine[span, :], sine[span, :]
            )
            out[side, h] = q.astype(jnp.bfloat16)


def identity_mask():
    shape = (128, 128)
    return lax.broadcasted_iota(jnp.int32, shape, 0) == lax.broadcasted_iota(jnp.int32, shape, 1)


def attend(query, keys, values, begin, index, low, high, clear, acc, top):
    rows = begin.shape[0]
    scale = math.log2(math.e) / math.sqrt(128)
    acc[...] = jnp.zeros_like(acc)
    top[...] = jnp.full(top.shape, NEG, jnp.float32)

    def block(base, masked):
        key = keys[pl.ds(base, KEY_BLOCK), :]
        value = values[pl.ds(base, KEY_BLOCK), :]
        if masked:
            col = base + lax.broadcasted_iota(jnp.int32, (rows, KEY_BLOCK), 1)
            allowed = col >= begin
            if index is not None:
                allowed = allowed & (col <= index)
        for h in range(query.shape[0] // rows):
            span = pl.ds(h * rows, rows)
            raw = lax.dot_general(
                query[span, :], key, (((1,), (1,)), ((), ())), preferred_element_type=jnp.float32
            )
            if masked:
                raw = jnp.where(allowed, raw, MASKED)
            old = top[span, :]
            new = jnp.maximum(old, jnp.max(raw, axis=-1, keepdims=True))
            terms = jnp.exp2(raw * scale - new * scale)
            decay = jnp.exp2((old - new) * scale)
            top[span, :] = new
            acc[span, :] = acc[span, :] * decay + jnp.dot(
                terms.astype(jnp.bfloat16), value, preferred_element_type=jnp.float32
            )

    def step(b, carry):
        base = pl.multiple_of(b * KEY_BLOCK, KEY_BLOCK)
        plain = base >= clear
        if index is not None:
            plain = plain & (base + KEY_BLOCK <= high - rows)

        @pl.when(plain)
        def _():
            block(base, False)

        @pl.when(jnp.logical_not(plain))
        def _():
            block(base, True)

        return carry

    lax.fori_loop(low // KEY_BLOCK, (high + KEY_BLOCK - 1) // KEY_BLOCK, step, 0)
    summed = acc[:, 128:]
    safe = jnp.where(summed > 0, summed, 1.0)
    one = safe[:, 0:1]
    return acc[:, :128] / safe, jnp.where(one > 0, top[...] * scale + jnp.log2(one), NEG)


def own_kernel(where, begins, query, keys, values, out, log, acc, top):
    rows = begins.shape[1]
    index = where[2] + lax.broadcasted_iota(jnp.int32, (rows, 1), 0)
    limits = [where[3 + i] for i in range(3)]
    result, level = attend(query, keys, values, begins[0], index, *limits, acc, top)
    out[...] = result
    log[...] = level


def remote_kernel(where, begins, near, far, *refs):
    mine, other = refs[:2], refs[2:4]
    out1, out2, keys, values, acc, top = refs[4:]
    block = mine[0].shape[1]
    values[:, 128:] = jnp.ones((values.shape[0], 128), values.dtype)
    for core, (first, second) in enumerate(((mine, other), (other, mine))):

        @pl.when(where[0] == core)
        def _(first=first, second=second):
            for k in range(8):
                spot = pl.ds(pl.multiple_of((where[1] ^ PEER[k]) * block, block), block)
                keys[spot, :] = first[k // 4][k % 4]
                values[spot, :128] = second[k // 4][k % 4]

    eye = identity_mask()
    size = near.shape[0]
    for s, query, out in ((1, near, out1), (2, far, out2)):
        limits = [where[3 + 3 * s + i] for i in range(3)]
        result, log = attend(query, keys, values, begins[s], None, *limits, acc, top)
        out[0:size, :] = result.astype(jnp.bfloat16)
        rest = jnp.concatenate(
            [
                jnp.sum(jnp.where(eye, log[g * 128 : (g + 1) * 128, :], 0.0), axis=0, keepdims=True)
                for g in range(size // 128)
            ]
            + [jnp.zeros((16 - size // 128, 128), jnp.float32)],
            axis=0,
        )
        for part in range(3):
            piece = rest.astype(jnp.bfloat16)
            out[size + 16 * part : size + 16 * (part + 1), :] = piece
            rest = rest - piece.astype(jnp.float32)


def combine_kernel(where, o0, l0, r1, r2, out):
    rows = out.shape[0]
    size = o0.shape[0]
    eye = identity_mask()

    def column(ref):
        level = sum(
            ref[size + 16 * part : size + 16 * (part + 1), :].astype(jnp.float32)
            for part in (2, 1, 0)
        )
        pieces = [
            jnp.sum(jnp.where(eye, level[g : g + 1, :], 0.0), axis=1, keepdims=True)
            for g in range(size // 128)
        ]
        return jnp.concatenate(pieces, axis=0)

    a = l0[...]
    b = jnp.where(where[1] == 1, column(r1), NEG)
    c = jnp.where(where[2] == 1, column(r2), NEG)
    top = jnp.maximum(jnp.maximum(a, b), c)
    a, b, c = jnp.exp2(a - top), jnp.exp2(b - top), jnp.exp2(c - top)
    summed = a * o0[...]
    summed = summed + b * r1[0:size, :].astype(jnp.float32) + c * r2[0:size, :].astype(jnp.float32)
    result = (summed / (a + b + c)).astype(jnp.bfloat16)
    for side in range(2):
        first = 256 * (where[0] if side == 0 else 1 - where[0])
        for h in range(2):
            k = side * 2 + h
            cols = pl.ds(pl.multiple_of(first + h * 128, 128), 128)
            out[:, cols] = result[k * rows : (k + 1) * rows, :]


def across(v, bit):
    return lax.ppermute(v, "z", [(i, i ^ bit) for i in range(8)])


def after(v, *earlier):
    return lax.optimization_barrier((v, *earlier))[0]


def body(hidden, norm_gain, query_gain, key_gain, weight_store, documents, owners):
    x, z, c, w = (lax.axis_index(a) for a in ("x", "z", "c", "w"))
    nx, nz = (lax.axis_size(a) for a in ("x", "z"))
    rows = hidden.shape[0]
    slots = owners.shape[0]
    panel = weight_store.shape[0]
    swap = [(0, 1), (1, 0)]
    bf16, f32 = jnp.bfloat16, jnp.float32
    table = jnp.arange(slots, dtype=jnp.int32)

    riders = jnp.pad(documents.astype(bf16), (0, 256 - rows), constant_values=NO_SEGMENT)
    riders = jnp.pad(riders[None], ((0, 15), (0, weight_store.shape[1] - 256)))
    both = lax.all_gather(jnp.concatenate([weight_store, riders], axis=0), "c", axis=0)
    pair_docs = both[:, panel, :256]
    columns = both[:, :panel].reshape(2 * panel, -1)
    columns = jnp.concatenate(
        [
            lax.dynamic_slice_in_dim(columns, 512 + 128 * c, 128, 1),
            lax.dynamic_slice_in_dim(columns, 256 * c, 256, 1),
        ],
        axis=1,
    )
    tail = jnp.pad(pair_docs.reshape(4, 128), ((0, 12), (0, 256)))
    line = jnp.concatenate([columns, tail], axis=0)
    pair_docs = pair_docs[:, :rows].astype(jnp.int32)

    line = line[None]
    step = across(line, 4)
    far = lax.ppermute(hidden, "w", swap)
    own_near = lax.all_gather(hidden, "y", axis=0)
    step, far, own_near = lax.optimization_barrier((step, far, own_near))

    line = jnp.concatenate([line, step], axis=0)
    step = across(line, 2)
    other_near = lax.ppermute(own_near, "c", swap)
    own_far = lax.all_gather(far, "y", axis=0)
    step, other_near, own_far = lax.optimization_barrier((step, other_near, own_far))

    line = jnp.concatenate([line, step], axis=0)
    step = across(line, 1)
    other_far = lax.ppermute(own_far, "c", swap)
    line = jnp.concatenate([line, step], axis=0)

    def copies(v):
        return jnp.broadcast_to(v[None], (nx, *v.shape))

    pair_blocks = lax.all_to_all(copies(line[:, :, :128]), "x", 0, 0)
    query_line = copies(line[:, : 2 * panel, 128:])
    other_far, query_line = lax.optimization_barrier((other_far, query_line))
    query_blocks = lax.all_to_all(after(query_line, pair_blocks), "x", 0, 0)

    spot = jnp.stack([c, z, w]).astype(jnp.int32)
    features = norm_gain.shape[0]
    (normed,) = call(
        norm_kernel,
        [jax.ShapeDtypeStruct((2 * rows, features), bf16)],
        1,
        5,
        [pltpu.VMEM((2 * rows, features), bf16), pltpu.SemaphoreType.DMA],
        4 * 10**9,
        out_hbm=True,
    )(spot, norm_gain.astype(f32)[None, :], own_near, own_far, other_near, other_far)

    riding = pair_blocks[:, :, 2 * panel : 2 * panel + 4, :].astype(f32)
    starts = jnp.sum(
        (riding.reshape(-1, 1) < table.astype(f32)[None, :]).astype(f32), axis=0
    ).astype(jnp.int32)

    def begin_of(docs):
        return jnp.sum(
            (docs[:, None] == table[None, :]).astype(jnp.int32) * starts[None, :], axis=1
        )

    pair_begin = begin_of(pair_docs.reshape(-1))
    plane = nz * 2 * rows
    token = x * plane + z * 2 * rows + jnp.arange(2 * rows, dtype=jnp.int32)
    positions = token - pair_begin
    exponent = jnp.arange(64, dtype=f32) * (2.0 / 128)
    frequency = jnp.exp(exponent * -math.log(rope_base))
    angles = positions.astype(f32)[:, None] * frequency[None, :]
    cosine, sine = jnp.cos(angles), jnp.sin(angles)
    cosine = jnp.concatenate([cosine, cosine], axis=1)
    sine = jnp.concatenate([-sine, sine], axis=1)
    spread = [lax.dynamic_slice_in_dim(pair_begin, c * rows, rows, 0)]
    for s in (1, 2):
        place = (jnp.minimum(x + s, nx - 1), 0, 2 * c, 0)
        docs = lax.dynamic_slice(riding, place, (1, 1, 2, 128)).reshape(-1)[:rows]
        spread.append(begin_of(docs.astype(jnp.int32)))
    spread = jnp.stack(spread) - x * plane

    offsets = panel * jnp.sum(
        table[:, None] * (owners[:, None] == table[None, :]).astype(jnp.int32), axis=0
    )
    def project(kernel, out_shape, gain, blocks):
        scratch = [
            pltpu.VMEM((features, blocks.shape[-1]), bf16),
            pltpu.SemaphoreType.DMA((4,)),
            pltpu.VMEM(normed.shape, bf16),
            pltpu.VMEM(cosine.shape, f32),
            pltpu.VMEM(sine.shape, f32),
            pltpu.VMEM(blocks.shape, bf16),
        ]
        (result,) = call(
            functools.partial(kernel, panel),
            [jax.ShapeDtypeStruct(out_shape, bf16)],
            2,
            1,
            scratch,
            3 * 10**9,
            n_hbm=4,
            limit=WIDE_LIMIT,
        )(offsets, spot, normed, cosine, sine, blocks, gain[None, :])
        return result

    pair = project(pair_kernel, (2 * rows, 128), key_gain, pair_blocks)

    inside = z * 2 * rows + c * rows
    low = [jnp.clip(spread[s, 0], 0, plane) for s in range(3)]
    high = [inside + rows] + [jnp.where(x + s < nx, plane, 0) for s in (1, 2)]
    limits = [v for s in range(3) for v in (low[s], high[s], spread[s, rows - 1])]
    ranges = jnp.stack([c, z, inside] + limits).astype(jnp.int32)
    begins = spread[:, :, None]

    mine0 = jnp.stack([pair, across(pair, 4)])
    mine0, ranges, begins = lax.optimization_barrier((mine0, ranges, begins))
    mine0 = jnp.concatenate([mine0, across(mine0, 2)], axis=0)
    query = project(query_kernel, (2, 2, rows, 128), query_gain, query_blocks)

    mine0, query = lax.optimization_barrier((mine0, query))
    mine1 = across(mine0, 1)
    own_query = lax.dynamic_index_in_dim(query, c, 0, keepdims=False)
    sent_query = lax.dynamic_index_in_dim(query, 1 - c, 0, keepdims=False)
    q0 = jnp.concatenate([own_query, lax.ppermute(sent_query, "c", swap)], axis=0)
    q0 = q0.reshape(4 * rows, 128)
    mine = [mine0, mine1]
    q1 = lax.ppermute(q0, "x", [(i, i - 1) for i in range(1, nx)])
    q2 = lax.ppermute(q0, "x", [(i, i - 2) for i in range(2, nx)])
    other = [lax.ppermute(v, "c", swap) for v in (after(mine0, q0), after(mine1, q1, q2))]

    state = [pltpu.VMEM((4 * rows, 256), f32), pltpu.VMEM((4 * rows, 1), f32)]
    r1, r2, keys, values = call(
        remote_kernel,
        [jax.ShapeDtypeStruct((4 * rows + 48, 128), bf16)] * 2
        + [jax.ShapeDtypeStruct((plane, 128 * k), bf16) for k in (1, 2)],
        1,
        7,
        state,
        10**10,
    )(ranges, begins, q1, q2, *mine, *other)
    r1 = lax.ppermute(r1, "x", [(i, i + 1) for i in range(nx - 1)])
    r2 = lax.ppermute(r2, "x", [(i, i + 2) for i in range(nx - 2)])
    o0, l0 = call(
        own_kernel,
        [
            jax.ShapeDtypeStruct((4 * rows, 128), f32),
            jax.ShapeDtypeStruct((4 * rows, 1), f32),
        ],
        1,
        4,
        state,
        10**10,
    )(ranges, begins, q0, keys, values)
    came = jnp.stack([c, (x >= 1).astype(jnp.int32), (x >= 2).astype(jnp.int32)]).astype(jnp.int32)
    (context,) = call(combine_kernel, [jax.ShapeDtypeStruct((rows, 512), bf16)], 1, 4)(
        came, o0, l0, r1, r2
    )

    own_part = lax.dynamic_slice_in_dim(pair, c * rows, rows, 0)
    other_part = lax.dynamic_slice_in_dim(other[0][0], c * rows, rows, 0)
    keys_fresh = jnp.where(c == 0, own_part, other_part)
    values_fresh = jnp.where(c == 0, other_part, own_part)
    return keys_fresh, values_fresh, context


def solution(mesh):
    fine = Mesh(mesh.devices.reshape(4, 8, 2, 4, 2), ("x", "z", "c", "y", "w"))
    ctx, head = ("x", "z", "c"), ("y", "w")
    in_specs = (P(ctx, head), P(), P(), P(), P(ctx, head), P(ctx), P())
    out_specs = (P(ctx, head), P(ctx, head), P(ctx, head))
    return jax.shard_map(body, mesh=fine, in_specs=in_specs, out_specs=out_specs, check_vma=False)
```

```python
import functools
import math

import jax
import jax.numpy as jnp
from jax import lax
from jax.experimental import pallas as pl
from jax.experimental.pallas import tpu as pltpu
from jax.sharding import Mesh
from jax.sharding import PartitionSpec as P

epsilon = 1e-06
rope_base = 1000000.0
NEG = -1e30
MASKED = -3e38
KEY_BLOCK = 1024
NO_SEGMENT = 100.0
VMEM_LIMIT = 14 * 1024 * 1024
WIDE_LIMIT = 44 * 1024 * 1024


def call(kernel, out_shape, n_smem, n_vmem, scratch=(), flops=0, n_hbm=0, out_hbm=False, limit=VMEM_LIMIT):
    specs = [pl.BlockSpec(memory_space=pltpu.SMEM)] * n_smem
    specs += [pl.BlockSpec(memory_space=pltpu.HBM)] * n_hbm
    specs += [pl.BlockSpec(memory_space=pltpu.VMEM)] * n_vmem
    out = pl.BlockSpec(memory_space=pltpu.HBM if out_hbm else pltpu.VMEM)
    return pl.pallas_call(
        kernel,
        out_shape=out_shape,
        in_specs=specs,
        out_specs=[out] * len(out_shape),
        scratch_shapes=list(scratch),
        compiler_params=pltpu.CompilerParams(vmem_limit_bytes=limit),
        cost_estimate=pl.CostEstimate(flops=flops, bytes_accessed=4 << 20, transcendentals=0),
    )


PEER = (0, 4, 2, 6, 1, 5, 3, 7)


def head_norm_rope(v, gain, cosine, sine):
    mean = jnp.mean(v * v, axis=-1, keepdims=True)
    v = v * lax.rsqrt(mean + epsilon) * gain
    return v * cosine + pltpu.roll(v, 64, 1) * sine


def collect(offsets, where, blocks, weights, panel):
    nx, nz = blocks.shape[:2]
    for s in range(nx):
        for k, peer in enumerate(PEER):
            for c in range(2):
                slot = s * (2 * nz) + (where[1] ^ peer) * 2 + c
                first = pl.multiple_of(offsets[slot], 16)
                weights[pl.ds(first, panel), :] = blocks[s, k, c * panel : (c + 1) * panel, :]


def norm_kernel(where, norm_gain, *refs):
    hidden, out, normed, sem = refs[:-3], refs[-3], refs[-2], refs[-1]
    ny, rows, width = hidden[0].shape
    for side in range(2):
        first = pl.multiple_of(rows * (where[0] if side == 0 else 1 - where[0]), rows)
        total = jnp.zeros((rows, 128), jnp.float32)
        for half in range(2):
            for s in range(ny):
                v = hidden[side * 2 + half][s].astype(jnp.float32)
                v = v * v
                for k in range(width // 128):
                    total = total + v[:, k * 128 : (k + 1) * 128]
        mean = jnp.sum(total, axis=-1, keepdims=True) * (1.0 / (2 * ny * width))
        scale = lax.rsqrt(mean + epsilon)
        for half in range(2):
            for s in range(ny):
                source = s * 2 + (where[2] ^ half)
                cols = pl.ds(pl.multiple_of(source * width, 128), width)
                v = hidden[side * 2 + half][s].astype(jnp.float32)
                v = v * scale * norm_gain[:, cols]
                normed[pl.ds(first, rows), cols] = v.astype(jnp.bfloat16)
    copy = pltpu.make_async_copy(normed, out, sem)
    copy.start()
    copy.wait()


def fetch(offsets, where, sources, buffers, weights, sems, panel):
    copies = [
        pltpu.make_async_copy(source, buffer, sems.at[i])
        for i, (source, buffer) in enumerate(zip(sources, buffers, strict=True))
    ]
    for copy in copies[::-1]:
        copy.start()
    copies[3].wait()
    collect(offsets, where, buffers[3], weights, panel)
    for copy in copies[:3]:
        copy.wait()


def pair_kernel(panel, offsets, where, *refs):
    sources, (gain, out, weights, sems), buffers = refs[:4], refs[4:8], refs[8:]
    fetch(offsets, where, sources, buffers, weights, sems, panel)
    normed, cosine, sine, _ = buffers
    v = jnp.dot(normed[...], weights[...], preferred_element_type=jnp.float32)
    keys = head_norm_rope(v, gain[...], cosine[...], sine[...])
    out[...] = jnp.where(where[0] == 0, keys, v).astype(jnp.bfloat16)


def query_kernel(panel, offsets, where, *refs):
    sources, (gain, out, weights, sems), buffers = refs[:4], refs[4:8], refs[8:]
    fetch(offsets, where, sources, buffers, weights, sems, panel)
    normed, cosine, sine, _ = buffers
    rows = out.shape[2]
    for side in range(2):
        span = pl.ds(side * rows, rows)
        v = jnp.dot(normed[span, :], weights[...], preferred_element_type=jnp.float32)
        for h in range(2):
            q = head_norm_rope(
                v[:, h * 128 : (h + 1) * 128], gain[...], cosine[span, :], sine[span, :]
            )
            out[side, h] = q.astype(jnp.bfloat16)


def identity_mask():
    shape = (128, 128)
    return lax.broadcasted_iota(jnp.int32, shape, 0) == lax.broadcasted_iota(jnp.int32, shape, 1)


def attend(query, keys, values, begin, index, low, high, clear, acc, top):
    rows = begin.shape[0]
    scale = math.log2(math.e) / math.sqrt(128)
    acc[...] = jnp.zeros_like(acc)
    top[...] = jnp.full(top.shape, NEG, jnp.float32)

    def block(base, masked):
        key = keys[pl.ds(base, KEY_BLOCK), :]
        value = values[pl.ds(base, KEY_BLOCK), :]
        if masked:
            col = base + lax.broadcasted_iota(jnp.int32, (rows, KEY_BLOCK), 1)
            allowed = col >= begin
            if index is not None:
                allowed = allowed & (col <= index)
        for h in range(query.shape[0] // rows):
            span = pl.ds(h * rows, rows)
            raw = lax.dot_general(
                query[span, :], key, (((1,), (1,)), ((), ())), preferred_element_type=jnp.float32
            )
            if masked:
                raw = jnp.where(allowed, raw, MASKED)
            old = top[span, :]
            new = jnp.maximum(old, jnp.max(raw, axis=-1, keepdims=True))
            terms = jnp.exp2(raw * scale - new * scale)
            decay = jnp.exp2((old - new) * scale)
            top[span, :] = new
            acc[span, :] = acc[span, :] * decay + jnp.dot(
                terms.astype(jnp.bfloat16), value, preferred_element_type=jnp.float32
            )

    def step(b, carry):
        base = pl.multiple_of(b * KEY_BLOCK, KEY_BLOCK)
        plain = base >= clear
        if index is not None:
            plain = plain & (base + KEY_BLOCK <= high - rows)

        @pl.when(plain)
        def _():
            block(base, False)

        @pl.when(jnp.logical_not(plain))
        def _():
            block(base, True)

        return carry

    lax.fori_loop(low // KEY_BLOCK, (high + KEY_BLOCK - 1) // KEY_BLOCK, step, 0)
    summed = acc[:, 128:]
    safe = jnp.where(summed > 0, summed, 1.0)
    one = safe[:, 0:1]
    return acc[:, :128] / safe, jnp.where(one > 0, top[...] * scale + jnp.log2(one), NEG)


def own_kernel(where, begins, query, keys, values, out, log, acc, top):
    rows = begins.shape[1]
    index = where[2] + lax.broadcasted_iota(jnp.int32, (rows, 1), 0)
    limits = [where[3 + i] for i in range(3)]
    result, level = attend(query, keys, values, begins[0], index, *limits, acc, top)
    out[...] = result
    log[...] = level


def remote_kernel(where, begins, near, far, *refs):
    mine, other = refs[:2], refs[2:4]
    out1, out2, keys, values, acc, top = refs[4:]
    block = mine[0].shape[1]
    values[:, 128:] = jnp.ones((values.shape[0], 128), values.dtype)
    for core, (first, second) in enumerate(((mine, other), (other, mine))):

        @pl.when(where[0] == core)
        def _(first=first, second=second):
            for k in range(8):
                spot = pl.ds(pl.multiple_of((where[1] ^ PEER[k]) * block, block), block)
                keys[spot, :] = first[k // 4][k % 4]
                values[spot, :128] = second[k // 4][k % 4]

    eye = identity_mask()
    size = near.shape[0]
    for s, query, out in ((1, near, out1), (2, far, out2)):
        limits = [where[3 + 3 * s + i] for i in range(3)]
        result, log = attend(query, keys, values, begins[s], None, *limits, acc, top)
        out[0:size, :] = result.astype(jnp.bfloat16)
        rest = jnp.concatenate(
            [
                jnp.sum(jnp.where(eye, log[g * 128 : (g + 1) * 128, :], 0.0), axis=0, keepdims=True)
                for g in range(size // 128)
            ]
            + [jnp.zeros((16 - size // 128, 128), jnp.float32)],
            axis=0,
        )
        for part in range(3):
            piece = rest.astype(jnp.bfloat16)
            out[size + 16 * part : size + 16 * (part + 1), :] = piece
            rest = rest - piece.astype(jnp.float32)


def combine_kernel(where, o0, l0, r1, r2, out):
    rows = out.shape[0]
    size = o0.shape[0]
    eye = identity_mask()

    def column(ref):
        level = sum(
            ref[size + 16 * part : size + 16 * (part + 1), :].astype(jnp.float32)
            for part in (2, 1, 0)
        )
        pieces = [
            jnp.sum(jnp.where(eye, level[g : g + 1, :], 0.0), axis=1, keepdims=True)
            for g in range(size // 128)
        ]
        return jnp.concatenate(pieces, axis=0)

    a = l0[...]
    b = jnp.where(where[1] == 1, column(r1), NEG)
    c = jnp.where(where[2] == 1, column(r2), NEG)
    top = jnp.maximum(jnp.maximum(a, b), c)
    a, b, c = jnp.exp2(a - top), jnp.exp2(b - top), jnp.exp2(c - top)
    summed = a * o0[...]
    summed = summed + b * r1[0:size, :].astype(jnp.float32) + c * r2[0:size, :].astype(jnp.float32)
    result = (summed / (a + b + c)).astype(jnp.bfloat16)
    for side in range(2):
        first = 256 * (where[0] if side == 0 else 1 - where[0])
        for h in range(2):
            k = side * 2 + h
            cols = pl.ds(pl.multiple_of(first + h * 128, 128), 128)
            out[:, cols] = result[k * rows : (k + 1) * rows, :]


def across(v, bit):
    return lax.ppermute(v, "z", [(i, i ^ bit) for i in range(8)])


def after(v, *earlier):
    return lax.optimization_barrier((v, *earlier))[0]


def body(hidden, norm_gain, query_gain, key_gain, weight_store, documents, owners):
    x, z, c, w = (lax.axis_index(a) for a in ("x", "z", "c", "w"))
    nx, nz = (lax.axis_size(a) for a in ("x", "z"))
    rows = hidden.shape[0]
    slots = owners.shape[0]
    panel = weight_store.shape[0]
    swap = [(0, 1), (1, 0)]
    bf16, f32 = jnp.bfloat16, jnp.float32
    table = jnp.arange(slots, dtype=jnp.int32)

    riders = jnp.pad(documents.astype(bf16), (0, 256 - rows), constant_values=NO_SEGMENT)
    riders = jnp.pad(riders[None], ((0, 15), (0, weight_store.shape[1] - 256)))
    both = lax.all_gather(jnp.concatenate([weight_store, riders], axis=0), "c", axis=0)
    pair_docs = both[:, panel, :256]
    columns = both[:, :panel].reshape(2 * panel, -1)
    columns = jnp.concatenate(
        [
            lax.dynamic_slice_in_dim(columns, 512 + 128 * c, 128, 1),
            lax.dynamic_slice_in_dim(columns, 256 * c, 256, 1),
        ],
        axis=1,
    )
    tail = jnp.pad(pair_docs.reshape(4, 128), ((0, 12), (0, 256)))
    line = jnp.concatenate([columns, tail], axis=0)
    pair_docs = pair_docs[:, :rows].astype(jnp.int32)

    line = line[None]
    step = across(line, 4)
    far = lax.ppermute(hidden, "w", swap)
    own_near = lax.all_gather(hidden, "y", axis=0)
    step, far, own_near = lax.optimization_barrier((step, far, own_near))

    line = jnp.concatenate([line, step], axis=0)
    step = across(line, 2)
    other_near = lax.ppermute(own_near, "c", swap)
    own_far = lax.all_gather(far, "y", axis=0)
    step, other_near, own_far = lax.optimization_barrier((step, other_near, own_far))

    line = jnp.concatenate([line, step], axis=0)
    step = across(line, 1)
    other_far = lax.ppermute(own_far, "c", swap)
    line = jnp.concatenate([line, step], axis=0)

    def copies(v):
        return jnp.broadcast_to(v[None], (nx, *v.shape))

    pair_blocks = lax.all_to_all(copies(line[:, :, :128]), "x", 0, 0)
    query_line = copies(line[:, : 2 * panel, 128:])
    other_far, query_line = lax.optimization_barrier((other_far, query_line))
    query_blocks = lax.all_to_all(after(query_line, pair_blocks), "x", 0, 0)

    spot = jnp.stack([c, z, w]).astype(jnp.int32)
    features = norm_gain.shape[0]
    (normed,) = call(
        norm_kernel,
        [jax.ShapeDtypeStruct((2 * rows, features), bf16)],
        1,
        5,
        [pltpu.VMEM((2 * rows, features), bf16), pltpu.SemaphoreType.DMA],
        4 * 10**9,
        out_hbm=True,
    )(spot, norm_gain.astype(f32)[None, :], own_near, own_far, other_near, other_far)

    riding = pair_blocks[:, :, 2 * panel : 2 * panel + 4, :].astype(f32)
    starts = jnp.sum(
        (riding.reshape(-1, 1) < table.astype(f32)[None, :]).astype(f32), axis=0
    ).astype(jnp.int32)

    def begin_of(docs):
        return jnp.sum(
            (docs[:, None] == table[None, :]).astype(jnp.int32) * starts[None, :], axis=1
        )

    pair_begin = begin_of(pair_docs.reshape(-1))
    plane = nz * 2 * rows
    token = x * plane + z * 2 * rows + jnp.arange(2 * rows, dtype=jnp.int32)
    positions = token - pair_begin
    exponent = jnp.arange(64, dtype=f32) * (2.0 / 128)
    frequency = jnp.exp(exponent * -math.log(rope_base))
    angles = positions.astype(f32)[:, None] * frequency[None, :]
    cosine, sine = jnp.cos(angles), jnp.sin(angles)
    cosine = jnp.concatenate([cosine, cosine], axis=1)
    sine = jnp.concatenate([-sine, sine], axis=1)
    spread = [lax.dynamic_slice_in_dim(pair_begin, c * rows, rows, 0)]
    for s in (1, 2):
        place = (jnp.minimum(x + s, nx - 1), 0, 2 * c, 0)
        docs = lax.dynamic_slice(riding, place, (1, 1, 2, 128)).reshape(-1)[:rows]
        spread.append(begin_of(docs.astype(jnp.int32)))
    spread = jnp.stack(spread) - x * plane

    offsets = panel * jnp.sum(
        table[:, None] * (owners[:, None] == table[None, :]).astype(jnp.int32), axis=0
    )
    def project(kernel, out_shape, gain, blocks):
        scratch = [
            pltpu.VMEM((features, blocks.shape[-1]), bf16),
            pltpu.SemaphoreType.DMA((4,)),
            pltpu.VMEM(normed.shape, bf16),
            pltpu.VMEM(cosine.shape, f32),
            pltpu.VMEM(sine.shape, f32),
            pltpu.VMEM(blocks.shape, bf16),
        ]
        (result,) = call(
            functools.partial(kernel, panel),
            [jax.ShapeDtypeStruct(out_shape, bf16)],
            2,
            1,
            scratch,
            3 * 10**9,
            n_hbm=4,
            limit=WIDE_LIMIT,
        )(offsets, spot, normed, cosine, sine, blocks, gain[None, :])
        return result

    pair = project(pair_kernel, (2 * rows, 128), key_gain, pair_blocks)

    inside = z * 2 * rows + c * rows
    low = [jnp.clip(spread[s, 0], 0, plane) for s in range(3)]
    high = [inside + rows] + [jnp.where(x + s < nx, plane, 0) for s in (1, 2)]
    limits = [v for s in range(3) for v in (low[s], high[s], spread[s, rows - 1])]
    ranges = jnp.stack([c, z, inside] + limits).astype(jnp.int32)
    begins = spread[:, :, None]

    mine0 = jnp.stack([pair, across(pair, 4)])
    mine0, ranges, begins = lax.optimization_barrier((mine0, ranges, begins))
    mine0 = jnp.concatenate([mine0, across(mine0, 2)], axis=0)
    mine0, query_blocks = lax.optimization_barrier((mine0, query_blocks))
    mine1 = across(mine0, 1)
    query = project(query_kernel, (2, 2, rows, 128), query_gain, query_blocks)

    own_query = lax.dynamic_index_in_dim(query, c, 0, keepdims=False)
    sent_query = lax.dynamic_index_in_dim(query, 1 - c, 0, keepdims=False)
    q0 = jnp.concatenate([own_query, lax.ppermute(sent_query, "c", swap)], axis=0)
    q0 = q0.reshape(4 * rows, 128)
    mine = [mine0, mine1]
    q1 = lax.ppermute(q0, "x", [(i, i - 1) for i in range(1, nx)])
    q2 = lax.ppermute(q0, "x", [(i, i - 2) for i in range(2, nx)])
    other = [lax.ppermute(v, "c", swap) for v in (after(mine0, q0), after(mine1, q0))]

    state = [pltpu.VMEM((4 * rows, 256), f32), pltpu.VMEM((4 * rows, 1), f32)]
    r1, r2, keys, values = call(
        remote_kernel,
        [jax.ShapeDtypeStruct((4 * rows + 48, 128), bf16)] * 2
        + [jax.ShapeDtypeStruct((plane, 128 * k), bf16) for k in (1, 2)],
        1,
        7,
        state,
        10**10,
    )(ranges, begins, q1, q2, *mine, *other)
    r1 = lax.ppermute(r1, "x", [(i, i + 1) for i in range(nx - 1)])
    r2 = lax.ppermute(r2, "x", [(i, i + 2) for i in range(nx - 2)])
    o0, l0 = call(
        own_kernel,
        [
            jax.ShapeDtypeStruct((4 * rows, 128), f32),
            jax.ShapeDtypeStruct((4 * rows, 1), f32),
        ],
        1,
        4,
        state,
        10**10,
    )(ranges, begins, q0, keys, values)
    came = jnp.stack([c, (x >= 1).astype(jnp.int32), (x >= 2).astype(jnp.int32)]).astype(jnp.int32)
    (context,) = call(combine_kernel, [jax.ShapeDtypeStruct((rows, 512), bf16)], 1, 4)(
        came, o0, l0, r1, r2
    )

    own_part = lax.dynamic_slice_in_dim(pair, c * rows, rows, 0)
    other_part = lax.dynamic_slice_in_dim(other[0][0], c * rows, rows, 0)
    keys_fresh = jnp.where(c == 0, own_part, other_part)
    values_fresh = jnp.where(c == 0, other_part, own_part)
    return keys_fresh, values_fresh, context


def solution(mesh):
    fine = Mesh(mesh.devices.reshape(4, 8, 2, 4, 2), ("x", "z", "c", "y", "w"))
    ctx, head = ("x", "z", "c"), ("y", "w")
    in_specs = (P(ctx, head), P(), P(), P(), P(ctx, head), P(ctx), P())
    out_specs = (P(ctx, head), P(ctx, head), P(ctx, head))
    return jax.shard_map(body, mesh=fine, in_specs=in_specs, out_specs=out_specs, check_vma=False)
```
